128 devices in a mesh: space: 64 (over x, y_lo, z, core), head: 2 (over y_hi).
Axes of the slice: x: 4, y: 4 (y_hi: 2, y_lo: 2; y = y_hi * 2 + y_lo), z: 4, core: 2. Of those that a mesh axis runs over, the one named last changes fastest.
Arguments:
- grid_feat: bfloat16 [131072, 1024], P('space', 'head'), may hold values from -6 to 6
- mesh_feat: bfloat16 [8192, 1024], P('space', 'head'), may hold values from -6 to 6
- edge_src: int32 [8192, 16], P('space'), may hold values from 0 to 131071, as said below
- degree: int32 [8192], P('space'), may hold values from 8 to 16
- offsets: int32 [16], replicated, may hold values from -32 to 32, as said below
- w_kv: bfloat16 [2, 1024, 1024], P(None, None, 'head'), may hold values from -0.1875 to 0.1875
- w_query: bfloat16 [1024, 1024], P(None, 'head'), may hold values from -0.1875 to 0.1875
- w_out: bfloat16 [1024, 1024], P('head'), may hold values from -0.1875 to 0.1875
- w_mesh: bfloat16 [3, 1024, 1024], P(None, None, 'head'), may hold values from -0.1875 to 0.1875
- w_mesh_out: bfloat16 [1024, 1024], P('head'), may hold values from -0.1875 to 0.1875
- cotangent: bfloat16 [8192, 1024], P('space', 'head'), may hold values from -6 to 6
Outputs:
- encoded: bfloat16 [8192, 1024], P('space', 'head')
- mesh_out: bfloat16 [8192, 1024], P('space', 'head')
- grad_grid: bfloat16 [131072, 1024], P('space', 'head')
- grad_kv: float32 [2, 1024, 1024], P(None, None, 'head')
The draws below stay inside these ranges and needn't reach their ends.
Inputs may be any that keep to these rules, and one draw needn't show every extreme that they name: `edge_src`: an edge of a mesh node of shard s (nodes s*128 to (s+1)*128 - 1) comes from grid rows s*2048 - 128 to (s+1)*2048 + 127 inside the grid; the first node of every shard but the first reaches the lowest of these rows and the last node of every shard but the last the highest. Slots at and after degree are padding. 16 distinct offsets that include -32 and 32.
All inputs are finite; a program needn't handle non-finite values.
Results may differ from the reference program's by a relative error of at most 0.02.
Values may be sent and summed in bfloat16 or wider, within the bound.
A program may use at most 128 MiB of HBM per device.

```python
import math
import jax
import jax.numpy as jnp
from jax import lax

D = 1024
HEADS = 16
HEAD_SIZE = 64
G_DEV = 2048
GRID_PER_MESH = 16
K = 16
RIM = 128
R = 32
W = 16
M_DEV = 128
GRID = 131072
MESH = 8192


def draw_edge_src(key, part):
    key = jax.random.fold_in(key, 11)
    stride = G_DEV // GRID_PER_MESH * 0 + GRID_PER_MESH
    nodes = jnp.arange(MESH, dtype=jnp.int32)
    shard = nodes // M_DEV
    local = nodes % M_DEV
    base = shard * G_DEV + local * stride
    shift_amount = jax.random.randint(key, (MESH, K), -RIM, stride + RIM, dtype=jnp.int32)
    source = base[:, None] + shift_amount
    lowest = shard * G_DEV - RIM
    highest = shard * G_DEV + G_DEV - 1 + RIM
    first_slot = jnp.where(local == 0, lowest, jnp.where(local == M_DEV - 1, highest, source[:, 0]))
    source = source.at[:, 0].set(first_slot)
    return jnp.clip(source, 0, GRID - 1).astype(jnp.int32)


def draw_offsets(key, part):
    key = jax.random.fold_in(key, 12)
    inner = jax.random.permutation(key, 2 * R - 1).astype(jnp.int32) - (R - 1)
    ends = jnp.array([-R, R], dtype=jnp.int32)
    return jnp.concatenate([ends, inner[:W - 2]]).astype(jnp.int32)


def touch_ends(values, key, low, top_value):
    longest = values.shape.index(max(values.shape))
    spots = []
    for shift in (0, 1):
        where = [jax.random.randint(jax.random.fold_in(key, axis), (), 0, length) for axis, length in enumerate(values.shape)]
        where[longest] = (where[longest] + shift) % values.shape[longest]
        spots.append(tuple(where))
    return values.at[spots[0]].set(low).at[spots[1]].set(top_value)


def levels(key, extent, pieces, smallest, high):
    factor_of, own = 1.0, jax.random.fold_in(key, 6)
    for axis_at, blocks in pieces:
        heights = jnp.exp(jax.random.uniform(jax.random.fold_in(own, axis_at), (blocks,), jnp.float32, smallest / len(pieces), high / len(pieces)))
        factor_of = factor_of * jnp.repeat(heights, extent[axis_at] // blocks).reshape([-1 if axis == axis_at else 1 for axis in range(len(extent))])
    return factor_of


def normal_values(key, shape, spread, reach, cuts=(), held_as=jnp.bfloat16):
    entries = spread * jax.random.normal(key, shape, jnp.float32)
    if cuts:
        entries = entries * levels(key, shape, cuts, -0.22, 0.18)
    return jnp.clip(entries, -reach, reach).astype(held_as)


def setup_inputs(seed: int = 0) -> dict:
    keys = jax.random.split(jax.random.key(seed), 12)
    grid_feat = normal_values(keys[0], (GRID, D), 1.0, 6.0, ((0, 64), (1, 2)))
    mesh_feat = normal_values(keys[1], (MESH, D), 1.0, 6.0, ((0, 64), (1, 2)))
    edge_src = draw_edge_src(jax.random.fold_in(keys[11], 71), 0)
    degree = touch_ends(jax.random.randint(keys[3], (MESH,), K // 2, K + 1), jax.random.fold_in(keys[3], 1), K // 2, K).astype(jnp.int32)
    offsets = draw_offsets(jax.random.fold_in(keys[11], 71), 0)
    w_kv = normal_values(keys[5], (2, D, D), D ** -0.5, 0.1875, ((2, 2),))
    w_query = normal_values(keys[6], (D, D), D ** -0.5, 0.1875, ((1, 2),))
    w_out = normal_values(keys[7], (D, D), D ** -0.5, 0.1875, ((0, 2),))
    w_mesh = normal_values(keys[8], (3, D, D), D ** -0.5, 0.1875, ((2, 2),))
    w_mesh_out = normal_values(keys[9], (D, D), D ** -0.5, 0.1875, ((0, 2),))
    cotangent = normal_values(keys[10], (MESH, D), 1.0, 6.0, ((0, 64), (1, 2)))
    return dict(grid_feat=grid_feat, mesh_feat=mesh_feat, edge_src=edge_src, degree=degree, offsets=offsets, w_kv=w_kv, w_query=w_query, w_out=w_out, w_mesh=w_mesh, w_mesh_out=w_mesh_out, cotangent=cotangent)


score_cap = 3.0

def capped_softmax(query, key_rows, live):
    rows, slots = (key_rows.shape[0], key_rows.shape[1])
    query_heads = query.astype(jnp.float32).reshape(rows, HEADS, HEAD_SIZE)
    key_heads = key_rows.astype(jnp.float32).reshape(rows, slots, HEADS, HEAD_SIZE)
    raw_scores = jnp.einsum('nzi,ngzi->ngz', query_heads, key_heads) / math.sqrt(HEAD_SIZE)
    capped = score_cap * jnp.tanh(raw_scores / score_cap)
    weights = jnp.where(live[:, :, None], jnp.exp(capped), 0.0)
    prob = weights / lax.optimization_barrier(jnp.sum(weights, axis=1, keepdims=True))
    return (prob, capped)

def weighted(prob_matrix, value_rows):
    rows, slots = (value_rows.shape[0], value_rows.shape[1])
    value_heads = value_rows.astype(jnp.float32).reshape(rows, slots, HEADS, HEAD_SIZE)
    attention_output = jnp.einsum('ztg,ztgw->zgw', prob_matrix.astype(jnp.float32), value_heads)
    return attention_output.reshape(rows, D).astype(jnp.bfloat16)

def reference(grid_feat, mesh_feat, edge_src, degree, offsets, w_kv, w_query, w_out, w_mesh, w_mesh_out, cotangent):
    key_rows = jnp.dot(grid_feat, w_kv[0], preferred_element_type=jnp.float32).astype(jnp.bfloat16)
    value_rows = jnp.dot(grid_feat, w_kv[1], preferred_element_type=jnp.float32).astype(jnp.bfloat16)
    query = jnp.dot(mesh_feat, w_query, preferred_element_type=jnp.float32).astype(jnp.bfloat16)
    edge_keys = key_rows[edge_src]
    edge_values = value_rows[edge_src]
    live = jnp.arange(K, dtype=jnp.int32)[None, :] < degree[:, None]
    prob, capped = capped_softmax(query, edge_keys, live)
    prob_matrix = prob.astype(jnp.bfloat16)
    attention_weights = weighted(prob_matrix, edge_values)
    encoded = (mesh_feat.astype(jnp.float32) + jnp.dot(attention_weights, w_out, preferred_element_type=jnp.float32)).astype(jnp.bfloat16)
    mesh_q = jnp.dot(encoded, w_mesh[0], preferred_element_type=jnp.float32).astype(jnp.bfloat16)
    mesh_k = jnp.dot(encoded, w_mesh[1], preferred_element_type=jnp.float32).astype(jnp.bfloat16)
    mesh_v = jnp.dot(encoded, w_mesh[2], preferred_element_type=jnp.float32).astype(jnp.bfloat16)
    position = jnp.arange(MESH, dtype=jnp.int32)[:, None] + offsets[None, :]
    valid = (position >= 0) & (position < MESH)
    clipped = jnp.clip(position, 0, MESH - 1).astype(jnp.int32)
    mesh_prob, mesh_capped = capped_softmax(mesh_q, mesh_k[clipped], valid)
    matt = weighted(mesh_prob.astype(jnp.bfloat16), mesh_v[clipped])
    mesh_out = (encoded.astype(jnp.float32) + jnp.dot(matt, w_mesh_out, preferred_element_type=jnp.float32)).astype(jnp.bfloat16)
    d_att = jnp.dot(cotangent, w_out.T, preferred_element_type=jnp.float32).astype(jnp.bfloat16)
    head_width = d_att.astype(jnp.float32).reshape(MESH, HEADS, HEAD_SIZE)
    value_heads = edge_values.astype(jnp.float32).reshape(MESH, K, HEADS, HEAD_SIZE)
    prob_gradient = jnp.einsum('nzi,ngzi->ngz', head_width, value_heads)
    ds = prob * (prob_gradient - lax.optimization_barrier(jnp.sum(prob * prob_gradient, axis=1, keepdims=True)))
    dr = ds * (1.0 - (capped / score_cap) ** 2) / math.sqrt(HEAD_SIZE)
    query_heads = query.astype(jnp.float32).reshape(MESH, HEADS, HEAD_SIZE)
    dk_edges = (dr[:, :, :, None] * query_heads[:, None, :, :]).reshape(MESH * K, D)
    dv_edges = (prob_matrix.astype(jnp.float32)[:, :, :, None] * head_width[:, None, :, :]).reshape(MESH * K, D)
    flat_src = edge_src.reshape(MESH * K)
    grad_k = jax.ops.segment_sum(dk_edges, flat_src, num_segments=GRID).astype(jnp.bfloat16)
    grad_v = jax.ops.segment_sum(dv_edges, flat_src, num_segments=GRID).astype(jnp.bfloat16)
    grad_kv = jnp.stack([jnp.dot(grid_feat.T, grad_k, preferred_element_type=jnp.float32), jnp.dot(grid_feat.T, grad_v, preferred_element_type=jnp.float32)])
    grad_grid = (jnp.dot(grad_k, w_kv[0].T, preferred_element_type=jnp.float32) + jnp.dot(grad_v, w_kv[1].T, preferred_element_type=jnp.float32)).astype(jnp.bfloat16)
    return (encoded, mesh_out, grad_grid, grad_kv)
```

```python
import functools

import jax
import jax.numpy as jnp
from jax import lax
from jax.experimental import pallas as pl
from jax.experimental.pallas import tpu as pltpu
from jax.sharding import PartitionSpec as P

BF = jnp.bfloat16
F32 = jnp.float32
I32 = jnp.int32
MESH = pl.DeviceIdType.MESH

M = 128
K = 16
G = 2048
RIM = 128
WIDE = G + 2 * RIM
R = 32
W = 16
F = 512
HL = 8
SPACE = 64
CHIPS = SPACE // 2
CAP = 3.0
SCALE = 0.125

E1M, E1C, HUP, HDOWN, WY, WFWD, E2, E3, E4, E5, E6, KUP, KDOWN, E8, GUP, GDOWN, PRE, SWAP = range(18)
N_REMOTE = 18


def dot(a, b):
    return jnp.dot(a, b, preferred_element_type=F32)


def dot_t(a, b):
    return lax.dot_general(a, b, (((1,), (1,)), ((), ())), preferred_element_type=F32)


def dot_first(a, b):
    return lax.dot_general(a, b, (((0,), (0,)), ((), ())), preferred_element_type=F32)


def iota(shape, dim):
    return lax.broadcasted_iota(I32, shape, dim)


def body(
    grid_in, mesh_in, src, deg, off, wkv_in, wq_in, wo_in, wm_in, wmo_in, cot_in,
    enc_out, mesh_out, gg_out, gkv_out,
    wide, mf, cf, wkv_own, wkv_oth, wq, wo, wm, wmo, qd, qdt, xs, ut, zy, srow,
    sd, sd_send, sd_recv, pb, att_own, att_send, att_recv, enc_own, enc_send, enc_recv, ef, mkv, mq,
    mo_own, mo_send, mo_recv, mo_val, gedge, halo_send, halo_recv, ggs,
    gb, pre, rsb, fin,
    lsem, osem, ssem, rsem, rs_s, rs_r, ag_s, ag_r, fw_s, fw_r,
):
    s = lax.axis_index("space")
    g = lax.axis_index("head")
    o = 1 - g
    core = s % 2
    chip = s // 2
    sib = s + 1 - 2 * core
    up = (s + 1) % SPACE
    down = (s + SPACE - 1) % SPACE
    ylo = (s // 8) % 2
    across = s + 8 - 16 * ylo
    far = s - 1 + 2 * core
    far = (far + SPACE) % SPACE

    def remote(src_ref, dst_ref, n, dev):
        return pltpu.make_async_remote_copy(
            src_ref=src_ref, dst_ref=dst_ref, send_sem=ssem.at[n], recv_sem=rsem.at[n],
            device_id=dev, device_id_type=MESH,
        )

    partner = (s, o)
    mine = pl.ds(pl.multiple_of(g * F, F), F)
    other = pl.ds(pl.multiple_of(o * F, F), F)

    local = [
        (mesh_in, mf.at[0]),
        (cot_in, cf.at[0]),
        (wq_in.at[mine, :], wq.at[0]),
        (wo_in.at[:, mine], wo.at[0]),
        (wq_in.at[other, :], wq.at[1]),
        (wo_in.at[:, other], wo.at[1]),
        (wkv_in.at[:, mine, :], wkv_own),
        (grid_in, wide.at[pl.ds(RIM, G), :]),
        (wm_in.at[:, mine, :], wm.at[0]),
        (wm_in.at[:, other, :], wm.at[1]),
        (wmo_in.at[:, mine], wmo.at[0]),
        (wmo_in.at[:, other], wmo.at[1]),
    ]
    loads = [pltpu.make_async_copy(a, b, lsem.at[i]) for i, (a, b) in enumerate(local)]
    for c in loads:
        c.start()

    barrier = pltpu.get_barrier_semaphore()
    for dev in (partner, (across, o), (sib, g), (far, g)):
        pl.semaphore_signal(barrier, inc=1, device_id=dev, device_id_type=MESH)

    def greet(i, carry):
        pl.semaphore_signal(
            barrier, inc=1, device_id=(((chip + i) % CHIPS) * 2 + core, g), device_id_type=MESH
        )
        return carry

    lax.fori_loop(1, CHIPS, greet, 0)
    pl.semaphore_wait(barrier, 4 + CHIPS - 1)

    e1m = remote(mesh_in, mf.at[1], E1M, partner)
    e1c = remote(cot_in, cf.at[1], E1C, partner)
    hup = remote(grid_in.at[pl.ds(G - RIM, RIM), :], wide.at[pl.ds(0, RIM), :], HUP, (up, g))
    hdown = remote(grid_in.at[pl.ds(0, RIM), :], wide.at[pl.ds(RIM + G, RIM), :], HDOWN, (down, g))
    wy = remote(wkv_in.at[core, other, :], wkv_oth.at[core], WY, (across, o))
    wfwd = remote(wkv_oth.at[core], wkv_oth.at[core], WFWD, (sib, g))
    e1m.start()
    e1c.start()
    hup.start()
    hdown.start()
    wy.start()

    base = s * G - RIM
    rel = src[...] - base
    rel = jnp.where((rel >= 0) & (rel < WIDE), rel, 4095)
    hi = (rel // 64).astype(F32).astype(BF)
    lo = (rel % 64).astype(F32).astype(BF)
    spread = jnp.where(iota((K, 256), 0) == (iota((K, 256), 1) & 15), 1.0, 0.0).astype(BF)
    flat = dot(hi, spread) * 64.0 + dot(lo, spread)
    flat = jnp.where((iota((M, 256), 0) & 15) == iota((M, 256), 1) // 16, flat, 0.0)
    for t in range(8):
        srow[0:1, t * 256 : (t + 1) * 256] = jnp.sum(
            flat[t * 16 : (t + 1) * 16], axis=0, keepdims=True
        )

    for n in (0, 1, 2, 3):
        loads[n].wait()
    qa = dot(mf[0], wq[0])
    da = dot_t(cf[0], wo[0])
    loads[4].wait()
    loads[5].wait()
    e1m.wait_recv()
    e1c.wait_recv()
    qa = qa + dot(mf[1], wq[1])
    da = da + dot_t(cf[1], wo[1])
    qd[0, 0] = qa.astype(BF)
    qd[0, 1] = da.astype(BF)
    e2 = remote(qd.at[0], qd.at[1], E2, partner)
    e2.start()

    def turn(side):
        for k in range(2):
            qdt[side, k] = qd[side, k].astype(F32).T.astype(BF)

    turn(0)

    def expand(side, weights):
        for k in range(2):
            for a in range(2):
                x4 = qd[side, k, :, a * 256 : (a + 1) * 256].astype(F32)
                head = iota((M, 256), 1) // 64
                lhs = jnp.concatenate(
                    [jnp.where(head == i, x4, 0.0).astype(BF) for i in range(4)], axis=0
                )
                out = dot_t(lhs, weights[k, :, a * 256 : (a + 1) * 256]).astype(BF)
                n = side * HL + a * 4
                ut[k, n : n + 4] = out.reshape(4, M, F)

    loads[6].wait()
    expand(0, wkv_own)

    loads[7].wait()
    hup.wait_recv()
    hdown.wait_recv()

    def gather(t, carry):
        n = pl.multiple_of(t * 32, 32)
        part = (src[pl.ds(n, 32), :] - base).astype(F32)
        part = jnp.broadcast_to(part[:, None, :], (32, K, K)).reshape(512, K)
        pick = (iota((512, K), 0) & 15) == iota((512, K), 1)
        col = jnp.sum(jnp.where(pick, part, 0.0), axis=1, keepdims=True).astype(I32)
        hot = jnp.where(iota((512, WIDE), 1) == col, 1.0, 0.0).astype(BF)
        xs[pl.ds(pl.multiple_of(t * 512, 512), 512), :] = dot(hot, wide[...]).astype(BF)
        return carry

    lax.fori_loop(0, 4, gather, 0)

    wy.wait_recv()
    wfwd.start()
    e2.wait_recv()
    turn(1)
    pltpu.make_async_remote_copy(
        src_ref=wkv_oth.at[1 - core], dst_ref=wkv_oth.at[1 - core], send_sem=ssem.at[WFWD],
        recv_sem=rsem.at[WFWD], device_id=(sib, g), device_id_type=MESH,
    ).wait_recv()
    expand(1, wkv_oth)

    def scores(t, carry):
        xg = xs[pl.ds(pl.multiple_of(t * 256, 256), 256), :]
        lane = iota((K, 256), 1) & 15
        for k in range(2):
            ug = ut[k, :, pl.ds(pl.multiple_of(t * 16, 16), 16), :].reshape(256, F)
            full = dot_t(xg, ug).reshape(16, K, 256)
            total = jnp.zeros((K, 256), F32)
            for m in range(16):
                total = total + jnp.where(lane == m, full[m], 0.0)
            sd[k, t] = total
            sd_send[k, t] = total.astype(BF)
        return carry

    lax.fori_loop(0, 8, scores, 0)
    e3 = remote(sd_send, sd_recv, E3, partner)
    e3.start()

    dg = deg[...].astype(F32)
    dg = jnp.where(iota((8, M), 1) // 16 == iota((8, M), 0), dg, 0.0).astype(BF)
    tile = jnp.where((iota((M, 128), 0) & 15) == (iota((M, 128), 1) & 15), 1.0, 0.0).astype(BF)
    dlane = dot(dg, tile)
    live = iota((8, K, 128), 1).astype(F32) < dlane[:, None, :]

    e3.wait_recv()
    for side in range(2):
        a, b = side * 128, (1 - side) * 128
        raw = (sd[0, :, :, a : a + 128] + sd_recv[0, :, :, b : b + 128].astype(F32)) * SCALE
        dp = sd[1, :, :, a : a + 128] + sd_recv[1, :, :, b : b + 128].astype(F32)
        th = jnp.tanh(raw * (1.0 / CAP))
        wgt = jnp.where(live, jnp.exp(CAP * th), 0.0)
        prob = wgt / jnp.sum(wgt, axis=1, keepdims=True)
        ds = prob * (dp - jnp.sum(prob * dp, axis=1, keepdims=True))
        dr = ds * (1.0 - th * th) * SCALE
        pb[0, :, :, a : a + 128] = prob.astype(BF)
        pb[1, :, :, a : a + 128] = dr.astype(BF)

    def sums(t, carry):
        xg = xs[pl.ds(pl.multiple_of(t * 256, 256), 256), :]
        same = (iota((256, 256), 0) & 15) == iota((256, 256), 1) // 16
        sel = jnp.where(iota((K, 256), 0) == (iota((K, 256), 1) & 15), 1.0, 0.0).astype(BF)
        for k in range(2):
            pt = jnp.where(same, dot_first(pb[k, t], sel), 0.0).astype(BF)
            out = dot(pt, xg).astype(BF)
            zy[k, :, pl.ds(pl.multiple_of(t * 16, 16), 16), :] = out.reshape(16, 16, F)
        return carry

    lax.fori_loop(0, 8, sums, 0)

    def diagonal(x):
        x = x.reshape(4, M, 256)
        head = iota((M, 256), 1) // 64
        out = jnp.zeros((M, 256), F32)
        for i in range(4):
            out = out + jnp.where(head == i, x[i], 0.0)
        return out

    for a in range(2):
        z4 = zy[0, HL + a * 4 : HL + a * 4 + 4].reshape(4 * M, F)
        att_send[:, a * 256 : (a + 1) * 256] = diagonal(
            dot(z4, wkv_oth[1, :, a * 256 : (a + 1) * 256])
        ).astype(BF)
    e4 = remote(att_send, att_recv, E4, partner)
    e4.start()
    for a in range(2):
        z4 = zy[0, a * 4 : a * 4 + 4].reshape(4 * M, F)
        att_own[:, a * 256 : (a + 1) * 256] = diagonal(
            dot(z4, wkv_own[1, :, a * 256 : (a + 1) * 256])
        )

    def weight_terms(n, carry):
        k = (1 - core) + n * (2 * core - 1)
        for side in range(2):
            block0 = (g if side == 0 else o) * 16
            for p in range(4):
                x = qdt[side, k, p * 128 : (p + 1) * 128, :].astype(F32)
                first = iota((128, M), 0) < 64
                lhs = jnp.concatenate(
                    [jnp.where(first, x, 0.0).astype(BF), jnp.where(first, 0.0, x).astype(BF)], axis=1
                )
                h = side * HL + 2 * p
                rhs = zy[1 - k, h : h + 2].reshape(2 * M, F)
                out = dot(lhs, rhs).astype(BF)
                for f in range(4):
                    gb[k, block0 + p * 4 + f] = out[:, f * 128 : (f + 1) * 128]
        return carry

    weight_terms(0, 0)
    presum = remote(gb.at[1 - core], pre, PRE, (sib, g))
    presum.start()
    weight_terms(1, 0)

    e4.wait_recv()
    att = (att_own[...] + att_recv[...].astype(F32)).astype(BF)
    enc_send[...] = dot(att, wo[1]).astype(BF)
    e5 = remote(enc_send, enc_recv, E5, partner)
    e5.start()
    enc_own[...] = dot(att, wo[0])

    presum.wait_recv()

    def scatter_copy(i):
        block = ((chip + i) % CHIPS + 16 * g) % CHIPS
        return pltpu.make_async_remote_copy(
            src_ref=gb.at[core, block], dst_ref=rsb.at[i], send_sem=rs_s.at[i], recv_sem=rs_r.at[i],
            device_id=(((chip + i) % CHIPS) * 2 + core, g), device_id_type=MESH,
        )

    def reduce_send(i, carry):
        block = ((chip + i) % CHIPS + 16 * g) % CHIPS
        gb[core, block] = (gb[core, block].astype(F32) + pre[block].astype(F32)).astype(BF)
        scatter_copy(i).start()
        return carry

    lax.fori_loop(1, CHIPS, reduce_send, 0)

    e5.wait_recv()
    enc = (mf[0].astype(F32) + enc_own[...] + enc_recv[...].astype(F32)).astype(BF)
    ef[0] = enc
    e6 = remote(ef.at[0], ef.at[1], E6, partner)
    e6.start()
    enc_copy = pltpu.make_async_copy(ef.at[0], enc_out, osem.at[0])
    enc_copy.start()

    def edge_grads(t, carry):
        rows = pl.ds(pl.multiple_of(t * 16, 16), 16)
        match = (iota((16, K, 256), 2) & 15) == iota((16, K, 256), 0)
        total = jnp.zeros((256, F), F32)
        for k in range(2):
            p = jnp.broadcast_to(pb[1 - k, t].astype(F32)[None], (16, K, 256))
            p = jnp.where(match, p, 0.0).astype(BF).reshape(256, 256)
            total = total + dot(p, ut[k, :, rows, :].reshape(256, F))
        gedge[pl.ds(pl.multiple_of(t * 256, 256), 256), :] = total.astype(BF)
        return carry

    lax.fori_loop(0, 8, edge_grads, 0)

    loads[8].wait()
    loads[9].wait()
    e6.wait_recv()
    for k in range(2):
        mkv[k, R : R + M, :] = (dot(ef[0], wm[0, 1 + k]) + dot(ef[1], wm[1, 1 + k])).astype(BF)
    kup = remote(mkv.at[:, pl.ds(M, R), :], mkv.at[:, pl.ds(0, R), :], KUP, (up, g))
    kdown = remote(mkv.at[:, pl.ds(R, R), :], mkv.at[:, pl.ds(R + M, R), :], KDOWN, (down, g))
    kup.start()
    kdown.start()
    mq[...] = (dot(ef[0], wm[0, 0]) + dot(ef[1], wm[1, 0])).astype(BF)

    def rows_of(first, count):
        hot = jnp.where(
            (iota((count, G), 0) + first).astype(F32) == srow[0:1, :], 1.0, 0.0
        ).astype(BF)
        return dot(hot, gedge[...])

    halo_send[0] = rows_of(0, RIM).astype(BF)
    halo_send[1] = rows_of(RIM + G, RIM).astype(BF)
    gdown = remote(halo_send.at[0], halo_recv.at[1], GDOWN, (down, g))
    gup = remote(halo_send.at[1], halo_recv.at[0], GUP, (up, g))
    gdown.start()
    gup.start()

    where_n = iota((M, 256), 1) - R
    delta = where_n - iota((M, 256), 0)
    allowed = delta == off[0]
    for j in range(1, W):
        allowed = allowed | (delta == off[j])
    where_g = where_n + s * M
    allowed = allowed & (where_g >= 0) & (where_g < M * SPACE)
    allow = jnp.where(allowed[:, : M + 2 * R], 1.0, 0.0)
    allow4 = jnp.concatenate([allow] * 4, axis=0)
    kup.wait_recv()
    kdown.wait_recv()
    matts = []
    for a in range(2):
        cols = slice(a * 256, (a + 1) * 256)
        x4 = mq[:, cols].astype(F32)
        head = iota((M, 256), 1) // 64
        lhs = jnp.concatenate([jnp.where(head == i, x4, 0.0).astype(BF) for i in range(4)], axis=0)
        raw = dot_t(lhs, mkv[0, :, cols]) * SCALE
        wgt = jnp.exp(CAP * jnp.tanh(raw * (1.0 / CAP))) * allow4
        prob = (wgt / jnp.sum(wgt, axis=1, keepdims=True)).astype(BF)
        matts.append(diagonal(dot(prob, mkv[1, :, cols])).astype(BF))
    matt = jnp.concatenate(matts, axis=1)
    loads[10].wait()
    loads[11].wait()
    mo_send[...] = dot(matt, wmo[1]).astype(BF)
    e8 = remote(mo_send, mo_recv, E8, partner)
    e8.start()
    mo_own[...] = dot(matt, wmo[0])

    own_block = (chip + 16 * g) % CHIPS
    block_sum = gb[core, own_block].astype(F32) + pre[own_block].astype(F32)

    def reduce_recv(i, total):
        scatter_copy(i).wait_recv()
        return total + rsb[i].astype(F32)

    block_sum = lax.fori_loop(1, CHIPS, reduce_recv, block_sum)
    fin[0] = block_sum.T.astype(BF)
    swap = remote(fin.at[0], fin.at[1], SWAP, partner)
    swap.start()

    def interior(t, carry):
        n = pl.multiple_of(t * 512, 512)
        ggs[pl.ds(n, 512), :] = rows_of(n + RIM, 512).astype(BF)
        return carry

    lax.fori_loop(0, 1, interior, 0)

    swap.wait_recv()
    late = chip // 16

    def place(k, c):
        half = g + (c // 16) * (1 - 2 * g)
        row = pl.multiple_of((half * 4 + c % 4) * 128, 128)
        col = pl.multiple_of(((c % 16) // 4) * 128, 128)
        return gkv_out.at[k, pl.ds(row, 128), pl.ds(col, 128)]

    def spread_copy(i, c):
        return pltpu.make_async_remote_copy(
            src_ref=fin.at[late], dst_ref=place(core, c), send_sem=ag_s.at[i], recv_sem=ag_r.at[i],
            device_id=(((chip + i) % CHIPS) * 2 + core, g), device_id_type=MESH,
        )

    def pass_copy(i, k):
        c = (chip + CHIPS - i) % CHIPS
        return pltpu.make_async_remote_copy(
            src_ref=place(k, c), dst_ref=place(k, c), send_sem=fw_s.at[i], recv_sem=fw_r.at[i],
            device_id=(sib, g), device_id_type=MESH,
        )

    def spread_send(i, carry):
        spread_copy(i, chip).start()
        return carry

    lax.fori_loop(1, CHIPS, spread_send, 0)
    own_copy = pltpu.make_async_copy(fin.at[late], place(core, chip), osem.at[1])
    own_copy.start()

    lax.fori_loop(1, 4, interior, 0)
    gdown.wait_recv()
    gup.wait_recv()
    ggs[0:RIM, :] = (ggs[0:RIM, :].astype(F32) + halo_recv[0].astype(F32)).astype(BF)
    ggs[G - RIM : G, :] = (ggs[G - RIM : G, :].astype(F32) + halo_recv[1].astype(F32)).astype(BF)
    gg_copy = pltpu.make_async_copy(ggs, gg_out, osem.at[2])
    gg_copy.start()

    e8.wait_recv()
    mo_val[...] = (ef[0].astype(F32) + mo_own[...] + mo_recv[...].astype(F32)).astype(BF)
    mo_copy = pltpu.make_async_copy(mo_val, mesh_out, osem.at[3])
    mo_copy.start()

    own_copy.wait()
    pass_copy(0, core).start()

    def pass_on(i, carry):
        spread_copy(i, (chip + CHIPS - i) % CHIPS).wait_recv()
        pass_copy(i, core).start()
        return carry

    lax.fori_loop(1, CHIPS, pass_on, 0)

    def finish(i, carry):
        pass_copy(i, 1 - core).wait_recv()
        pass_copy(i, core).wait_send()
        return carry

    lax.fori_loop(0, CHIPS, finish, 0)

    def sent(i, carry):
        scatter_copy(i).wait_send()
        spread_copy(i, chip).wait_send()
        return carry

    lax.fori_loop(1, CHIPS, sent, 0)
    for c in (e1m, e1c, hup, hdown, wy, wfwd, e2, e3, e4, e5, e6, kup, kdown, e8, gdown, gup, presum, swap):
        c.wait_send()
    enc_copy.wait()
    gg_copy.wait()
    mo_copy.wait()


def shards(
    grid_feat, mesh_feat, edge_src, degree, offsets, w_kv, w_query, w_out, w_mesh, w_mesh_out, cotangent
):
    hbm = pl.BlockSpec(memory_space=pl.ANY)
    vmem = pl.BlockSpec(memory_space=pltpu.VMEM)
    smem = pl.BlockSpec(memory_space=pltpu.SMEM)

    def v(*shape, dtype=BF):
        return pltpu.VMEM(shape, dtype)

    dma = pltpu.SemaphoreType.DMA
    scratch = dict(
        wide=v(WIDE, F), mf=v(2, M, F), cf=v(2, M, F), wkv_own=v(2, F, F), wkv_oth=v(2, F, F),
        wq=v(2, F, F), wo=v(2, F, F), wm=v(2, 3, F, F), wmo=v(2, F, F),
        qd=v(2, 2, M, F), qdt=v(2, 2, F, M), xs=v(G, F), ut=v(2, 16, M, F), zy=v(2, 16, M, F),
        srow=v(8, G, dtype=F32),
        sd=v(2, 8, K, 256, dtype=F32), sd_send=v(2, 8, K, 256), sd_recv=v(2, 8, K, 256), pb=v(2, 8, K, 256),
        att_own=v(M, F, dtype=F32), att_send=v(M, F), att_recv=v(M, F),
        enc_own=v(M, F, dtype=F32), enc_send=v(M, F), enc_recv=v(M, F), ef=v(2, M, F),
        mkv=v(2, M + 2 * R, F), mq=v(M, F),
        mo_own=v(M, F, dtype=F32), mo_send=v(M, F), mo_recv=v(M, F), mo_val=v(M, F),
        gedge=v(G, F), halo_send=v(2, RIM, F), halo_recv=v(2, RIM, F), ggs=v(G, F),
        gb=v(2, CHIPS, 128, 128), pre=v(CHIPS, 128, 128), rsb=v(CHIPS, 128, 128), fin=v(2, 128, 128),
        lsem=dma((12,)), osem=dma((4,)), ssem=dma((N_REMOTE,)), rsem=dma((N_REMOTE,)),
        rs_s=dma((CHIPS,)), rs_r=dma((CHIPS,)), ag_s=dma((CHIPS,)), ag_r=dma((CHIPS,)),
        fw_s=dma((CHIPS,)), fw_r=dma((CHIPS,)),
    )
    enc, mesh_out, grad_grid, grad_kv = pl.pallas_call(
        body,
        out_shape=(
            jax.ShapeDtypeStruct((M, F), BF),
            jax.ShapeDtypeStruct((M, F), BF),
            jax.ShapeDtypeStruct((G, F), BF),
            jax.ShapeDtypeStruct((2, 2 * F, F), BF),
        ),
        in_specs=[hbm, hbm, vmem, vmem, smem, hbm, hbm, hbm, hbm, hbm, hbm],
        out_specs=(hbm, hbm, hbm, hbm),
        scratch_shapes=list(scratch.values()),
        compiler_params=pltpu.CompilerParams(
            collective_id=0, has_side_effects=True, vmem_limit_bytes=58 * 2**20
        ),
        name="encoder",
    )(
        grid_feat, mesh_feat, edge_src, degree.reshape(1, M), offsets, w_kv, w_query, w_out, w_mesh,
        w_mesh_out, cotangent,
    )
    return enc, mesh_out, grad_grid, grad_kv.astype(F32)


def solution(mesh):
    in_specs = (
        P("space", "head"),
        P("space", "head"),
        P("space", None),
        P("space"),
        P(),
        P(None, None, "head"),
        P(None, "head"),
        P("head", None),
        P(None, None, "head"),
        P("head", None),
        P("space", "head"),
    )
    out_specs = (P("space", "head"), P("space", "head"), P("space", "head"), P(None, None, "head"))
    return jax.shard_map(shards, mesh=mesh, in_specs=in_specs, out_specs=out_specs, check_vma=False)
```

```python
import functools

import jax
import jax.numpy as jnp
from jax import lax
from jax.experimental import pallas as pl
from jax.experimental.pallas import tpu as pltpu
from jax.sharding import PartitionSpec as P

BF = jnp.bfloat16
F32 = jnp.float32
I32 = jnp.int32
MESH = pl.DeviceIdType.MESH

M = 128
K = 16
G = 2048
RIM = 128
WIDE = G + 2 * RIM
R = 32
W = 16
F = 512
HL = 8
SPACE = 64
CHIPS = SPACE // 2
CAP = 3.0
SCALE = 0.125

(
    E1M, E1C, HUP, HDOWN, WY, WX, WZ, WXZ, E2, E3, E4, E5, E6, KUP, KDOWN, E8, GUP, GDOWN, AGP,
    WF, PRE,
) = list(range(20)) + [23]
N_REMOTE = 27


def dot(a, b):
    return jnp.dot(a, b, preferred_element_type=F32)


def dot_t(a, b):
    return lax.dot_general(a, b, (((1,), (1,)), ((), ())), preferred_element_type=F32)


def dot_first(a, b):
    return lax.dot_general(a, b, (((0,), (0,)), ((), ())), preferred_element_type=F32)


def iota(shape, dim):
    return lax.broadcasted_iota(I32, shape, dim)


def body(
    grid_in, mesh_in, src, deg, off, wkv_in, wq_in, wo_in, wm_in, wmo_in, cot_in,
    enc_out, mesh_out, gg_out, gkv_out,
    nodes, wide, mf, cf, wkv_own, wkv_oth, wq, wo, wm, wmo, qd, qdt, xs, ut, zy, srow,
    sd, sd_send, sd_recv, pb, att_own, att_send, att_recv, enc_own, enc_send, enc_recv, ef, mkv, mq,
    mo_own, mo_send, mo_recv, mo_val, gedge, halo_send, halo_recv, ggs,
    gb, pre, rsb, fin,
    lsem, osem, ssem, rsem, rs_s, rs_r, ag_s, ag_r, fw_s, fw_r, known,
):
    s = lax.axis_index("space")
    g = lax.axis_index("head")
    o = 1 - g
    core = s % 2
    chip = s // 2
    sib = s + 1 - 2 * core
    up = (s + 1) % SPACE
    down = (s + SPACE - 1) % SPACE

    def flip(bit):
        return s + bit - 2 * bit * ((s // bit) % 2)

    across = flip(8)
    beside_x, beside_z = flip(16), flip(2)
    beside_xz = beside_x + beside_z - s
    quarter = (chip // 8 % 2) * 2 + chip % 2
    far = s - 1 + 2 * core
    far = (far + SPACE) % SPACE

    def remote(src_ref, dst_ref, n, dev):
        return pltpu.make_async_remote_copy(
            src_ref=src_ref, dst_ref=dst_ref, send_sem=ssem.at[n], recv_sem=rsem.at[n],
            device_id=dev, device_id_type=MESH,
        )

    partner = (s, o)
    mine = pl.ds(pl.multiple_of(g * F, F), F)
    other = pl.ds(pl.multiple_of(o * F, F), F)

    local = [
        (mesh_in, mf.at[0]),
        (cot_in, cf.at[0]),
        (wq_in.at[mine, :], wq.at[0]),
        (wo_in.at[:, mine], wo.at[0]),
        (wq_in.at[other, :], wq.at[1]),
        (wo_in.at[:, other], wo.at[1]),
        (wkv_in.at[:, mine, :], wkv_own),
        (grid_in, wide.at[pl.ds(RIM, G), :]),
        (wm_in.at[:, mine, :], wm.at[0]),
        (wm_in.at[:, other, :], wm.at[1]),
        (wmo_in.at[:, mine], wmo.at[0]),
        (wmo_in.at[:, other], wmo.at[1]),
    ]
    loads = [pltpu.make_async_copy(a, b, lsem.at[i]) for i, (a, b) in enumerate(local)]
    for c in loads:
        c.start()

    bits = [partner, (flip(2), g), (flip(4), g), (flip(8), g), (flip(16), g), (flip(32), g)]
    first = bits + [(across, o), (sib, g), (far, g), (beside_xz, g)]
    barrier = pltpu.get_barrier_semaphore()
    for dev in first:
        pl.semaphore_signal(barrier, inc=1, device_id=dev, device_id_type=MESH)
    pl.semaphore_wait(barrier, len(first))

    def tell(b):
        pl.semaphore_signal(known.at[b], inc=1, device_id=bits[b], device_id_type=MESH)

    def hear(b):
        pl.semaphore_wait(known.at[b], 1)

    e1m = remote(mesh_in, mf.at[1], E1M, partner)
    e1c = remote(cot_in, cf.at[1], E1C, partner)
    hup = remote(grid_in.at[pl.ds(G - RIM, RIM), :], wide.at[pl.ds(0, RIM), :], HUP, (up, g))
    hdown = remote(grid_in.at[pl.ds(0, RIM), :], wide.at[pl.ds(RIM + G, RIM), :], HDOWN, (down, g))

    def piece(k, q):
        return wkv_oth.at[k, pl.ds(pl.multiple_of(q * 128, 128), 128), :]

    other_rows = pl.ds(pl.multiple_of(o * F + quarter * 128, 128), 128)
    wy = remote(wkv_in.at[core, other_rows, :], piece(core, quarter), WY, (across, o))
    wx = remote(piece(core, quarter), piece(core, quarter), WX, (beside_x, g))
    wz = remote(piece(core, quarter), piece(core, quarter), WZ, (beside_z, g))
    wxz = remote(piece(core, quarter), piece(core, quarter), WXZ, (beside_xz, g))
    part = [quarter]
    part.append(quarter + 1 - 2 * (quarter % 2))
    part.append(quarter + 2 - 4 * (quarter // 2))
    part.append(part[1] + part[2] - quarter)
    wfwd = [remote(piece(core, q), piece(core, q), WF + n, (sib, g)) for n, q in enumerate(part)]
    wback = [remote(piece(1 - core, q), piece(1 - core, q), WF + n, (sib, g)) for n, q in enumerate(part)]
    wy.start()
    e1m.start()
    e1c.start()
    hup.start()
    hdown.start()
    tell(0)

    base = s * G - RIM
    source = src[...].astype(F32).T.astype(I32)
    nodes[...] = source
    rel = source - base
    rel = jnp.where((rel >= 0) & (rel < WIDE), rel, 4095)
    hi = (rel // 64).astype(F32).astype(BF)
    lo = (rel % 64).astype(F32).astype(BF)
    spread = jnp.where(iota((K, 256), 0) == (iota((K, 256), 1) & 15), 1.0, 0.0).astype(BF)
    flat = dot(hi, spread) * 64.0 + dot(lo, spread)
    flat = jnp.where((iota((M, 256), 0) & 15) == iota((M, 256), 1) // 16, flat, 0.0)
    for t in range(8):
        srow[0:1, t * 256 : (t + 1) * 256] = jnp.sum(
            flat[t * 16 : (t + 1) * 16], axis=0, keepdims=True
        )

    loads[7].wait()
    hup.wait_recv()
    hdown.wait_recv()

    def gather(t, carry):
        n = pl.multiple_of(t * 32, 32)
        part = (nodes[pl.ds(n, 32), :] - base).astype(F32)
        part = jnp.broadcast_to(part[:, None, :], (32, K, K)).reshape(512, K)
        pick = (iota((512, K), 0) & 15) == iota((512, K), 1)
        col = jnp.sum(jnp.where(pick, part, 0.0), axis=1, keepdims=True).astype(I32)
        hot = jnp.where(iota((512, WIDE), 1) == col, 1.0, 0.0).astype(BF)
        xs[pl.ds(pl.multiple_of(t * 512, 512), 512), :] = dot(hot, wide[...]).astype(BF)
        return carry


    lax.fori_loop(0, 2, gather, 0)
    wy.wait_recv()
    wx.start()
    wz.start()
    wxz.start()
    wfwd[0].start()
    hear(0)
    tell(1)
    lax.fori_loop(2, 3, gather, 0)

    for n in (0, 1, 2, 3):
        loads[n].wait()
    qa = dot(mf[0], wq[0])
    da = dot_t(cf[0], wo[0])
    loads[4].wait()
    loads[5].wait()
    e1m.wait_recv()
    e1c.wait_recv()
    qa = qa + dot(mf[1], wq[1])
    da = da + dot_t(cf[1], wo[1])
    qd[0, 0] = qa.astype(BF)
    qd[0, 1] = da.astype(BF)
    e2 = remote(qd.at[0], qd.at[1], E2, partner)
    e2.start()

    lax.fori_loop(3, 4, gather, 0)
    hear(1)
    tell(2)

    def turn(side):
        for k in range(2):
            qdt[side, k] = qd[side, k].astype(F32).T.astype(BF)

    turn(0)

    def expand(side, weights):
        for k in range(2):
            for a in range(2):
                x4 = qd[side, k, :, a * 256 : (a + 1) * 256].astype(F32)
                head = iota((M, 256), 1) // 64
                lhs = jnp.concatenate(
                    [jnp.where(head == i, x4, 0.0).astype(BF) for i in range(4)], axis=0
                )
                out = dot_t(lhs, weights[k, :, a * 256 : (a + 1) * 256]).astype(BF)
                n = side * HL + a * 4
                ut[k, n : n + 4] = out.reshape(4, M, F)

    loads[6].wait()
    expand(0, wkv_own)

    hear(2)
    tell(3)
    for n, c in ((1, wz), (2, wx), (3, wxz)):
        remote(piece(core, part[n]), piece(core, part[n]), (WZ, WX, WXZ)[n - 1], partner).wait_recv()
        wfwd[n].start()
    e2.wait_recv()
    turn(1)
    hear(3)
    tell(4)
    for c in wback:
        c.wait_recv()
    expand(1, wkv_oth)
    hear(4)
    tell(5)

    def scores(t, carry):
        xg = xs[pl.ds(pl.multiple_of(t * 256, 256), 256), :]
        lane = iota((K, 256), 1) & 15
        for k in range(2):
            ug = ut[k, :, pl.ds(pl.multiple_of(t * 16, 16), 16), :].reshape(256, F)
            full = dot_t(xg, ug).reshape(16, K, 256)
            total = jnp.zeros((K, 256), F32)
            for m in range(16):
                total = total + jnp.where(lane == m, full[m], 0.0)
            sd[k, t] = total
            sd_send[k, t] = total.astype(BF)
        return carry

    lax.fori_loop(0, 8, scores, 0)
    e3 = remote(sd_send, sd_recv, E3, partner)
    e3.start()

    hear(5)

    dg = deg[...].astype(F32)
    dg = jnp.where(iota((8, M), 1) // 16 == iota((8, M), 0), dg, 0.0).astype(BF)
    tile = jnp.where((iota((M, 128), 0) & 15) == (iota((M, 128), 1) & 15), 1.0, 0.0).astype(BF)
    dlane = dot(dg, tile)
    live = iota((8, K, 128), 1).astype(F32) < dlane[:, None, :]

    e3.wait_recv()
    for side in range(2):
        a, b = side * 128, (1 - side) * 128
        raw = (sd[0, :, :, a : a + 128] + sd_recv[0, :, :, b : b + 128].astype(F32)) * SCALE
        dp = sd[1, :, :, a : a + 128] + sd_recv[1, :, :, b : b + 128].astype(F32)
        th = jnp.tanh(raw * (1.0 / CAP))
        wgt = jnp.where(live, jnp.exp(CAP * th), 0.0)
        prob = wgt / jnp.sum(wgt, axis=1, keepdims=True)
        ds = prob * (dp - jnp.sum(prob * dp, axis=1, keepdims=True))
        dr = ds * (1.0 - th * th) * SCALE
        pb[0, :, :, a : a + 128] = prob.astype(BF)
        pb[1, :, :, a : a + 128] = dr.astype(BF)

    def sums(t, carry):
        xg = xs[pl.ds(pl.multiple_of(t * 256, 256), 256), :]
        same = (iota((256, 256), 0) & 15) == iota((256, 256), 1) // 16
        sel = jnp.where(iota((K, 256), 0) == (iota((K, 256), 1) & 15), 1.0, 0.0).astype(BF)
        for k in range(2):
            pt = jnp.where(same, dot_first(pb[k, t], sel), 0.0).astype(BF)
            out = dot(pt, xg).astype(BF)
            zy[k, :, pl.ds(pl.multiple_of(t * 16, 16), 16), :] = out.reshape(16, 16, F)
        return carry

    lax.fori_loop(0, 8, sums, 0)

    def diagonal(x):
        x = x.reshape(4, M, 256)
        head = iota((M, 256), 1) // 64
        out = jnp.zeros((M, 256), F32)
        for i in range(4):
            out = out + jnp.where(head == i, x[i], 0.0)
        return out

    for a in range(2):
        z4 = zy[0, HL + a * 4 : HL + a * 4 + 4].reshape(4 * M, F)
        att_send[:, a * 256 : (a + 1) * 256] = diagonal(
            dot(z4, wkv_oth[1, :, a * 256 : (a + 1) * 256])
        ).astype(BF)
    e4 = remote(att_send, att_recv, E4, partner)
    e4.start()
    for a in range(2):
        z4 = zy[0, a * 4 : a * 4 + 4].reshape(4 * M, F)
        att_own[:, a * 256 : (a + 1) * 256] = diagonal(
            dot(z4, wkv_own[1, :, a * 256 : (a + 1) * 256])
        )

    def weight_terms(n, carry):
        k = (1 - core) + n * (2 * core - 1)
        for side in range(2):
            for p in range(4):
                x = qdt[side, k, p * 128 : (p + 1) * 128, :].astype(F32)
                first = iota((128, M), 0) < 64
                lhs = jnp.concatenate(
                    [jnp.where(first, x, 0.0).astype(BF), jnp.where(first, 0.0, x).astype(BF)], axis=1
                )
                h = side * HL + 2 * p
                rhs = zy[1 - k, h : h + 2].reshape(2 * M, F)
                out = dot(lhs, rhs).astype(BF)
                for f in range(4):
                    place_at = (16 * side + 4 * p + f + CHIPS - chip) % CHIPS
                    gb[k, place_at] = out[:, f * 128 : (f + 1) * 128]
        return carry

    weight_terms(0, 0)
    presum = [
        remote(gb.at[1 - core, pl.ds(8 * n, 8)], pre.at[pl.ds(8 * n, 8)], PRE + n, (sib, g))
        for n in range(4)
    ]
    for c in presum:
        c.start()
    weight_terms(1, 0)

    def scatter_copy(i):
        return pltpu.make_async_remote_copy(
            src_ref=gb.at[core, i], dst_ref=rsb.at[i], send_sem=rs_s.at[i], recv_sem=rs_r.at[i],
            device_id=(((chip + i) % CHIPS) * 2 + core, g), device_id_type=MESH,
        )

    def reduce_send(i, carry):
        gb[core, i] = (gb[core, i].astype(F32) + pre[i].astype(F32)).astype(BF)
        scatter_copy(i).start()
        return carry

    for n in range(4):
        presum[n].wait_recv()
        lax.fori_loop(max(1, 8 * n), 8 * n + 8, reduce_send, 0)

    e4.wait_recv()
    att = (att_own[...] + att_recv[...].astype(F32)).astype(BF)
    enc_send[...] = dot(att, wo[1]).astype(BF)
    e5 = remote(enc_send, enc_recv, E5, partner)
    e5.start()
    enc_own[...] = dot(att, wo[0])

    def edge_grads(t, carry):
        rows = pl.ds(pl.multiple_of(t * 16, 16), 16)
        match = (iota((16, K, 256), 2) & 15) == iota((16, K, 256), 0)
        total = jnp.zeros((256, F), F32)
        for k in range(2):
            p = jnp.broadcast_to(pb[1 - k, t].astype(F32)[None], (16, K, 256))
            p = jnp.where(match, p, 0.0).astype(BF).reshape(256, 256)
            total = total + dot(p, ut[k, :, rows, :].reshape(256, F))
        gedge[pl.ds(pl.multiple_of(t * 256, 256), 256), :] = total.astype(BF)
        return carry

    lax.fori_loop(0, 8, edge_grads, 0)

    def rows_of(first, count):
        hot = jnp.where(
            (iota((count, G), 0) + first).astype(F32) == srow[0:1, :], 1.0, 0.0
        ).astype(BF)
        return dot(hot, gedge[...])

    halo_send[0] = rows_of(0, RIM).astype(BF)
    halo_send[1] = rows_of(RIM + G, RIM).astype(BF)
    gdown = remote(halo_send.at[0], halo_recv.at[1], GDOWN, (down, g))
    gup = remote(halo_send.at[1], halo_recv.at[0], GUP, (up, g))
    gdown.start()
    gup.start()

    e5.wait_recv()
    enc = (mf[0].astype(F32) + enc_own[...] + enc_recv[...].astype(F32)).astype(BF)
    ef[0] = enc
    e6 = remote(ef.at[0], ef.at[1], E6, partner)
    e6.start()
    enc_copy = pltpu.make_async_copy(ef.at[0], enc_out, osem.at[0])
    enc_copy.start()

    def interior(t, carry):
        n = pl.multiple_of(t * 512, 512)
        ggs[pl.ds(n, 512), :] = rows_of(n + RIM, 512).astype(BF)
        return carry

    lax.fori_loop(0, 2, interior, 0)

    loads[8].wait()
    loads[9].wait()
    e6.wait_recv()
    for k in range(2):
        mkv[k, R : R + M, :] = (dot(ef[0], wm[0, 1 + k]) + dot(ef[1], wm[1, 1 + k])).astype(BF)
    kup = remote(mkv.at[:, pl.ds(M, R), :], mkv.at[:, pl.ds(0, R), :], KUP, (up, g))
    kdown = remote(mkv.at[:, pl.ds(R, R), :], mkv.at[:, pl.ds(R + M, R), :], KDOWN, (down, g))
    kup.start()
    kdown.start()
    mq[...] = (dot(ef[0], wm[0, 0]) + dot(ef[1], wm[1, 0])).astype(BF)

    block_sum = gb[core, 0].astype(F32) + pre[0].astype(F32)

    def reduce_recv(i, total):
        scatter_copy(i).wait_recv()
        return total + rsb[i].astype(F32)

    block_sum = lax.fori_loop(1, CHIPS, reduce_recv, block_sum)
    fin[...] = block_sum.T.astype(BF)

    late = chip // 16
    group = g + late * (1 - 2 * g)

    def place(k, half, c):
        row = pl.multiple_of((half * 4 + c % 4) * 128, 128)
        col = pl.multiple_of(((c % 16) // 4) * 128, 128)
        return gkv_out.at[k, pl.ds(row, 128), pl.ds(col, 128)]

    def spread_copy(i):
        return pltpu.make_async_remote_copy(
            src_ref=fin, dst_ref=place(core, g, chip), send_sem=ag_s.at[i], recv_sem=ag_r.at[i],
            device_id=(((chip + i) % CHIPS) * 2 + core, group), device_id_type=MESH,
        )

    def arrived(i, k):
        c = (chip + CHIPS - i) % CHIPS
        return place(k, g + (c // 16) * (1 - 2 * g), c)

    def spread_recv(i):
        return pltpu.make_async_remote_copy(
            src_ref=fin, dst_ref=arrived(i, core), send_sem=ag_s.at[i], recv_sem=ag_r.at[i],
            device_id=partner, device_id_type=MESH,
        )

    def pass_copy(i, k):
        return pltpu.make_async_remote_copy(
            src_ref=arrived(i, k), dst_ref=arrived(i, k), send_sem=fw_s.at[i], recv_sem=fw_r.at[i],
            device_id=(sib, g), device_id_type=MESH,
        )

    own_copy = pltpu.make_async_copy(fin, place(core, g, chip), osem.at[1])
    own_send = remote(fin, place(core, g, chip), AGP, partner)

    @pl.when(late == 0)
    def _():
        own_copy.start()

    @pl.when(late == 1)
    def _():
        own_send.start()

    def spread_send(i, carry):
        spread_copy(i).start()
        return carry

    lax.fori_loop(1, CHIPS, spread_send, 0)

    where_n = iota((M, 256), 1) - R
    delta = where_n - iota((M, 256), 0)
    allowed = delta == off[0]
    for j in range(1, W):
        allowed = allowed | (delta == off[j])
    where_g = where_n + s * M
    allowed = allowed & (where_g >= 0) & (where_g < M * SPACE)
    allow = jnp.where(allowed[:, : M + 2 * R], 1.0, 0.0)
    allow4 = jnp.concatenate([allow] * 4, axis=0)
    kup.wait_recv()
    kdown.wait_recv()
    matts = []
    for a in range(2):
        cols = slice(a * 256, (a + 1) * 256)
        x4 = mq[:, cols].astype(F32)
        head = iota((M, 256), 1) // 64
        lhs = jnp.concatenate([jnp.where(head == i, x4, 0.0).astype(BF) for i in range(4)], axis=0)
        raw = dot_t(lhs, mkv[0, :, cols]) * SCALE
        wgt = jnp.exp(CAP * jnp.tanh(raw * (1.0 / CAP))) * allow4
        prob = (wgt / jnp.sum(wgt, axis=1, keepdims=True)).astype(BF)
        matts.append(diagonal(dot(prob, mkv[1, :, cols])).astype(BF))
    matt = jnp.concatenate(matts, axis=1)
    loads[10].wait()
    loads[11].wait()
    mo_send[...] = dot(matt, wmo[1]).astype(BF)
    e8 = remote(mo_send, mo_recv, E8, partner)
    e8.start()
    mo_own[...] = dot(matt, wmo[0])

    lax.fori_loop(2, 4, interior, 0)
    gdown.wait_recv()
    gup.wait_recv()
    ggs[0:RIM, :] = (ggs[0:RIM, :].astype(F32) + halo_recv[0].astype(F32)).astype(BF)
    ggs[G - RIM : G, :] = (ggs[G - RIM : G, :].astype(F32) + halo_recv[1].astype(F32)).astype(BF)
    gg_copy = pltpu.make_async_copy(ggs, gg_out, osem.at[2])
    gg_copy.start()

    e8.wait_recv()
    mo_val[...] = (ef[0].astype(F32) + mo_own[...] + mo_recv[...].astype(F32)).astype(BF)
    mo_copy = pltpu.make_async_copy(mo_val, mesh_out, osem.at[3])
    mo_copy.start()

    @pl.when(late == 0)
    def _():
        own_copy.wait()

    @pl.when(late == 1)
    def _():
        remote(fin, arrived(0, core), AGP, partner).wait()

    pass_copy(0, core).start()

    def pass_on(i, carry):
        spread_recv(i).wait_recv()
        pass_copy(i, core).start()
        return carry

    lax.fori_loop(1, CHIPS, pass_on, 0)

    def finish(i, carry):
        pass_copy(i, 1 - core).wait_recv()
        pass_copy(i, core).wait_send()
        return carry

    lax.fori_loop(0, CHIPS, finish, 0)

    def sent(i, carry):
        scatter_copy(i).wait_send()
        spread_copy(i).wait_send()
        return carry

    lax.fori_loop(1, CHIPS, sent, 0)
    singles = [e1m, e1c, hup, hdown, wy, wx, wz, wxz, e2, e3, e4, e5, e6, kup, kdown, e8, gdown, gup]
    for c in singles + wfwd + presum:
        c.wait_send()
    enc_copy.wait()
    gg_copy.wait()
    mo_copy.wait()


def shards(
    grid_feat, mesh_feat, edge_src, degree, offsets, w_kv, w_query, w_out, w_mesh, w_mesh_out, cotangent
):
    hbm = pl.BlockSpec(memory_space=pl.ANY)
    vmem = pl.BlockSpec(memory_space=pltpu.VMEM)
    smem = pl.BlockSpec(memory_space=pltpu.SMEM)

    def v(*shape, dtype=BF):
        return pltpu.VMEM(shape, dtype)

    dma = pltpu.SemaphoreType.DMA
    scratch = dict(
        nodes=v(M, K, dtype=I32), wide=v(WIDE, F), mf=v(2, M, F), cf=v(2, M, F), wkv_own=v(2, F, F), wkv_oth=v(2, F, F),
        wq=v(2, F, F), wo=v(2, F, F), wm=v(2, 3, F, F), wmo=v(2, F, F),
        qd=v(2, 2, M, F), qdt=v(2, 2, F, M), xs=v(G, F), ut=v(2, 16, M, F), zy=v(2, 16, M, F),
        srow=v(8, G, dtype=F32),
        sd=v(2, 8, K, 256, dtype=F32), sd_send=v(2, 8, K, 256), sd_recv=v(2, 8, K, 256), pb=v(2, 8, K, 256),
        att_own=v(M, F, dtype=F32), att_send=v(M, F), att_recv=v(M, F),
        enc_own=v(M, F, dtype=F32), enc_send=v(M, F), enc_recv=v(M, F), ef=v(2, M, F),
        mkv=v(2, M + 2 * R, F), mq=v(M, F),
        mo_own=v(M, F, dtype=F32), mo_send=v(M, F), mo_recv=v(M, F), mo_val=v(M, F),
        gedge=v(G, F), halo_send=v(2, RIM, F), halo_recv=v(2, RIM, F), ggs=v(G, F),
        gb=v(2, CHIPS, 128, 128), pre=v(CHIPS, 128, 128), rsb=v(CHIPS, 128, 128), fin=v(128, 128),
        lsem=dma((12,)), osem=dma((4,)), ssem=dma((N_REMOTE,)), rsem=dma((N_REMOTE,)),
        rs_s=dma((CHIPS,)), rs_r=dma((CHIPS,)), ag_s=dma((CHIPS,)), ag_r=dma((CHIPS,)),
        fw_s=dma((CHIPS,)), fw_r=dma((CHIPS,)), known=pltpu.SemaphoreType.REGULAR((6,)),
    )
    enc, mesh_out, grad_grid, grad_kv = pl.pallas_call(
        body,
        out_shape=(
            jax.ShapeDtypeStruct((M, F), BF),
            jax.ShapeDtypeStruct((M, F), BF),
            jax.ShapeDtypeStruct((G, F), BF),
            jax.ShapeDtypeStruct((2, 2 * F, F), BF),
        ),
        in_specs=[hbm, hbm, vmem, vmem, smem, hbm, hbm, hbm, hbm, hbm, hbm],
        out_specs=(hbm, hbm, hbm, hbm),
        scratch_shapes=list(scratch.values()),
        compiler_params=pltpu.CompilerParams(
            collective_id=0, has_side_effects=True, vmem_limit_bytes=58 * 2**20
        ),
        name="encoder",
    )(
        grid_feat, mesh_feat, edge_src.T, degree.reshape(1, M), offsets, w_kv, w_query, w_out, w_mesh,
        w_mesh_out, cotangent,
    )
    return enc, mesh_out, grad_grid, grad_kv.astype(F32)


def solution(mesh):
    in_specs = (
        P("space", "head"),
        P("space", "head"),
        P("space", None),
        P("space"),
        P(),
        P(None, None, "head"),
        P(None, "head"),
        P("head", None),
        P(None, None, "head"),
        P("head", None),
        P("space", "head"),
    )
    out_specs = (P("space", "head"), P("space", "head"), P("space", "head"), P(None, None, "head"))
    return jax.shard_map(shards, mesh=mesh, in_specs=in_specs, out_specs=out_specs, check_vma=False)
```

```python
import functools

import jax
import jax.numpy as jnp
from jax import lax
from jax.experimental import pallas as pl
from jax.experimental.pallas import tpu as pltpu
from jax.sharding import PartitionSpec as P

BF = jnp.bfloat16
F32 = jnp.float32
I32 = jnp.int32
MESH = pl.DeviceIdType.MESH

M = 128
K = 16
G = 2048
RIM = 128
WIDE = G + 2 * RIM
R = 32
W = 16
F = 512
HL = 8
SPACE = 64
CHIPS = SPACE // 2
CAP = 3.0
SCALE = 0.125

(
    E1M, E1C, HUP, HDOWN, E2, E3A, E3B, E4, E5, E6, KUP, KDOWN, E8, GUP, GDOWN, AGP,
    WY, WR, WF, PRE,
) = list(range(17)) + [18, 24, 32]
N_REMOTE = 36


def dot(a, b):
    return jnp.dot(a, b, preferred_element_type=F32)


def dot_t(a, b):
    return lax.dot_general(a, b, (((1,), (1,)), ((), ())), preferred_element_type=F32)


def dot_first(a, b):
    return lax.dot_general(a, b, (((0,), (0,)), ((), ())), preferred_element_type=F32)


def iota(shape, dim):
    return lax.broadcasted_iota(I32, shape, dim)


def body(
    grid_in, mesh_in, src, deg, off, wkv_in, wq_in, wo_in, wm_in, wmo_in, cot_in,
    enc_out, mesh_out, gg_out, gkv_out,
    nodes, wide, mf, cf, wkv_own, wkv_oth, wq, wo, wm, wmo, qd, qdt, xs, ut, zy, srow,
    sd, sd_send, sd_recv, pb, att_own, att_send, att_recv, enc_own, enc_send, enc_recv, ef, mkv, mq,
    mo_own, mo_send, mo_recv, mo_val, gedge, halo_send, halo_recv, ggs,
    gb, pre, rsb, fin,
    lsem, osem, ssem, rsem, rs_s, rs_r, ag_s, ag_r, fw_s, fw_r, known,
):
    s = lax.axis_index("space")
    g = lax.axis_index("head")
    o = 1 - g
    core = s % 2
    chip = s // 2
    sib = s + 1 - 2 * core
    up = (s + 1) % SPACE
    down = (s + SPACE - 1) % SPACE

    def flip(bit):
        return s + bit - 2 * bit * ((s // bit) % 2)

    across = flip(8)
    at_x, at_z = chip // 8, chip % 4

    def along(axis, d):
        return (s + 16 * d) % SPACE if axis == 0 else s - 2 * at_z + 2 * ((at_z + d) % 4)

    far = s - 1 + 2 * core
    far = (far + SPACE) % SPACE

    def remote(src_ref, dst_ref, n, dev):
        return pltpu.make_async_remote_copy(
            src_ref=src_ref, dst_ref=dst_ref, send_sem=ssem.at[n], recv_sem=rsem.at[n],
            device_id=dev, device_id_type=MESH,
        )

    partner = (s, o)
    mine = pl.ds(pl.multiple_of(g * F, F), F)
    other = pl.ds(pl.multiple_of(o * F, F), F)

    local = [
        (mesh_in, mf.at[0]),
        (cot_in, cf.at[0]),
        (wq_in.at[mine, :], wq.at[0]),
        (wo_in.at[:, mine], wo.at[0]),
        (wq_in.at[other, :], wq.at[1]),
        (wo_in.at[:, other], wo.at[1]),
        (wkv_in.at[:, mine, :], wkv_own),
        (grid_in, wide.at[pl.ds(RIM, G), :]),
        (wm_in.at[:, mine, :], wm.at[0]),
        (wm_in.at[:, other, :], wm.at[1]),
        (wmo_in.at[:, mine], wmo.at[0]),
        (wmo_in.at[:, other], wmo.at[1]),
    ]
    loads = [pltpu.make_async_copy(a, b, lsem.at[i]) for i, (a, b) in enumerate(local)]
    for c in loads:
        c.start()

    bits = [partner, (flip(2), g), (flip(4), g), (flip(8), g), (flip(16), g), (flip(32), g)]
    first = bits + [(across, o), (sib, g), (far, g), (flip(16) + flip(32) - s, g), (flip(2) + flip(4) - s, g)]
    barrier = pltpu.get_barrier_semaphore()
    for dev in first:
        pl.semaphore_signal(barrier, inc=1, device_id=dev, device_id_type=MESH)
    pl.semaphore_wait(barrier, len(first))

    def tell(b):
        pl.semaphore_signal(known.at[b], inc=1, device_id=bits[b], device_id_type=MESH)

    def hear(b):
        pl.semaphore_wait(known.at[b], 1)

    e1m = remote(mesh_in, mf.at[1], E1M, partner)
    e1c = remote(cot_in, cf.at[1], E1C, partner)
    hup = remote(grid_in.at[pl.ds(G - RIM, RIM), :], wide.at[pl.ds(0, RIM), :], HUP, (up, g))
    hdown = remote(grid_in.at[pl.ds(0, RIM), :], wide.at[pl.ds(RIM + G, RIM), :], HDOWN, (down, g))

    def piece(k, axis, q):
        return wkv_oth.at[k, pl.ds(pl.multiple_of(axis * 256 + q * 64, 64), 64), :]

    at = (at_x, at_z)
    wy, wring, wfwd, wback = [], [], [], []
    for axis in range(2):
        rows = pl.ds(pl.multiple_of(o * F + axis * 256 + at[axis] * 64, 64), 64)
        here = piece(core, axis, at[axis])
        wy.append(remote(wkv_in.at[core, rows, :], here, WY + axis, (across, o)))
        for d in range(4):
            q = (at[axis] + 4 - d) % 4
            if d:
                n = WR + 3 * axis + d - 1
                wring.append((
                    remote(here, here, n, (along(axis, d), g)),
                    remote(piece(core, axis, q), piece(core, axis, q), n, partner),
                ))
            n = WF + 4 * axis + d
            wfwd.append(remote(piece(core, axis, q), piece(core, axis, q), n, (sib, g)))
            wback.append(remote(piece(1 - core, axis, q), piece(1 - core, axis, q), n, (sib, g)))
    for c in wy:
        c.start()
    e1m.start()
    e1c.start()
    hup.start()
    hdown.start()
    tell(0)

    base = s * G - RIM
    source = src[...].astype(F32).T.astype(I32)
    nodes[...] = source
    rel = source - base
    rel = jnp.where((rel >= 0) & (rel < WIDE), rel, 4095)
    hi = (rel // 64).astype(F32).astype(BF)
    lo = (rel % 64).astype(F32).astype(BF)
    spread = jnp.where(iota((K, 256), 0) == (iota((K, 256), 1) & 15), 1.0, 0.0).astype(BF)
    flat = dot(hi, spread) * 64.0 + dot(lo, spread)
    flat = jnp.where((iota((M, 256), 0) & 15) == iota((M, 256), 1) // 16, flat, 0.0)
    for t in range(8):
        srow[0:1, t * 256 : (t + 1) * 256] = jnp.sum(
            flat[t * 16 : (t + 1) * 16], axis=0, keepdims=True
        )

    loads[7].wait()
    hup.wait_recv()
    hdown.wait_recv()

    def gather(t, carry):
        n = pl.multiple_of(t * 32, 32)
        part = (nodes[pl.ds(n, 32), :] - base).astype(F32)
        part = jnp.broadcast_to(part[:, None, :], (32, K, K)).reshape(512, K)
        pick = (iota((512, K), 0) & 15) == iota((512, K), 1)
        col = jnp.sum(jnp.where(pick, part, 0.0), axis=1, keepdims=True).astype(I32)
        hot = jnp.where(iota((512, WIDE), 1) == col, 1.0, 0.0).astype(BF)
        xs[pl.ds(pl.multiple_of(t * 512, 512), 512), :] = dot(hot, wide[...]).astype(BF)
        return carry


    lax.fori_loop(0, 2, gather, 0)
    for c in wy:
        c.wait_recv()
    for c, _ in wring:
        c.start()
    wfwd[0].start()
    wfwd[4].start()
    hear(0)
    tell(1)
    lax.fori_loop(2, 3, gather, 0)

    for n in (0, 1, 2, 3):
        loads[n].wait()
    qa = dot(mf[0], wq[0])
    da = dot_t(cf[0], wo[0])
    loads[4].wait()
    loads[5].wait()
    e1m.wait_recv()
    e1c.wait_recv()
    qa = qa + dot(mf[1], wq[1])
    da = da + dot_t(cf[1], wo[1])
    qd[0, 0] = qa.astype(BF)
    qd[0, 1] = da.astype(BF)
    e2 = remote(qd.at[0], qd.at[1], E2, partner)
    e2.start()

    lax.fori_loop(3, 4, gather, 0)
    hear(1)
    tell(2)

    def turn(side):
        for k in range(2):
            qdt[side, k] = qd[side, k].astype(F32).T.astype(BF)

    turn(0)

    def expand(side, weights):
        for k in range(2):
            for a in range(2):
                x4 = qd[side, k, :, a * 256 : (a + 1) * 256].astype(F32)
                head = iota((M, 256), 1) // 64
                lhs = jnp.concatenate(
                    [jnp.where(head == i, x4, 0.0).astype(BF) for i in range(4)], axis=0
                )
                out = dot_t(lhs, weights[k, :, a * 256 : (a + 1) * 256]).astype(BF)
                n = side * HL + a * 4
                ut[k, n : n + 4] = out.reshape(4, M, F)

    loads[6].wait()
    expand(0, wkv_own)

    hear(2)
    tell(3)

    def scores(side):
        def step(t, carry):
            xg = xs[pl.ds(pl.multiple_of(t * 256, 256), 256), :]
            lane = iota((K, 256), 1) & 15
            ug = ut[:, side * HL : side * HL + HL, pl.ds(pl.multiple_of(t * 16, 16), 16), :]
            full = dot_t(xg, ug.reshape(256, F)).reshape(16, K, 256)
            total = jnp.where(lane == 0, full[0], 0.0)
            for m in range(1, 16):
                total = total + jnp.where(lane == m, full[m], 0.0)
            sd[side, t] = total
            sd_send[side, t] = total.astype(BF)
            return carry

        lax.fori_loop(0, 8, step, 0, unroll=2)

    e3a = remote(sd_send.at[0], sd_recv.at[1], E3A, partner)
    e3b = remote(sd_send.at[1], sd_recv.at[0], E3B, partner)
    scores(0)
    e3a.start()
    for n, (_, c) in enumerate(wring):
        c.wait_recv()
        wfwd[n + 1 + n // 3].start()
    e2.wait_recv()
    turn(1)
    hear(3)
    tell(4)
    for c in wback:
        c.wait_recv()
    expand(1, wkv_oth)
    hear(4)
    tell(5)

    scores(1)
    e3b.start()
    hear(5)

    dg = deg[...].astype(F32)
    dg = jnp.where(iota((8, M), 1) // 16 == iota((8, M), 0), dg, 0.0).astype(BF)
    tile = jnp.where((iota((M, 128), 0) & 15) == (iota((M, 128), 1) & 15), 1.0, 0.0).astype(BF)
    dlane = dot(dg, tile)
    live = iota((8, K, 128), 1).astype(F32) < dlane[:, None, :]

    for side in (1, 0):
        (e3a if side else e3b).wait_recv()
        raw = (sd[side, :, :, :128] + sd_recv[side, :, :, :128].astype(F32)) * SCALE
        dp = sd[side, :, :, 128:] + sd_recv[side, :, :, 128:].astype(F32)
        th = jnp.tanh(raw * (1.0 / CAP))
        wgt = jnp.where(live, jnp.exp(CAP * th), 0.0)
        prob = wgt / jnp.sum(wgt, axis=1, keepdims=True)
        ds = prob * (dp - jnp.sum(prob * dp, axis=1, keepdims=True))
        dr = ds * (1.0 - th * th) * SCALE
        a = side * 128
        pb[:, :, a : a + 128] = dr.astype(BF)
        pb[:, :, 256 + a : 256 + a + 128] = prob.astype(BF)

    def sums(t, carry):
        xg = xs[pl.ds(pl.multiple_of(t * 256, 256), 256), :]
        same = (iota((512, 256), 0) & 15) == iota((512, 256), 1) // 16
        sel = jnp.where(iota((K, 256), 0) == (iota((K, 256), 1) & 15), 1.0, 0.0).astype(BF)
        pt = jnp.where(same, dot_first(pb[t], sel), 0.0).astype(BF)
        out = dot(pt, xg).astype(BF)
        zy[:, :, pl.ds(pl.multiple_of(t * 16, 16), 16), :] = out.reshape(2, 16, 16, F)
        return carry

    lax.fori_loop(0, 8, sums, 0, unroll=2)

    def diagonal(x):
        x = x.reshape(4, M, 256)
        head = iota((M, 256), 1) // 64
        out = jnp.zeros((M, 256), F32)
        for i in range(4):
            out = out + jnp.where(head == i, x[i], 0.0)
        return out

    def weight_terms(n, carry):
        k = (1 - core) + n * (2 * core - 1)
        for side in range(2):
            for p in range(4):
                x = qdt[side, k, p * 128 : (p + 1) * 128, :].astype(F32)
                first = iota((128, M), 0) < 64
                lhs = jnp.concatenate(
                    [jnp.where(first, x, 0.0).astype(BF), jnp.where(first, 0.0, x).astype(BF)], axis=1
                )
                h = side * HL + 2 * p
                rhs = zy[k, h : h + 2].reshape(2 * M, F)
                out = dot(lhs, rhs).astype(BF)
                for f in range(4):
                    place_at = (16 * side + 4 * p + f + CHIPS - chip) % CHIPS
                    gb[k, place_at] = out[:, f * 128 : (f + 1) * 128]
        return carry

    weight_terms(0, 0)
    presum = [
        remote(gb.at[1 - core, pl.ds(8 * n, 8)], pre.at[pl.ds(8 * n, 8)], PRE + n, (sib, g))
        for n in range(4)
    ]
    for c in presum:
        c.start()
    for a in range(2):
        z4 = zy[1, HL + a * 4 : HL + a * 4 + 4].reshape(4 * M, F)
        att_send[:, a * 256 : (a + 1) * 256] = diagonal(
            dot(z4, wkv_oth[1, :, a * 256 : (a + 1) * 256])
        ).astype(BF)
    e4 = remote(att_send, att_recv, E4, partner)
    e4.start()
    weight_terms(1, 0)
    for a in range(2):
        z4 = zy[1, a * 4 : a * 4 + 4].reshape(4 * M, F)
        att_own[:, a * 256 : (a + 1) * 256] = diagonal(
            dot(z4, wkv_own[1, :, a * 256 : (a + 1) * 256])
        )


    def scatter_copy(i):
        return pltpu.make_async_remote_copy(
            src_ref=gb.at[core, i], dst_ref=rsb.at[i], send_sem=rs_s.at[i], recv_sem=rs_r.at[i],
            device_id=(((chip + i) % CHIPS) * 2 + core, g), device_id_type=MESH,
        )

    def reduce_send(i, carry):
        gb[core, i] = (gb[core, i].astype(F32) + pre[i].astype(F32)).astype(BF)
        scatter_copy(i).start()
        return carry

    for n in range(2):
        presum[n].wait_recv()
        lax.fori_loop(max(1, 8 * n), 8 * n + 8, reduce_send, 0)

    e4.wait_recv()
    att = (att_own[...] + att_recv[...].astype(F32)).astype(BF)
    enc_send[...] = dot(att, wo[1]).astype(BF)
    e5 = remote(enc_send, enc_recv, E5, partner)
    e5.start()
    enc_own[...] = dot(att, wo[0])

    for n in range(2, 4):
        presum[n].wait_recv()
        lax.fori_loop(8 * n, 8 * n + 8, reduce_send, 0)

    def edge_grads(t, carry):
        rows = pl.ds(pl.multiple_of(t * 16, 16), 16)
        match = (iota((16, K, 512), 2) & 15) == iota((16, K, 512), 0)
        p = jnp.broadcast_to(pb[t].astype(F32)[None], (16, K, 512))
        p = jnp.where(match, p, 0.0).astype(BF).reshape(256, 512)
        total = dot(p, ut[:, :, rows, :].reshape(512, F))
        gedge[pl.ds(pl.multiple_of(t * 256, 256), 256), :] = total.astype(BF)
        return carry

    lax.fori_loop(0, 8, edge_grads, 0, unroll=2)

    def rows_of(first, count):
        hot = jnp.where(
            (iota((count, G), 0) + first).astype(F32) == srow[0:1, :], 1.0, 0.0
        ).astype(BF)
        return dot(hot, gedge[...])

    halo_send[0] = rows_of(0, RIM).astype(BF)
    halo_send[1] = rows_of(RIM + G, RIM).astype(BF)
    gdown = remote(halo_send.at[0], halo_recv.at[1], GDOWN, (down, g))
    gup = remote(halo_send.at[1], halo_recv.at[0], GUP, (up, g))
    gdown.start()
    gup.start()

    e5.wait_recv()
    enc = (mf[0].astype(F32) + enc_own[...] + enc_recv[...].astype(F32)).astype(BF)
    ef[0] = enc
    e6 = remote(ef.at[0], ef.at[1], E6, partner)
    e6.start()
    enc_copy = pltpu.make_async_copy(ef.at[0], enc_out, osem.at[0])
    enc_copy.start()

    def interior(t, carry):
        n = pl.multiple_of(t * 512, 512)
        ggs[pl.ds(n, 512), :] = rows_of(n + RIM, 512).astype(BF)
        return carry

    lax.fori_loop(0, 3, interior, 0)

    loads[8].wait()
    loads[9].wait()
    e6.wait_recv()
    for k in range(2):
        mkv[k, R : R + M, :] = (dot(ef[0], wm[0, 1 + k]) + dot(ef[1], wm[1, 1 + k])).astype(BF)
    kup = remote(mkv.at[:, pl.ds(M, R), :], mkv.at[:, pl.ds(0, R), :], KUP, (up, g))
    kdown = remote(mkv.at[:, pl.ds(R, R), :], mkv.at[:, pl.ds(R + M, R), :], KDOWN, (down, g))
    kup.start()
    kdown.start()
    mq[...] = (dot(ef[0], wm[0, 0]) + dot(ef[1], wm[1, 0])).astype(BF)

    lax.fori_loop(3, 4, interior, 0)

    block_sum = gb[core, 0].astype(F32) + pre[0].astype(F32)

    def reduce_recv(i, total):
        scatter_copy(i).wait_recv()
        return total + rsb[i].astype(F32)

    block_sum = lax.fori_loop(1, CHIPS, reduce_recv, block_sum)
    fin[...] = block_sum.T.astype(BF)

    late = chip // 16
    group = g + late * (1 - 2 * g)

    def place(k, half, c):
        row = pl.multiple_of((half * 4 + c % 4) * 128, 128)
        col = pl.multiple_of(((c % 16) // 4) * 128, 128)
        return gkv_out.at[k, pl.ds(row, 128), pl.ds(col, 128)]

    def spread_copy(i):
        return pltpu.make_async_remote_copy(
            src_ref=fin, dst_ref=place(core, g, chip), send_sem=ag_s.at[i], recv_sem=ag_r.at[i],
            device_id=(((chip + i) % CHIPS) * 2 + core, group), device_id_type=MESH,
        )

    def arrived(i, k):
        c = (chip + CHIPS - i) % CHIPS
        return place(k, g + (c // 16) * (1 - 2 * g), c)

    def spread_recv(i):
        return pltpu.make_async_remote_copy(
            src_ref=fin, dst_ref=arrived(i, core), send_sem=ag_s.at[i], recv_sem=ag_r.at[i],
            device_id=partner, device_id_type=MESH,
        )

    def pass_copy(i, k):
        return pltpu.make_async_remote_copy(
            src_ref=arrived(i, k), dst_ref=arrived(i, k), send_sem=fw_s.at[i], recv_sem=fw_r.at[i],
            device_id=(sib, g), device_id_type=MESH,
        )

    own_copy = pltpu.make_async_copy(fin, place(core, g, chip), osem.at[1])
    own_send = remote(fin, place(core, g, chip), AGP, partner)

    @pl.when(late == 0)
    def _():
        own_copy.start()

    @pl.when(late == 1)
    def _():
        own_send.start()

    def spread_send(i, carry):
        spread_copy(i).start()
        return carry

    lax.fori_loop(1, CHIPS, spread_send, 0)

    where_n = iota((M, 256), 1) - R
    delta = where_n - iota((M, 256), 0)
    allowed = delta == off[0]
    for j in range(1, W):
        allowed = allowed | (delta == off[j])
    where_g = where_n + s * M
    allowed = allowed & (where_g >= 0) & (where_g < M * SPACE)
    allow = jnp.where(allowed[:, : M + 2 * R], 1.0, 0.0)
    allow4 = jnp.concatenate([allow] * 4, axis=0)
    kup.wait_recv()
    kdown.wait_recv()
    matts = []
    for a in range(2):
        cols = slice(a * 256, (a + 1) * 256)
        x4 = mq[:, cols].astype(F32)
        head = iota((M, 256), 1) // 64
        lhs = jnp.concatenate([jnp.where(head == i, x4, 0.0).astype(BF) for i in range(4)], axis=0)
        raw = dot_t(lhs, mkv[0, :, cols]) * SCALE
        wgt = jnp.exp(CAP * jnp.tanh(raw * (1.0 / CAP))) * allow4
        prob = (wgt / jnp.sum(wgt, axis=1, keepdims=True)).astype(BF)
        matts.append(diagonal(dot(prob, mkv[1, :, cols])).astype(BF))
    matt = jnp.concatenate(matts, axis=1)
    loads[10].wait()
    loads[11].wait()
    mo_send[...] = dot(matt, wmo[1]).astype(BF)
    e8 = remote(mo_send, mo_recv, E8, partner)
    e8.start()
    mo_own[...] = dot(matt, wmo[0])

    gdown.wait_recv()
    gup.wait_recv()
    ggs[0:RIM, :] = (ggs[0:RIM, :].astype(F32) + halo_recv[0].astype(F32)).astype(BF)
    ggs[G - RIM : G, :] = (ggs[G - RIM : G, :].astype(F32) + halo_recv[1].astype(F32)).astype(BF)
    gg_copy = pltpu.make_async_copy(ggs, gg_out, osem.at[2])
    gg_copy.start()

    def sent(i, carry):
        scatter_copy(i).wait_send()
        return carry

    lax.fori_loop(1, CHIPS, sent, 0)
    singles = [e1m, e1c, hup, hdown, e2, e3a, e3b, e4, e5, e6, kup, kdown, gdown, gup]
    for c in singles + wy + [c for c, _ in wring] + wfwd + presum:
        c.wait_send()
    e8.wait()
    mo_val[...] = (ef[0].astype(F32) + mo_own[...] + mo_recv[...].astype(F32)).astype(BF)
    mo_copy = pltpu.make_async_copy(mo_val, mesh_out, osem.at[3])
    mo_copy.start()

    @pl.when(late == 0)
    def _():
        own_copy.wait()

    @pl.when(late == 1)
    def _():
        remote(fin, arrived(0, core), AGP, partner).wait()

    pass_copy(0, core).start()

    def pass_on(i, carry):
        spread_copy(i).wait_send()
        spread_recv(i).wait_recv()
        pass_copy(i, core).start()
        return carry

    lax.fori_loop(1, CHIPS, pass_on, 0)

    def finish(i, carry):
        pass_copy(i, 1 - core).wait_recv()
        pass_copy(i, core).wait_send()
        return carry

    lax.fori_loop(0, CHIPS, finish, 0)

    enc_copy.wait()
    gg_copy.wait()
    mo_copy.wait()


def write_results(enc, mesh_o, gg, gkv, enc_out, mesh_out, gg_out, gkv_out, e, m, r, low, wide, s_in, s_out, k_in, k_out):
    plain = ((enc, e, enc_out), (mesh_o, m, mesh_out), (gg, r, gg_out))
    parts = [(n // 4, pl.ds(n % 4 * 256, 256)) for n in range(8)]
    loads = [pltpu.make_async_copy(gkv.at[k, rows], low.at[k, rows], k_in.at[n]) for n, (k, rows) in enumerate(parts)]
    others = [pltpu.make_async_copy(a, b, s_in.at[n]) for n, (a, b, _) in enumerate(plain)]
    for c in loads + others:
        c.start()
    stores = []
    for n, (k, rows) in enumerate(parts):
        loads[n].wait()
        wide[k, rows] = low[k, rows].astype(F32)
        stores.append(pltpu.make_async_copy(wide.at[k, rows], gkv_out.at[k, rows], k_out.at[n]))
        stores[-1].start()
    for n, (_, b, c) in enumerate(plain):
        others[n].wait()
        stores.append(pltpu.make_async_copy(b, c, s_out.at[n]))
        stores[-1].start()
    for c in stores:
        c.wait()


def shards(
    grid_feat, mesh_feat, edge_src, degree, offsets, w_kv, w_query, w_out, w_mesh, w_mesh_out, cotangent
):
    hbm = pl.BlockSpec(memory_space=pl.ANY)
    vmem = pl.BlockSpec(memory_space=pltpu.VMEM)
    smem = pl.BlockSpec(memory_space=pltpu.SMEM)

    def v(*shape, dtype=BF):
        return pltpu.VMEM(shape, dtype)

    dma = pltpu.SemaphoreType.DMA
    scratch = dict(
        nodes=v(M, K, dtype=I32), wide=v(WIDE, F), mf=v(2, M, F), cf=v(2, M, F), wkv_own=v(2, F, F), wkv_oth=v(2, F, F),
        wq=v(2, F, F), wo=v(2, F, F), wm=v(2, 3, F, F), wmo=v(2, F, F),
        qd=v(2, 2, M, F), qdt=v(2, 2, F, M), xs=v(G, F), ut=v(2, 16, M, F), zy=v(2, 16, M, F),
        srow=v(8, G, dtype=F32),
        sd=v(2, 8, K, 256, dtype=F32), sd_send=v(2, 8, K, 256), sd_recv=v(2, 8, K, 256), pb=v(8, K, 512),
        att_own=v(M, F, dtype=F32), att_send=v(M, F), att_recv=v(M, F),
        enc_own=v(M, F, dtype=F32), enc_send=v(M, F), enc_recv=v(M, F), ef=v(2, M, F),
        mkv=v(2, M + 2 * R, F), mq=v(M, F),
        mo_own=v(M, F, dtype=F32), mo_send=v(M, F), mo_recv=v(M, F), mo_val=v(M, F),
        gedge=v(G, F), halo_send=v(2, RIM, F), halo_recv=v(2, RIM, F), ggs=v(G, F),
        gb=v(2, CHIPS, 128, 128), pre=v(CHIPS, 128, 128), rsb=v(CHIPS, 128, 128), fin=v(128, 128),
        lsem=dma((12,)), osem=dma((4,)), ssem=dma((N_REMOTE,)), rsem=dma((N_REMOTE,)),
        rs_s=dma((CHIPS,)), rs_r=dma((CHIPS,)), ag_s=dma((CHIPS,)), ag_r=dma((CHIPS,)),
        fw_s=dma((CHIPS,)), fw_r=dma((CHIPS,)), known=pltpu.SemaphoreType.REGULAR((6,)),
    )
    enc, mesh_out, grad_grid, grad_kv = pl.pallas_call(
        body,
        out_shape=(
            jax.ShapeDtypeStruct((M, F), BF),
            jax.ShapeDtypeStruct((M, F), BF),
            jax.ShapeDtypeStruct((G, F), BF),
            jax.ShapeDtypeStruct((2, 2 * F, F), BF),
        ),
        in_specs=[hbm, hbm, vmem, vmem, smem, hbm, hbm, hbm, hbm, hbm, hbm],
        out_specs=(hbm, hbm, hbm, hbm),
        scratch_shapes=list(scratch.values()),
        compiler_params=pltpu.CompilerParams(
            collective_id=0, has_side_effects=True, vmem_limit_bytes=58 * 2**20
        ),
        name="encoder",
    )(
        grid_feat, mesh_feat, edge_src.T, degree.reshape(1, M), offsets, w_kv, w_query, w_out, w_mesh,
        w_mesh_out, cotangent,
    )
    dma = pltpu.SemaphoreType.DMA
    return pl.pallas_call(
        write_results,
        out_shape=(
            jax.ShapeDtypeStruct((M, F), BF),
            jax.ShapeDtypeStruct((M, F), BF),
            jax.ShapeDtypeStruct((G, F), BF),
            jax.ShapeDtypeStruct((2, 2 * F, F), F32),
        ),
        in_specs=[hbm] * 4,
        out_specs=(hbm,) * 4,
        scratch_shapes=[
            v(M, F), v(M, F), v(G, F), v(2, 2 * F, F), v(2, 2 * F, F, dtype=F32),
            dma((3,)), dma((3,)), dma((8,)), dma((8,)),
        ],
        compiler_params=pltpu.CompilerParams(vmem_limit_bytes=24 * 2**20),
        name="results",
    )(enc, mesh_out, grad_grid, grad_kv)


def solution(mesh):
    in_specs = (
        P("space", "head"),
        P("space", "head"),
        P("space", None),
        P("space"),
        P(),
        P(None, None, "head"),
        P(None, "head"),
        P("head", None),
        P(None, None, "head"),
        P("head", None),
        P("space", "head"),
    )
    out_specs = (P("space", "head"), P("space", "head"), P("space", "head"), P(None, None, "head"))
    return jax.shard_map(shards, mesh=mesh, in_specs=in_specs, out_specs=out_specs, check_vma=False)
```

```python
import functools

import jax
import jax.numpy as jnp
from jax import lax
from jax.experimental import pallas as pl
from jax.experimental.pallas import tpu as pltpu
from jax.sharding import PartitionSpec as P

BF = jnp.bfloat16
F32 = jnp.float32
I32 = jnp.int32
MESH = pl.DeviceIdType.MESH

M = 128
K = 16
G = 2048
RIM = 128
WIDE = G + 2 * RIM
R = 32
W = 16
F = 512
HL = 8
SPACE = 64
CHIPS = SPACE // 2
CAP = 3.0
SCALE = 0.125

(
    E1M, E1C, HUP, HDOWN, E2, E3A, E3B, E4, E5, E6, KUP, KDOWN, E8, GUP, GDOWN, SWAP,
    WY, WR, WF, PRE,
) = list(range(17)) + [18, 24, 32]
N_REMOTE = 36


def dot(a, b):
    return jnp.dot(a, b, preferred_element_type=F32)


def dot_t(a, b):
    return lax.dot_general(a, b, (((1,), (1,)), ((), ())), preferred_element_type=F32)


def dot_first(a, b):
    return lax.dot_general(a, b, (((0,), (0,)), ((), ())), preferred_element_type=F32)


def iota(shape, dim):
    return lax.broadcasted_iota(I32, shape, dim)


def body(
    grid_in, mesh_in, src, deg, off, wkv_in, wq_in, wo_in, wm_in, wmo_in, cot_in,
    enc_out, mesh_out, gg_out, gkv_out,
    nodes, wide, mf, cf, wkv_own, wkv_oth, wq, wo, wm, wmo, qd, qdt, xs, ut, zy, srow,
    sd, sd_send, sd_recv, pb, att_own, att_send, att_recv, enc_own, enc_send, enc_recv, ef, mkv, mq,
    mo_own, mo_send, mo_recv, mo_val, gedge, halo_send, halo_recv, ggs,
    gb, pre, rsb, fin,
    lsem, osem, ssem, rsem, rs_s, rs_r, ag_s, ag_r, fw_s, fw_r, known,
):
    s = lax.axis_index("space")
    g = lax.axis_index("head")
    o = 1 - g
    core = s % 2
    chip = s // 2
    sib = s + 1 - 2 * core
    up = (s + 1) % SPACE
    down = (s + SPACE - 1) % SPACE

    def flip(bit):
        return s + bit - 2 * bit * ((s // bit) % 2)

    across = flip(8)
    at_x, at_z = chip // 8, chip % 4

    def along(axis, d):
        return (s + 16 * d) % SPACE if axis == 0 else s - 2 * at_z + 2 * ((at_z + d) % 4)

    far = s - 1 + 2 * core
    far = (far + SPACE) % SPACE

    def remote(src_ref, dst_ref, n, dev):
        return pltpu.make_async_remote_copy(
            src_ref=src_ref, dst_ref=dst_ref, send_sem=ssem.at[n], recv_sem=rsem.at[n],
            device_id=dev, device_id_type=MESH,
        )

    partner = (s, o)
    mine = pl.ds(pl.multiple_of(g * F, F), F)
    other = pl.ds(pl.multiple_of(o * F, F), F)

    local = [
        (mesh_in, mf.at[0]),
        (cot_in, cf.at[0]),
        (wq_in.at[mine, :], wq.at[0]),
        (wo_in.at[:, mine], wo.at[0]),
        (wq_in.at[other, :], wq.at[1]),
        (wo_in.at[:, other], wo.at[1]),
        (wkv_in.at[:, mine, :], wkv_own),
        (grid_in, wide.at[pl.ds(RIM, G), :]),
        (wm_in.at[:, mine, :], wm.at[0]),
        (wm_in.at[:, other, :], wm.at[1]),
        (wmo_in.at[:, mine], wmo.at[0]),
        (wmo_in.at[:, other], wmo.at[1]),
    ]
    loads = [pltpu.make_async_copy(a, b, lsem.at[i]) for i, (a, b) in enumerate(local)]
    for c in loads:
        c.start()

    bits = [partner, (flip(2), g), (flip(4), g), (flip(8), g), (flip(16), g), (flip(32), g)]
    first = bits + [(across, o), (sib, g), (far, g), (flip(16) + flip(32) - s, g), (flip(2) + flip(4) - s, g)]
    barrier = pltpu.get_barrier_semaphore()
    for dev in first:
        pl.semaphore_signal(barrier, inc=1, device_id=dev, device_id_type=MESH)
    pl.semaphore_wait(barrier, len(first))

    def tell(b):
        pl.semaphore_signal(known.at[b], inc=1, device_id=bits[b], device_id_type=MESH)

    def hear(b):
        pl.semaphore_wait(known.at[b], 1)

    e1m = remote(mesh_in, mf.at[1], E1M, partner)
    e1c = remote(cot_in, cf.at[1], E1C, partner)
    hup = remote(grid_in.at[pl.ds(G - RIM, RIM), :], wide.at[pl.ds(0, RIM), :], HUP, (up, g))
    hdown = remote(grid_in.at[pl.ds(0, RIM), :], wide.at[pl.ds(RIM + G, RIM), :], HDOWN, (down, g))

    def piece(k, axis, q):
        return wkv_oth.at[k, pl.ds(pl.multiple_of(axis * 256 + q * 64, 64), 64), :]

    at = (at_x, at_z)
    wy, wring, wfwd, wback = [], [], [], []
    for axis in range(2):
        rows = pl.ds(pl.multiple_of(o * F + axis * 256 + at[axis] * 64, 64), 64)
        here = piece(core, axis, at[axis])
        wy.append(remote(wkv_in.at[core, rows, :], here, WY + axis, (across, o)))
        for d in range(4):
            q = (at[axis] + 4 - d) % 4
            if d:
                n = WR + 3 * axis + d - 1
                wring.append((
                    remote(here, here, n, (along(axis, d), g)),
                    remote(piece(core, axis, q), piece(core, axis, q), n, partner),
                ))
            n = WF + 4 * axis + d
            wfwd.append(remote(piece(core, axis, q), piece(core, axis, q), n, (sib, g)))
            wback.append(remote(piece(1 - core, axis, q), piece(1 - core, axis, q), n, (sib, g)))
    for c in wy:
        c.start()
    hup.start()
    hdown.start()
    e1m.start()
    e1c.start()
    tell(0)

    base = s * G - RIM
    source = src[...].astype(F32).T.astype(I32)
    nodes[...] = source
    rel = source - base
    rel = jnp.where((rel >= 0) & (rel < WIDE), rel, 4095)
    hi = (rel // 64).astype(F32).astype(BF)
    lo = (rel % 64).astype(F32).astype(BF)
    spread = jnp.where(iota((K, 256), 0) == (iota((K, 256), 1) & 15), 1.0, 0.0).astype(BF)
    flat = dot(hi, spread) * 64.0 + dot(lo, spread)
    flat = jnp.where((iota((M, 256), 0) & 15) == iota((M, 256), 1) // 16, flat, 0.0)
    for t in range(8):
        srow[0:1, t * 256 : (t + 1) * 256] = jnp.sum(
            flat[t * 16 : (t + 1) * 16], axis=0, keepdims=True
        )

    for c in wy:
        c.wait_recv()
    for c, _ in wring:
        c.start()
    wfwd[0].start()
    wfwd[4].start()

    loads[7].wait()
    hup.wait_recv()
    hdown.wait_recv()

    def gather(t, carry):
        n = pl.multiple_of(t * 32, 32)
        part = (nodes[pl.ds(n, 32), :] - base).astype(F32)
        part = jnp.broadcast_to(part[:, None, :], (32, K, K)).reshape(512, K)
        pick = (iota((512, K), 0) & 15) == iota((512, K), 1)
        col = jnp.sum(jnp.where(pick, part, 0.0), axis=1, keepdims=True).astype(I32)
        hot = jnp.where(iota((512, WIDE), 1) == col, 1.0, 0.0).astype(BF)
        xs[pl.ds(pl.multiple_of(t * 512, 512), 512), :] = dot(hot, wide[...]).astype(BF)
        return carry

    lax.fori_loop(0, 3, gather, 0)
    hear(0)
    tell(1)

    for n in (0, 1, 2, 3):
        loads[n].wait()
    qa = dot(mf[0], wq[0])
    da = dot_t(cf[0], wo[0])
    loads[4].wait()
    loads[5].wait()
    e1m.wait_recv()
    e1c.wait_recv()
    qa = qa + dot(mf[1], wq[1])
    da = da + dot_t(cf[1], wo[1])
    qd[0, 0] = qa.astype(BF)
    qd[0, 1] = da.astype(BF)
    e2 = remote(qd.at[0], qd.at[1], E2, partner)
    e2.start()
    for n, (_, c) in enumerate(wring):
        c.wait_recv()
        wfwd[n + 1 + n // 3].start()

    lax.fori_loop(3, 4, gather, 0)
    hear(1)
    tell(2)

    def turn(side):
        for k in range(2):
            qdt[side, k] = qd[side, k].astype(F32).T.astype(BF)

    turn(0)

    def expand(side, weights):
        for k in range(2):
            for a in range(2):
                x4 = qd[side, k, :, a * 256 : (a + 1) * 256].astype(F32)
                head = iota((M, 256), 1) // 64
                lhs = jnp.concatenate(
                    [jnp.where(head == i, x4, 0.0).astype(BF) for i in range(4)], axis=0
                )
                out = dot_t(lhs, weights[k, :, a * 256 : (a + 1) * 256]).astype(BF)
                n = side * HL + a * 4
                ut[k, n : n + 4] = out.reshape(4, M, F)

    loads[6].wait()
    expand(0, wkv_own)

    hear(2)
    tell(3)

    def scores(side):
        def step(t, carry):
            xg = xs[pl.ds(pl.multiple_of(t * 256, 256), 256), :]
            lane = iota((K, 256), 1) & 15
            ug = ut[:, side * HL : side * HL + HL, pl.ds(pl.multiple_of(t * 16, 16), 16), :]
            full = dot_t(xg, ug.reshape(256, F)).reshape(16, K, 256)
            total = jnp.where(lane == 0, full[0], 0.0)
            for m in range(1, 16):
                total = total + jnp.where(lane == m, full[m], 0.0)
            sd[side, t] = total
            sd_send[side, t] = total.astype(BF)
            return carry

        lax.fori_loop(0, 8, step, 0, unroll=2)

    e3a = remote(sd_send.at[0], sd_recv.at[1], E3A, partner)
    e3b = remote(sd_send.at[1], sd_recv.at[0], E3B, partner)
    scores(0)
    e3a.start()
    e2.wait_recv()
    turn(1)
    hear(3)
    tell(4)
    for c in wback:
        c.wait_recv()
    expand(1, wkv_oth)
    hear(4)
    tell(5)

    scores(1)
    e3b.start()
    hear(5)

    dg = deg[...].astype(F32)
    dg = jnp.where(iota((8, M), 1) // 16 == iota((8, M), 0), dg, 0.0).astype(BF)
    tile = jnp.where((iota((M, 128), 0) & 15) == (iota((M, 128), 1) & 15), 1.0, 0.0).astype(BF)
    dlane = dot(dg, tile)
    live = iota((8, K, 128), 1).astype(F32) < dlane[:, None, :]

    for side in (1, 0):
        (e3a if side else e3b).wait_recv()
        raw = (sd[side, :, :, :128] + sd_recv[side, :, :, :128].astype(F32)) * SCALE
        dp = sd[side, :, :, 128:] + sd_recv[side, :, :, 128:].astype(F32)
        th = jnp.tanh(raw * (1.0 / CAP))
        wgt = jnp.where(live, jnp.exp(CAP * th), 0.0)
        prob = wgt / jnp.sum(wgt, axis=1, keepdims=True)
        ds = prob * (dp - jnp.sum(prob * dp, axis=1, keepdims=True))
        dr = ds * (1.0 - th * th) * SCALE
        a = side * 128
        pb[:, :, a : a + 128] = dr.astype(BF)
        pb[:, :, 256 + a : 256 + a + 128] = prob.astype(BF)

    def sums(t, carry):
        xg = xs[pl.ds(pl.multiple_of(t * 256, 256), 256), :]
        same = (iota((512, 256), 0) & 15) == iota((512, 256), 1) // 16
        sel = jnp.where(iota((K, 256), 0) == (iota((K, 256), 1) & 15), 1.0, 0.0).astype(BF)
        pt = jnp.where(same, dot_first(pb[t], sel), 0.0).astype(BF)
        out = dot(pt, xg).astype(BF)
        zy[:, :, pl.ds(pl.multiple_of(t * 16, 16), 16), :] = out.reshape(2, 16, 16, F)
        return carry

    lax.fori_loop(0, 8, sums, 0, unroll=2)

    def diagonal(x):
        x = x.reshape(4, M, 256)
        head = iota((M, 256), 1) // 64
        out = jnp.zeros((M, 256), F32)
        for i in range(4):
            out = out + jnp.where(head == i, x[i], 0.0)
        return out

    def weight_terms(n, carry):
        k = (1 - core) + n * (2 * core - 1)
        for side in range(2):
            for p in range(4):
                x = qdt[side, k, p * 128 : (p + 1) * 128, :].astype(F32)
                first = iota((128, M), 0) < 64
                lhs = jnp.concatenate(
                    [jnp.where(first, x, 0.0).astype(BF), jnp.where(first, 0.0, x).astype(BF)], axis=1
                )
                h = side * HL + 2 * p
                rhs = zy[k, h : h + 2].reshape(2 * M, F)
                out = dot(lhs, rhs).astype(BF)
                for f in range(4):
                    place_at = (16 * side + 4 * p + f + CHIPS - chip) % CHIPS
                    gb[k, place_at] = out[:, f * 128 : (f + 1) * 128]
        return carry

    weight_terms(0, 0)
    presum = [
        remote(gb.at[1 - core, pl.ds(8 * n, 8)], pre.at[pl.ds(8 * n, 8)], PRE + n, (sib, g))
        for n in range(4)
    ]
    for c in presum:
        c.start()
    for a in range(2):
        z4 = zy[1, HL + a * 4 : HL + a * 4 + 4].reshape(4 * M, F)
        att_send[:, a * 256 : (a + 1) * 256] = diagonal(
            dot(z4, wkv_oth[1, :, a * 256 : (a + 1) * 256])
        ).astype(BF)
    e4 = remote(att_send, att_recv, E4, partner)
    e4.start()
    weight_terms(1, 0)
    for a in range(2):
        z4 = zy[1, a * 4 : a * 4 + 4].reshape(4 * M, F)
        att_own[:, a * 256 : (a + 1) * 256] = diagonal(
            dot(z4, wkv_own[1, :, a * 256 : (a + 1) * 256])
        )


    def scatter_copy(i):
        return pltpu.make_async_remote_copy(
            src_ref=gb.at[core, i], dst_ref=rsb.at[i], send_sem=rs_s.at[i], recv_sem=rs_r.at[i],
            device_id=(((chip + i) % CHIPS) * 2 + core, g), device_id_type=MESH,
        )

    def reduce_send(i, carry):
        gb[core, i] = (gb[core, i].astype(F32) + pre[i].astype(F32)).astype(BF)
        scatter_copy(i).start()
        return carry

    for n in range(2):
        presum[n].wait_recv()
        lax.fori_loop(max(1, 8 * n), 8 * n + 8, reduce_send, 0)

    e4.wait_recv()
    att = (att_own[...] + att_recv[...].astype(F32)).astype(BF)
    enc_send[...] = dot(att, wo[1]).astype(BF)
    e5 = remote(enc_send, enc_recv, E5, partner)
    e5.start()
    enc_own[...] = dot(att, wo[0])

    for n in range(2, 4):
        presum[n].wait_recv()
        lax.fori_loop(8 * n, 8 * n + 8, reduce_send, 0)

    def edge_grads(t, carry):
        rows = pl.ds(pl.multiple_of(t * 16, 16), 16)
        match = (iota((16, K, 512), 2) & 15) == iota((16, K, 512), 0)
        p = jnp.broadcast_to(pb[t].astype(F32)[None], (16, K, 512))
        p = jnp.where(match, p, 0.0).astype(BF).reshape(256, 512)
        total = dot(p, ut[:, :, rows, :].reshape(512, F))
        gedge[pl.ds(pl.multiple_of(t * 256, 256), 256), :] = total.astype(BF)
        return carry

    lax.fori_loop(0, 8, edge_grads, 0, unroll=2)

    def rows_of(first, count):
        hot = jnp.where(
            (iota((count, G), 0) + first).astype(F32) == srow[0:1, :], 1.0, 0.0
        ).astype(BF)
        return dot(hot, gedge[...])

    halo_send[0] = rows_of(0, RIM).astype(BF)
    halo_send[1] = rows_of(RIM + G, RIM).astype(BF)
    gdown = remote(halo_send.at[0], halo_recv.at[1], GDOWN, (down, g))
    gup = remote(halo_send.at[1], halo_recv.at[0], GUP, (up, g))
    gdown.start()
    gup.start()

    e5.wait_recv()
    enc = (mf[0].astype(F32) + enc_own[...] + enc_recv[...].astype(F32)).astype(BF)
    ef[0] = enc
    e6 = remote(ef.at[0], ef.at[1], E6, partner)
    e6.start()
    enc_copy = pltpu.make_async_copy(ef.at[0], enc_out, osem.at[0])
    enc_copy.start()

    def interior(t, carry):
        n = pl.multiple_of(t * 512, 512)
        ggs[pl.ds(n, 512), :] = rows_of(n + RIM, 512).astype(BF)
        return carry

    lax.fori_loop(0, 4, interior, 0)

    block_sum = gb[core, 0].astype(F32) + pre[0].astype(F32)

    def reduce_recv(i, total):
        scatter_copy(i).wait_recv()
        return total + rsb[i].astype(F32)

    block_sum = lax.fori_loop(1, CHIPS, reduce_recv, block_sum)
    fin[0] = block_sum.T.astype(BF)

    late = chip // 16
    swap = remote(fin.at[0], fin.at[1], SWAP, partner)

    def place(k, c):
        half = g + (c // 16) * (1 - 2 * g)
        row = pl.multiple_of((half * 4 + c % 4) * 128, 128)
        col = pl.multiple_of(((c % 16) // 4) * 128, 128)
        return gkv_out.at[k, pl.ds(row, 128), pl.ds(col, 128)]

    def spread_copy(i):
        return pltpu.make_async_remote_copy(
            src_ref=fin.at[late], dst_ref=place(core, chip), send_sem=ag_s.at[i], recv_sem=ag_r.at[i],
            device_id=(((chip + i) % CHIPS) * 2 + core, g), device_id_type=MESH,
        )

    own_copy = pltpu.make_async_copy(fin.at[late], place(core, chip), osem.at[1])

    def spread_all():
        def step(i, carry):
            spread_copy(i).start()
            return carry

        lax.fori_loop(1, CHIPS, step, 0)
        own_copy.start()

    @pl.when(late == 0)
    def _():
        spread_all()

    @pl.when(late == 1)
    def _():
        swap.start()

    loads[8].wait()
    loads[9].wait()
    e6.wait_recv()
    for k in range(2):
        mkv[k, R : R + M, :] = (dot(ef[0], wm[0, 1 + k]) + dot(ef[1], wm[1, 1 + k])).astype(BF)
    kup = remote(mkv.at[:, pl.ds(M, R), :], mkv.at[:, pl.ds(0, R), :], KUP, (up, g))
    kdown = remote(mkv.at[:, pl.ds(R, R), :], mkv.at[:, pl.ds(R + M, R), :], KDOWN, (down, g))
    kup.start()
    kdown.start()
    mq[...] = (dot(ef[0], wm[0, 0]) + dot(ef[1], wm[1, 0])).astype(BF)

    @pl.when(late == 1)
    def _():
        swap.wait()
        spread_all()

    def arrived(i, k):
        return place(k, (chip + CHIPS - i) % CHIPS)

    def spread_recv(i):
        return pltpu.make_async_remote_copy(
            src_ref=fin.at[0], dst_ref=arrived(i, core), send_sem=ag_s.at[i], recv_sem=ag_r.at[i],
            device_id=partner, device_id_type=MESH,
        )

    def pass_copy(i, k):
        return pltpu.make_async_remote_copy(
            src_ref=arrived(i, k), dst_ref=arrived(i, k), send_sem=fw_s.at[i], recv_sem=fw_r.at[i],
            device_id=(sib, g), device_id_type=MESH,
        )

    where_n = iota((M, 256), 1) - R
    delta = where_n - iota((M, 256), 0)
    allowed = delta == off[0]
    for j in range(1, W):
        allowed = allowed | (delta == off[j])
    where_g = where_n + s * M
    allowed = allowed & (where_g >= 0) & (where_g < M * SPACE)
    allow = jnp.where(allowed[:, : M + 2 * R], 1.0, 0.0)
    allow4 = jnp.concatenate([allow] * 4, axis=0)
    kup.wait_recv()
    kdown.wait_recv()
    matts = []
    for a in range(2):
        cols = slice(a * 256, (a + 1) * 256)
        x4 = mq[:, cols].astype(F32)
        head = iota((M, 256), 1) // 64
        lhs = jnp.concatenate([jnp.where(head == i, x4, 0.0).astype(BF) for i in range(4)], axis=0)
        raw = dot_t(lhs, mkv[0, :, cols]) * SCALE
        wgt = jnp.exp(CAP * jnp.tanh(raw * (1.0 / CAP))) * allow4
        prob = (wgt / jnp.sum(wgt, axis=1, keepdims=True)).astype(BF)
        matts.append(diagonal(dot(prob, mkv[1, :, cols])).astype(BF))
    matt = jnp.concatenate(matts, axis=1)
    loads[10].wait()
    loads[11].wait()
    mo_send[...] = dot(matt, wmo[1]).astype(BF)
    e8 = remote(mo_send, mo_recv, E8, partner)
    e8.start()
    mo_own[...] = dot(matt, wmo[0])

    gdown.wait_recv()
    gup.wait_recv()
    ggs[0:RIM, :] = (ggs[0:RIM, :].astype(F32) + halo_recv[0].astype(F32)).astype(BF)
    ggs[G - RIM : G, :] = (ggs[G - RIM : G, :].astype(F32) + halo_recv[1].astype(F32)).astype(BF)
    gg_copy = pltpu.make_async_copy(ggs, gg_out, osem.at[2])
    gg_copy.start()

    def sent(i, carry):
        scatter_copy(i).wait_send()
        return carry

    lax.fori_loop(1, CHIPS, sent, 0)
    singles = [e1m, e1c, hup, hdown, e2, e3a, e3b, e4, e5, e6, kup, kdown, gdown, gup]
    for c in singles + wy + [c for c, _ in wring] + wfwd + presum:
        c.wait_send()
    e8.wait()
    mo_val[...] = (ef[0].astype(F32) + mo_own[...] + mo_recv[...].astype(F32)).astype(BF)
    mo_copy = pltpu.make_async_copy(mo_val, mesh_out, osem.at[3])
    mo_copy.start()

    own_copy.wait()
    pass_copy(0, core).start()

    def pass_on(i, carry):
        spread_copy(i).wait_send()
        spread_recv(i).wait_recv()
        pass_copy(i, core).start()
        return carry

    lax.fori_loop(1, CHIPS, pass_on, 0)

    def finish(i, carry):
        pass_copy(i, 1 - core).wait_recv()
        pass_copy(i, core).wait_send()
        return carry

    lax.fori_loop(0, CHIPS, finish, 0)

    enc_copy.wait()
    gg_copy.wait()
    mo_copy.wait()


def write_results(enc, mesh_o, gg, gkv, enc_out, mesh_out, gg_out, gkv_out, e, m, r, low, wide, s_in, s_out, k_in, k_out):
    plain = ((enc, e, enc_out), (mesh_o, m, mesh_out), (gg, r, gg_out))
    parts = [(n // 4, pl.ds(n % 4 * 256, 256)) for n in range(8)]
    loads = [pltpu.make_async_copy(gkv.at[k, rows], low.at[k, rows], k_in.at[n]) for n, (k, rows) in enumerate(parts)]
    others = [pltpu.make_async_copy(a, b, s_in.at[n]) for n, (a, b, _) in enumerate(plain)]
    for c in loads + others:
        c.start()
    stores = []
    for n, (k, rows) in enumerate(parts):
        loads[n].wait()
        wide[k, rows] = low[k, rows].astype(F32)
        stores.append(pltpu.make_async_copy(wide.at[k, rows], gkv_out.at[k, rows], k_out.at[n]))
        stores[-1].start()
    for n, (_, b, c) in enumerate(plain):
        others[n].wait()
        stores.append(pltpu.make_async_copy(b, c, s_out.at[n]))
        stores[-1].start()
    for c in stores:
        c.wait()


def shards(
    grid_feat, mesh_feat, edge_src, degree, offsets, w_kv, w_query, w_out, w_mesh, w_mesh_out, cotangent
):
    hbm = pl.BlockSpec(memory_space=pl.ANY)
    vmem = pl.BlockSpec(memory_space=pltpu.VMEM)
    smem = pl.BlockSpec(memory_space=pltpu.SMEM)

    def v(*shape, dtype=BF):
        return pltpu.VMEM(shape, dtype)

    dma = pltpu.SemaphoreType.DMA
    scratch = dict(
        nodes=v(M, K, dtype=I32), wide=v(WIDE, F), mf=v(2, M, F), cf=v(2, M, F), wkv_own=v(2, F, F), wkv_oth=v(2, F, F),
        wq=v(2, F, F), wo=v(2, F, F), wm=v(2, 3, F, F), wmo=v(2, F, F),
        qd=v(2, 2, M, F), qdt=v(2, 2, F, M), xs=v(G, F), ut=v(2, 16, M, F), zy=v(2, 16, M, F),
        srow=v(8, G, dtype=F32),
        sd=v(2, 8, K, 256, dtype=F32), sd_send=v(2, 8, K, 256), sd_recv=v(2, 8, K, 256), pb=v(8, K, 512),
        att_own=v(M, F, dtype=F32), att_send=v(M, F), att_recv=v(M, F),
        enc_own=v(M, F, dtype=F32), enc_send=v(M, F), enc_recv=v(M, F), ef=v(2, M, F),
        mkv=v(2, M + 2 * R, F), mq=v(M, F),
        mo_own=v(M, F, dtype=F32), mo_send=v(M, F), mo_recv=v(M, F), mo_val=v(M, F),
        gedge=v(G, F), halo_send=v(2, RIM, F), halo_recv=v(2, RIM, F), ggs=v(G, F),
        gb=v(2, CHIPS, 128, 128), pre=v(CHIPS, 128, 128), rsb=v(CHIPS, 128, 128), fin=v(2, 128, 128),
        lsem=dma((12,)), osem=dma((4,)), ssem=dma((N_REMOTE,)), rsem=dma((N_REMOTE,)),
        rs_s=dma((CHIPS,)), rs_r=dma((CHIPS,)), ag_s=dma((CHIPS,)), ag_r=dma((CHIPS,)),
        fw_s=dma((CHIPS,)), fw_r=dma((CHIPS,)), known=pltpu.SemaphoreType.REGULAR((6,)),
    )
    enc, mesh_out, grad_grid, grad_kv = pl.pallas_call(
        body,
        out_shape=(
            jax.ShapeDtypeStruct((M, F), BF),
            jax.ShapeDtypeStruct((M, F), BF),
            jax.ShapeDtypeStruct((G, F), BF),
            jax.ShapeDtypeStruct((2, 2 * F, F), BF),
        ),
        in_specs=[hbm, hbm, vmem, vmem, smem, hbm, hbm, hbm, hbm, hbm, hbm],
        out_specs=(hbm, hbm, hbm, hbm),
        scratch_shapes=list(scratch.values()),
        compiler_params=pltpu.CompilerParams(
            collective_id=0, has_side_effects=True, vmem_limit_bytes=58 * 2**20
        ),
        name="encoder",
    )(
        grid_feat, mesh_feat, edge_src.T, degree.reshape(1, M), offsets, w_kv, w_query, w_out, w_mesh,
        w_mesh_out, cotangent,
    )
    dma = pltpu.SemaphoreType.DMA
    return pl.pallas_call(
        write_results,
        out_shape=(
            jax.ShapeDtypeStruct((M, F), BF),
            jax.ShapeDtypeStruct((M, F), BF),
            jax.ShapeDtypeStruct((G, F), BF),
            jax.ShapeDtypeStruct((2, 2 * F, F), F32),
        ),
        in_specs=[hbm] * 4,
        out_specs=(hbm,) * 4,
        scratch_shapes=[
            v(M, F), v(M, F), v(G, F), v(2, 2 * F, F), v(2, 2 * F, F, dtype=F32),
            dma((3,)), dma((3,)), dma((8,)), dma((8,)),
        ],
        compiler_params=pltpu.CompilerParams(vmem_limit_bytes=58 * 2**20),
        name="results",
    )(enc, mesh_out, grad_grid, grad_kv)


def solution(mesh):
    in_specs = (
        P("space", "head"),
        P("space", "head"),
        P("space", None),
        P("space"),
        P(),
        P(None, None, "head"),
        P(None, "head"),
        P("head", None),
        P(None, None, "head"),
        P("head", None),
        P("space", "head"),
    )
    out_specs = (P("space", "head"), P("space", "head"), P("space", "head"), P(None, None, "head"))
    return jax.shard_map(shards, mesh=mesh, in_specs=in_specs, out_specs=out_specs, check_vma=False)
```

```python
import functools

import jax
import jax.numpy as jnp
from jax import lax
from jax.experimental import pallas as pl
from jax.experimental.pallas import tpu as pltpu
from jax.sharding import PartitionSpec as P

BF = jnp.bfloat16
F32 = jnp.float32
I32 = jnp.int32
MESH = pl.DeviceIdType.MESH

M = 128
K = 16
G = 2048
RIM = 128
WIDE = G + 2 * RIM
R = 32
W = 16
F = 512
HL = 8
SPACE = 64
CHIPS = SPACE // 2
CAP = 3.0
SCALE = 0.125

(
    E1M, E1C, HUP, HDOWN, E2, E3A, E3B, E4, E5, E6, KUP, KDOWN, E8, GUP, GDOWN,
    RS3, RS3P, AG1, WY, WR, WF, PRE, RS1, RS2, AG2, AG3, AGF,
) = list(range(19)) + [20, 26, 34, 36, 42, 48, 54, 60]
N_REMOTE = 68


def dot(a, b):
    return jnp.dot(a, b, preferred_element_type=F32)


def dot_t(a, b):
    return lax.dot_general(a, b, (((1,), (1,)), ((), ())), preferred_element_type=F32)


def dot_first(a, b):
    return lax.dot_general(a, b, (((0,), (0,)), ((), ())), preferred_element_type=F32)


def iota(shape, dim):
    return lax.broadcasted_iota(I32, shape, dim)


def body(
    grid_in, mesh_in, src, deg, off, wkv_in, wq_in, wo_in, wm_in, wmo_in, cot_in,
    enc_out, mesh_out, gg_out, gkv_out,
    nodes, wide, mf, cf, wkv_own, wkv_oth, wq, wo, wm, wmo, qd, qdt, xs, ut, zy, srow,
    sd, sd_send, sd_recv, pb, att_own, att_send, att_recv, enc_own, enc_send, enc_recv, ef, mkv, mq,
    mo_own, mo_send, mo_recv, mo_val, gedge, halo_send, halo_recv, ggs,
    gb, pre, rs1, rsum, rs2, tt, tp, rec, bq, bp, blocks,
    lsem, osem, ssem, rsem, out_s,
):
    s = lax.axis_index("space")
    g = lax.axis_index("head")
    o = 1 - g
    core = s % 2
    chip = s // 2
    sib = s + 1 - 2 * core
    up = (s + 1) % SPACE
    down = (s + SPACE - 1) % SPACE

    def flip(bit):
        return s + bit - 2 * bit * ((s // bit) % 2)

    ylo = (s // 8) % 2
    across = flip(8)
    at_x, at_z = chip // 8, chip % 4

    def along(axis, d):
        return (s + 16 * d) % SPACE if axis == 0 else s - 2 * at_z + 2 * ((at_z + d) % 4)

    far = s - 1 + 2 * core
    far = (far + SPACE) % SPACE

    def remote(src_ref, dst_ref, n, dev):
        return pltpu.make_async_remote_copy(
            src_ref=src_ref, dst_ref=dst_ref, send_sem=ssem.at[n], recv_sem=rsem.at[n],
            device_id=dev, device_id_type=MESH,
        )

    partner = (s, o)
    mine = pl.ds(pl.multiple_of(g * F, F), F)
    other = pl.ds(pl.multiple_of(o * F, F), F)

    local = [
        (mesh_in, mf.at[0]),
        (cot_in, cf.at[0]),
        (wq_in.at[mine, :], wq.at[0]),
        (wo_in.at[:, mine], wo.at[0]),
        (wq_in.at[other, :], wq.at[1]),
        (wo_in.at[:, other], wo.at[1]),
        (wkv_in.at[:, mine, :], wkv_own),
        (grid_in, wide.at[pl.ds(RIM, G), :]),
        (wm_in.at[:, mine, :], wm.at[0]),
        (wm_in.at[:, other, :], wm.at[1]),
        (wmo_in.at[:, mine], wmo.at[0]),
        (wmo_in.at[:, other], wmo.at[1]),
    ]
    loads = [pltpu.make_async_copy(a, b, lsem.at[i]) for i, (a, b) in enumerate(local)]
    for c in loads:
        c.start()

    first = [partner, (across, o), (across, g), (sib, g), (far, g)]
    first += [(along(axis, d), g) for axis in range(2) for d in (1, 2, 3)]
    barrier = pltpu.get_barrier_semaphore()
    for dev in first:
        pl.semaphore_signal(barrier, inc=1, device_id=dev, device_id_type=MESH)
    pl.semaphore_wait(barrier, len(first))

    e1m = remote(mesh_in, mf.at[1], E1M, partner)
    e1c = remote(cot_in, cf.at[1], E1C, partner)
    hup = remote(grid_in.at[pl.ds(G - RIM, RIM), :], wide.at[pl.ds(0, RIM), :], HUP, (up, g))
    hdown = remote(grid_in.at[pl.ds(0, RIM), :], wide.at[pl.ds(RIM + G, RIM), :], HDOWN, (down, g))

    def piece(k, axis, q):
        return wkv_oth.at[k, pl.ds(pl.multiple_of(axis * 256 + q * 64, 64), 64), :]

    at = (at_x, at_z)
    wy, wring, wfwd, wback = [], [], [], []
    for axis in range(2):
        rows = pl.ds(pl.multiple_of(o * F + axis * 256 + at[axis] * 64, 64), 64)
        here = piece(core, axis, at[axis])
        wy.append(remote(wkv_in.at[core, rows, :], here, WY + axis, (across, o)))
        for d in range(4):
            q = (at[axis] + 4 - d) % 4
            if d:
                n = WR + 3 * axis + d - 1
                wring.append((
                    remote(here, here, n, (along(axis, d), g)),
                    remote(piece(core, axis, q), piece(core, axis, q), n, partner),
                ))
            n = WF + 4 * axis + d
            wfwd.append(remote(piece(core, axis, q), piece(core, axis, q), n, (sib, g)))
            wback.append(remote(piece(1 - core, axis, q), piece(1 - core, axis, q), n, (sib, g)))
    for c in wy:
        c.start()
    hup.start()
    hdown.start()
    e1m.start()
    e1c.start()

    base = s * G - RIM
    source = src[...].astype(F32).T.astype(I32)
    nodes[...] = source
    rel = source - base
    rel = jnp.where((rel >= 0) & (rel < WIDE), rel, 4095)
    hi = (rel // 64).astype(F32).astype(BF)
    lo = (rel % 64).astype(F32).astype(BF)
    spread = jnp.where(iota((K, 256), 0) == (iota((K, 256), 1) & 15), 1.0, 0.0).astype(BF)
    flat = dot(hi, spread) * 64.0 + dot(lo, spread)
    flat = jnp.where((iota((M, 256), 0) & 15) == iota((M, 256), 1) // 16, flat, 0.0)
    for t in range(8):
        srow[0:1, t * 256 : (t + 1) * 256] = jnp.sum(
            flat[t * 16 : (t + 1) * 16], axis=0, keepdims=True
        )

    for c in wy:
        c.wait_recv()
    for c, _ in wring:
        c.start()
    wfwd[0].start()
    wfwd[4].start()

    loads[7].wait()
    hup.wait_recv()
    hdown.wait_recv()

    def gather(t, carry):
        n = pl.multiple_of(t * 32, 32)
        part = (nodes[pl.ds(n, 32), :] - base).astype(F32)
        part = jnp.broadcast_to(part[:, None, :], (32, K, K)).reshape(512, K)
        pick = (iota((512, K), 0) & 15) == iota((512, K), 1)
        col = jnp.sum(jnp.where(pick, part, 0.0), axis=1, keepdims=True).astype(I32)
        hot = jnp.where(iota((512, WIDE), 1) == col, 1.0, 0.0).astype(BF)
        xs[pl.ds(pl.multiple_of(t * 512, 512), 512), :] = dot(hot, wide[...]).astype(BF)
        return carry

    lax.fori_loop(0, 3, gather, 0)

    for n in (0, 1, 2, 3):
        loads[n].wait()
    qa = dot(mf[0], wq[0])
    da = dot_t(cf[0], wo[0])
    loads[4].wait()
    loads[5].wait()
    e1m.wait_recv()
    e1c.wait_recv()
    qa = qa + dot(mf[1], wq[1])
    da = da + dot_t(cf[1], wo[1])
    qd[0, 0] = qa.astype(BF)
    qd[0, 1] = da.astype(BF)
    e2 = remote(qd.at[0], qd.at[1], E2, partner)
    e2.start()
    for n, (_, c) in enumerate(wring):
        c.wait_recv()
        wfwd[n + 1 + n // 3].start()

    lax.fori_loop(3, 4, gather, 0)

    def turn(side):
        for k in range(2):
            qdt[side, k] = qd[side, k].astype(F32).T.astype(BF)

    turn(0)

    def expand(side, weights):
        for k in range(2):
            for a in range(2):
                x4 = qd[side, k, :, a * 256 : (a + 1) * 256].astype(F32)
                head = iota((M, 256), 1) // 64
                lhs = jnp.concatenate(
                    [jnp.where(head == i, x4, 0.0).astype(BF) for i in range(4)], axis=0
                )
                out = dot_t(lhs, weights[k, :, a * 256 : (a + 1) * 256]).astype(BF)
                n = side * HL + a * 4
                ut[k, n : n + 4] = out.reshape(4, M, F)

    loads[6].wait()
    expand(0, wkv_own)


    def scores(side):
        def step(t, carry):
            xg = xs[pl.ds(pl.multiple_of(t * 256, 256), 256), :]
            lane = iota((K, 256), 1) & 15
            ug = ut[:, side * HL : side * HL + HL, pl.ds(pl.multiple_of(t * 16, 16), 16), :]
            full = dot_t(xg, ug.reshape(256, F)).reshape(16, K, 256)
            total = jnp.where(lane == 0, full[0], 0.0)
            for m in range(1, 16):
                total = total + jnp.where(lane == m, full[m], 0.0)
            sd[side, t] = total
            sd_send[side, t] = total.astype(BF)
            return carry

        lax.fori_loop(0, 8, step, 0, unroll=2)

    e3a = remote(sd_send.at[0], sd_recv.at[1], E3A, partner)
    e3b = remote(sd_send.at[1], sd_recv.at[0], E3B, partner)
    scores(0)
    e3a.start()
    e2.wait_recv()
    turn(1)
    for c in wback:
        c.wait_recv()
    expand(1, wkv_oth)

    scores(1)
    e3b.start()

    dg = deg[...].astype(F32)
    dg = jnp.where(iota((8, M), 1) // 16 == iota((8, M), 0), dg, 0.0).astype(BF)
    tile = jnp.where((iota((M, 128), 0) & 15) == (iota((M, 128), 1) & 15), 1.0, 0.0).astype(BF)
    dlane = dot(dg, tile)
    live = iota((8, K, 128), 1).astype(F32) < dlane[:, None, :]

    for side in (1, 0):
        (e3a if side else e3b).wait_recv()
        raw = (sd[side, :, :, :128] + sd_recv[side, :, :, :128].astype(F32)) * SCALE
        dp = sd[side, :, :, 128:] + sd_recv[side, :, :, 128:].astype(F32)
        th = jnp.tanh(raw * (1.0 / CAP))
        wgt = jnp.where(live, jnp.exp(CAP * th), 0.0)
        prob = wgt / jnp.sum(wgt, axis=1, keepdims=True)
        ds = prob * (dp - jnp.sum(prob * dp, axis=1, keepdims=True))
        dr = ds * (1.0 - th * th) * SCALE
        a = side * 128
        pb[:, :, a : a + 128] = dr.astype(BF)
        pb[:, :, 256 + a : 256 + a + 128] = prob.astype(BF)

    def sums(t, carry):
        xg = xs[pl.ds(pl.multiple_of(t * 256, 256), 256), :]
        same = (iota((512, 256), 0) & 15) == iota((512, 256), 1) // 16
        sel = jnp.where(iota((K, 256), 0) == (iota((K, 256), 1) & 15), 1.0, 0.0).astype(BF)
        pt = jnp.where(same, dot_first(pb[t], sel), 0.0).astype(BF)
        out = dot(pt, xg).astype(BF)
        zy[:, :, pl.ds(pl.multiple_of(t * 16, 16), 16), :] = out.reshape(2, 16, 16, F)
        return carry

    lax.fori_loop(0, 8, sums, 0, unroll=2)

    def diagonal(x):
        x = x.reshape(4, M, 256)
        head = iota((M, 256), 1) // 64
        out = jnp.zeros((M, 256), F32)
        for i in range(4):
            out = out + jnp.where(head == i, x[i], 0.0)
        return out

    def weight_terms(n, carry):
        k = (1 - core) + n * (2 * core - 1)
        for side in range(2):
            for p in range(4):
                xt = qdt[side, k, p * 128 : (p + 1) * 128, :].astype(F32)
                first = iota((128, M), 0) < 64
                lhs = jnp.concatenate(
                    [jnp.where(first, xt, 0.0).astype(BF), jnp.where(first, 0.0, xt).astype(BF)], axis=1
                )
                h = side * HL + 2 * p
                rhs = zy[k, h : h + 2].reshape(2 * M, F)
                out = dot(lhs, rhs).astype(BF)
                for f in range(4):
                    x, y = 2 * side + p // 2, p % 2
                    gb[k, 0, f, 2 * x + y] = out[:64, f * 128 : (f + 1) * 128]
                    gb[k, 1, x, 2 * f + y] = out[64:, f * 128 : (f + 1) * 128]
        return carry

    weight_terms(0, 0)
    presum = [
        remote(gb.at[1 - core, n], pre.at[n], PRE + n, (sib, g))
        for n in range(2)
    ]
    for c in presum:
        c.start()
    for a in range(2):
        z4 = zy[1, HL + a * 4 : HL + a * 4 + 4].reshape(4 * M, F)
        att_send[:, a * 256 : (a + 1) * 256] = diagonal(
            dot(z4, wkv_oth[1, :, a * 256 : (a + 1) * 256])
        ).astype(BF)
    e4 = remote(att_send, att_recv, E4, partner)
    e4.start()
    weight_terms(1, 0)
    for a in range(2):
        z4 = zy[1, a * 4 : a * 4 + 4].reshape(4 * M, F)
        att_own[:, a * 256 : (a + 1) * 256] = diagonal(
            dot(z4, wkv_own[1, :, a * 256 : (a + 1) * 256])
        )


    line = (at_z, at_x)
    axis_of = (1, 0)

    def ring(h, stage, d):
        return (along(axis_of[h] if stage == 1 else 1 - axis_of[h], d), g)

    def ahead(n, d):
        return (n + d) % 4

    stage1 = [
        remote(gb.at[core, h, ahead(line[h], d)], rs1.at[h, d - 1], RS1 + 3 * h + d - 1, ring(h, 1, d))
        for h in range(2)
        for d in (1, 2, 3)
    ]
    for h in range(2):
        presum[h].wait_recv()
        for n in range(4):
            gb[core, h, n] = (gb[core, h, n].astype(F32) + pre[h, n].astype(F32)).astype(BF)
        for c in stage1[3 * h : 3 * h + 3]:
            c.start()

    e4.wait_recv()
    att = (att_own[...] + att_recv[...].astype(F32)).astype(BF)
    enc_send[...] = dot(att, wo[1]).astype(BF)
    e5 = remote(enc_send, enc_recv, E5, partner)
    e5.start()
    enc_own[...] = dot(att, wo[0])

    def edge_grads(t, carry):
        rows = pl.ds(pl.multiple_of(t * 16, 16), 16)
        match = (iota((16, K, 512), 2) & 15) == iota((16, K, 512), 0)
        p = jnp.broadcast_to(pb[t].astype(F32)[None], (16, K, 512))
        p = jnp.where(match, p, 0.0).astype(BF).reshape(256, 512)
        total = dot(p, ut[:, :, rows, :].reshape(512, F))
        gedge[pl.ds(pl.multiple_of(t * 256, 256), 256), :] = total.astype(BF)
        return carry

    lax.fori_loop(0, 8, edge_grads, 0, unroll=2)

    e5.wait_recv()
    enc = (mf[0].astype(F32) + enc_own[...] + enc_recv[...].astype(F32)).astype(BF)
    ef[0] = enc
    e6 = remote(ef.at[0], ef.at[1], E6, partner)
    e6.start()
    enc_copy = pltpu.make_async_copy(ef.at[0], enc_out, osem.at[0])
    enc_copy.start()

    def rows_of(first, count):
        hot = jnp.where(
            (iota((count, G), 0) + first).astype(F32) == srow[0:1, :], 1.0, 0.0
        ).astype(BF)
        return dot(hot, gedge[...])

    halo_send[0] = rows_of(0, RIM).astype(BF)
    halo_send[1] = rows_of(RIM + G, RIM).astype(BF)
    gdown = remote(halo_send.at[0], halo_recv.at[1], GDOWN, (down, g))
    gup = remote(halo_send.at[1], halo_recv.at[0], GUP, (up, g))
    gdown.start()
    gup.start()

    stage2 = [
        remote(
            rsum.at[h, pl.ds(2 * ahead(line[1 - h], d), 2)], rs2.at[h, d - 1], RS2 + 3 * h + d - 1, ring(h, 2, d)
        )
        for h in range(2)
        for d in (1, 2, 3)
    ]
    for h in range(2):
        for d in range(3):
            stage1[3 * h + d].wait_recv()
        total = gb[core, h, line[h]].astype(F32)
        for d in range(3):
            total = total + rs1[h, d].astype(F32)
        rsum[h] = total.astype(BF)
        for c in stage2[3 * h : 3 * h + 3]:
            c.start()

    def interior(t, carry):
        n = pl.multiple_of(t * 512, 512)
        ggs[pl.ds(n, 512), :] = rows_of(n + RIM, 512).astype(BF)
        return carry

    lax.fori_loop(0, 2, interior, 0)

    late = at_x // 2
    for h in range(2):
        for d in range(3):
            stage2[3 * h + d].wait_recv()
        total = rsum[h, pl.ds(2 * line[1 - h], 2)].astype(F32)
        for d in range(3):
            total = total + rs2[h, d].astype(F32)
        for y in range(2):
            tt[y, h] = total[y].astype(BF)
    stage3 = remote(tt.at[1 - ylo], rec, RS3, (across, g + late * (1 - 2 * g)))
    stage3p = remote(tt.at[ylo], tp, RS3P, partner)
    stage3.start()

    @pl.when(late == 1)
    def _():
        stage3p.start()

    loads[8].wait()
    loads[9].wait()
    e6.wait_recv()
    for k in range(2):
        mkv[k, R : R + M, :] = (dot(ef[0], wm[0, 1 + k]) + dot(ef[1], wm[1, 1 + k])).astype(BF)
    kup = remote(mkv.at[:, pl.ds(M, R), :], mkv.at[:, pl.ds(0, R), :], KUP, (up, g))
    kdown = remote(mkv.at[:, pl.ds(R, R), :], mkv.at[:, pl.ds(R + M, R), :], KDOWN, (down, g))
    kup.start()
    kdown.start()
    mq[...] = (dot(ef[0], wm[0, 0]) + dot(ef[1], wm[1, 0])).astype(BF)

    stage3.wait_recv()

    @pl.when(late == 0)
    def _():
        tp[...] = tt[ylo]

    @pl.when(late == 1)
    def _():
        stage3p.wait()

    block = (tp[...].astype(F32) + rec[...].astype(F32)).reshape(128, 128).T.astype(BF)

    bq[0, ylo] = block[:64]
    bq[1, ylo] = block[64:]
    back1 = remote(bq.at[:, ylo], bq.at[:, ylo], AG1, (across, g))
    back1.start()
    lax.fori_loop(2, 3, interior, 0)
    remote(bq.at[:, 1 - ylo], bq.at[:, 1 - ylo], AG1, (across, g)).wait_recv()

    back2, back2_in, back3, back3_in = [], [], [], []
    for h in range(2):
        for d in (1, 2, 3):
            n = 3 * h + d - 1
            from2, from3 = ahead(line[1 - h], 4 - d), ahead(line[h], 4 - d)
            back2.append(remote(bq.at[h], bp.at[h, line[1 - h]], AG2 + n, ring(h, 2, d)))
            back2_in.append(remote(bq.at[h], bp.at[h, from2], AG2 + n, partner))
            back3.append(remote(bp.at[h], blocks.at[core, h, line[h]], AG3 + n, ring(h, 1, d)))
            back3_in.append(remote(bp.at[h], blocks.at[core, h, from3], AG3 + n, partner))
    for c in back2:
        c.start()
    for h in range(2):
        bp[h, line[1 - h]] = bq[h]

    where_n = iota((M, 256), 1) - R
    delta = where_n - iota((M, 256), 0)
    allowed = delta == off[0]
    for j in range(1, W):
        allowed = allowed | (delta == off[j])
    where_g = where_n + s * M
    allowed = allowed & (where_g >= 0) & (where_g < M * SPACE)
    allow = jnp.where(allowed[:, : M + 2 * R], 1.0, 0.0)
    allow4 = jnp.concatenate([allow] * 4, axis=0)
    kup.wait_recv()
    kdown.wait_recv()
    matts = []
    for a in range(2):
        cols = slice(a * 256, (a + 1) * 256)
        x4 = mq[:, cols].astype(F32)
        head = iota((M, 256), 1) // 64
        lhs = jnp.concatenate([jnp.where(head == i, x4, 0.0).astype(BF) for i in range(4)], axis=0)
        raw = dot_t(lhs, mkv[0, :, cols]) * SCALE
        wgt = jnp.exp(CAP * jnp.tanh(raw * (1.0 / CAP))) * allow4
        prob = (wgt / jnp.sum(wgt, axis=1, keepdims=True)).astype(BF)
        matts.append(diagonal(dot(prob, mkv[1, :, cols])).astype(BF))
    matt = jnp.concatenate(matts, axis=1)
    loads[10].wait()
    loads[11].wait()
    mo_send[...] = dot(matt, wmo[1]).astype(BF)
    e8 = remote(mo_send, mo_recv, E8, partner)
    e8.start()
    mo_own[...] = dot(matt, wmo[0])

    for h in range(2):
        for c in back2_in[3 * h : 3 * h + 3]:
            c.wait_recv()
        for c in back3[3 * h : 3 * h + 3]:
            c.start()
        blocks[core, h, line[h]] = bp[h]

    def pass_copy(k, h, d):
        part = blocks.at[k, h, ahead(line[h], 4 - d)]
        return remote(part, part, AGF + 4 * h + d, (sib, g))

    def result_copy(k, h, d):
        n = ahead(line[h], 4 - d)
        return pltpu.make_async_copy(blocks.at[k, h, n], gkv_out.at[k, h, n], out_s.at[k, 4 * h + d])

    passed = [pass_copy(core, h, d) for h in range(2) for d in range(4)]
    handed = [pass_copy(1 - core, h, d) for h in range(2) for d in range(4)]
    mine_out = [result_copy(core, h, d) for h in range(2) for d in range(4)]
    other_out = [result_copy(1 - core, h, d) for h in range(2) for d in range(4)]
    for n in (0, 4):
        passed[n].start()
        mine_out[n].start()

    lax.fori_loop(3, 4, interior, 0)
    gdown.wait_recv()
    gup.wait_recv()
    ggs[0:RIM, :] = (ggs[0:RIM, :].astype(F32) + halo_recv[0].astype(F32)).astype(BF)
    ggs[G - RIM : G, :] = (ggs[G - RIM : G, :].astype(F32) + halo_recv[1].astype(F32)).astype(BF)
    gg_copy = pltpu.make_async_copy(ggs, gg_out, osem.at[2])
    gg_copy.start()

    singles = [e1m, e1c, hup, hdown, e2, e3a, e3b, e4, e5, e6, kup, kdown, gdown, gup, stage3, back1]
    for c in singles + wy + [c for c, _ in wring] + wfwd + presum + stage1 + stage2 + back2:
        c.wait_send()
    e8.wait()
    mo_val[...] = (ef[0].astype(F32) + mo_own[...] + mo_recv[...].astype(F32)).astype(BF)
    mo_copy = pltpu.make_async_copy(mo_val, mesh_out, osem.at[3])
    mo_copy.start()

    for d in (1, 2, 3):
        for h in range(2):
            back3_in[3 * h + d - 1].wait_recv()
            passed[4 * h + d].start()
            mine_out[4 * h + d].start()
    for c in back3:
        c.wait_send()
    for d in range(4):
        for h in range(2):
            handed[4 * h + d].wait_recv()
            other_out[4 * h + d].start()
    for c in passed:
        c.wait_send()
    enc_copy.wait()
    gg_copy.wait()
    mo_copy.wait()
    for c in mine_out + other_out:
        c.wait()


def write_results(enc, mesh_o, gg, gkv, enc_out, mesh_out, gg_out, gkv_out, e, m, r, low, wide, s_in, s_out, k_in, k_out):
    plain = ((enc, e, enc_out), (mesh_o, m, mesh_out), (gg, r, gg_out))
    g = lax.axis_index("head")
    loads = [pltpu.make_async_copy(gkv.at[k], low.at[k], k_in.at[k]) for k in range(2)]
    others = [pltpu.make_async_copy(a, b, s_in.at[n]) for n, (a, b, _) in enumerate(plain)]
    for c in loads + others:
        c.start()
    stores = []
    for k in range(2):
        loads[k].wait()
        for n in range(2):
            half = g if n == 0 else 1 - g
            for x in (2 * n, 2 * n + 1):
                for z in range(4):
                    for y in range(2):
                        col = (x % 2 * 2 + y) * 128
                        for h in range(2):
                            rows = pl.ds(pl.multiple_of(half * F + z * 128 + h * 64, 64), 64)
                            part = low[k, 0, z, x, y] if h == 0 else low[k, 1, x, z, y]
                            wide[k, rows, col : col + 128] = part.astype(F32)
            rows = pl.ds(pl.multiple_of(half * F, F), F)
            stores.append(pltpu.make_async_copy(wide.at[k, rows], gkv_out.at[k, rows], k_out.at[2 * k + n]))
            stores[-1].start()
    for n, (_, b, c) in enumerate(plain):
        others[n].wait()
        stores.append(pltpu.make_async_copy(b, c, s_out.at[n]))
        stores[-1].start()
    for c in stores:
        c.wait()


def shards(
    grid_feat, mesh_feat, edge_src, degree, offsets, w_kv, w_query, w_out, w_mesh, w_mesh_out, cotangent
):
    hbm = pl.BlockSpec(memory_space=pl.ANY)
    vmem = pl.BlockSpec(memory_space=pltpu.VMEM)
    smem = pl.BlockSpec(memory_space=pltpu.SMEM)

    def v(*shape, dtype=BF):
        return pltpu.VMEM(shape, dtype)

    dma = pltpu.SemaphoreType.DMA
    scratch = dict(
        nodes=v(M, K, dtype=I32), wide=v(WIDE, F), mf=v(2, M, F), cf=v(2, M, F), wkv_own=v(2, F, F), wkv_oth=v(2, F, F),
        wq=v(2, F, F), wo=v(2, F, F), wm=v(2, 3, F, F), wmo=v(2, F, F),
        qd=v(2, 2, M, F), qdt=v(2, 2, F, M), xs=v(G, F), ut=v(2, 16, M, F), zy=v(2, 16, M, F),
        srow=v(8, G, dtype=F32),
        sd=v(2, 8, K, 256, dtype=F32), sd_send=v(2, 8, K, 256), sd_recv=v(2, 8, K, 256), pb=v(8, K, 512),
        att_own=v(M, F, dtype=F32), att_send=v(M, F), att_recv=v(M, F),
        enc_own=v(M, F, dtype=F32), enc_send=v(M, F), enc_recv=v(M, F), ef=v(2, M, F),
        mkv=v(2, M + 2 * R, F), mq=v(M, F),
        mo_own=v(M, F, dtype=F32), mo_send=v(M, F), mo_recv=v(M, F), mo_val=v(M, F),
        gedge=v(G, F), halo_send=v(2, RIM, F), halo_recv=v(2, RIM, F), ggs=v(G, F),
        gb=v(2, 2, 4, 8, 64, 128), pre=v(2, 4, 8, 64, 128), rs1=v(2, 3, 8, 64, 128), rsum=v(2, 8, 64, 128),
        rs2=v(2, 3, 2, 64, 128), tt=v(2, 2, 64, 128), tp=v(2, 64, 128), rec=v(2, 64, 128),
        bq=v(2, 2, 64, 128), bp=v(2, 4, 2, 64, 128), blocks=v(2, 2, 4, 4, 2, 64, 128),
        lsem=dma((12,)), osem=dma((4,)), ssem=dma((N_REMOTE,)), rsem=dma((N_REMOTE,)),
        out_s=dma((2, 8)),
    )
    enc, mesh_out, grad_grid, grad_kv = pl.pallas_call(
        body,
        out_shape=(
            jax.ShapeDtypeStruct((M, F), BF),
            jax.ShapeDtypeStruct((M, F), BF),
            jax.ShapeDtypeStruct((G, F), BF),
            jax.ShapeDtypeStruct((2, 2, 4, 4, 2, 64, 128), BF),
        ),
        in_specs=[hbm, hbm, vmem, vmem, smem, hbm, hbm, hbm, hbm, hbm, hbm],
        out_specs=(hbm, hbm, hbm, hbm),
        scratch_shapes=list(scratch.values()),
        compiler_params=pltpu.CompilerParams(
            collective_id=0, has_side_effects=True, vmem_limit_bytes=58 * 2**20
        ),
        name="encoder",
    )(
        grid_feat, mesh_feat, edge_src.T, degree.reshape(1, M), offsets, w_kv, w_query, w_out, w_mesh,
        w_mesh_out, cotangent,
    )
    dma = pltpu.SemaphoreType.DMA
    return pl.pallas_call(
        write_results,
        out_shape=(
            jax.ShapeDtypeStruct((M, F), BF),
            jax.ShapeDtypeStruct((M, F), BF),
            jax.ShapeDtypeStruct((G, F), BF),
            jax.ShapeDtypeStruct((2, 2 * F, F), F32),
        ),
        in_specs=[hbm] * 4,
        out_specs=(hbm,) * 4,
        scratch_shapes=[
            v(M, F), v(M, F), v(G, F), v(2, 2, 4, 4, 2, 64, 128), v(2, 2 * F, F, dtype=F32),
            dma((3,)), dma((3,)), dma((2,)), dma((4,)),
        ],
        compiler_params=pltpu.CompilerParams(vmem_limit_bytes=58 * 2**20),
        name="results",
    )(enc, mesh_out, grad_grid, grad_kv)


def solution(mesh):
    in_specs = (
        P("space", "head"),
        P("space", "head"),
        P("space", None),
        P("space"),
        P(),
        P(None, None, "head"),
        P(None, "head"),
        P("head", None),
        P(None, None, "head"),
        P("head", None),
        P("space", "head"),
    )
    out_specs = (P("space", "head"), P("space", "head"), P("space", "head"), P(None, None, "head"))
    return jax.shard_map(shards, mesh=mesh, in_specs=in_specs, out_specs=out_specs, check_vma=False)
```

```python
import functools

import jax
import jax.numpy as jnp
from jax import lax
from jax.experimental import pallas as pl
from jax.experimental.pallas import tpu as pltpu
from jax.sharding import PartitionSpec as P

BF = jnp.bfloat16
F32 = jnp.float32
I32 = jnp.int32
MESH = pl.DeviceIdType.MESH

M = 128
K = 16
G = 2048
RIM = 128
WIDE = G + 2 * RIM
R = 32
W = 16
F = 512
HL = 8
SPACE = 64
CHIPS = SPACE // 2
CAP = 3.0
SCALE = 0.125

(
    E1M, E1C, HUP, HDOWN, E2, E3A, E3B, E4, E5, E6, KUP, KDOWN, E8, GUP, GDOWN,
    RS3, RS3P, E2D, WY, WR, WF, PRE, RS1, RS2, AG2, AG3, AGF,
) = list(range(19)) + [20, 26, 34, 42, 48, 54, 68, 74]
N_REMOTE = 82


def dot(a, b):
    return jnp.dot(a, b, preferred_element_type=F32)


def dot_t(a, b):
    return lax.dot_general(a, b, (((1,), (1,)), ((), ())), preferred_element_type=F32)


def dot_first(a, b):
    return lax.dot_general(a, b, (((0,), (0,)), ((), ())), preferred_element_type=F32)


def iota(shape, dim):
    return lax.broadcasted_iota(I32, shape, dim)


def body(
    grid_in, mesh_in, src, deg, off, wkv_in, wq_in, wo_in, wm_in, wmo_in, cot_in,
    enc_out, mesh_out, gg_out, gkv_out,
    nodes, wide, mf, cf, wkv_own, wkv_oth, wq, wo, wm, wmo, qd, qdt, xs, ut, zy, srow,
    sd, sd_send, sd_recv, pb, att_own, att_send, att_recv, enc_own, enc_send, enc_recv, ef, mkv, mq,
    mo_own, mo_send, mo_recv, mo_val, gedge, halo_send, halo_recv, ggs,
    gb, pre, rs1, rsum, rs2, tt, tp, rec, bq, bp, blocks,
    lsem, osem, ssem, rsem, out_s,
):
    s = lax.axis_index("space")
    g = lax.axis_index("head")
    o = 1 - g
    core = s % 2
    chip = s // 2
    sib = s + 1 - 2 * core
    up = (s + 1) % SPACE
    down = (s + SPACE - 1) % SPACE

    def flip(bit):
        return s + bit - 2 * bit * ((s // bit) % 2)

    ylo = (s // 8) % 2
    across = flip(8)
    at_x, at_z = chip // 8, chip % 4

    def along(axis, d):
        return (s + 16 * d) % SPACE if axis == 0 else s - 2 * at_z + 2 * ((at_z + d) % 4)

    far = s - 1 + 2 * core
    far = (far + SPACE) % SPACE

    def remote(src_ref, dst_ref, n, dev):
        return pltpu.make_async_remote_copy(
            src_ref=src_ref, dst_ref=dst_ref, send_sem=ssem.at[n], recv_sem=rsem.at[n],
            device_id=dev, device_id_type=MESH,
        )

    partner = (s, o)
    mine = pl.ds(pl.multiple_of(g * F, F), F)
    other = pl.ds(pl.multiple_of(o * F, F), F)

    local = [
        (mesh_in, mf.at[0]),
        (cot_in, cf.at[0]),
        (wq_in.at[mine, :], wq.at[0]),
        (wo_in.at[:, mine], wo.at[0]),
        (wq_in.at[other, :], wq.at[1]),
        (wo_in.at[:, other], wo.at[1]),
        (wkv_in.at[:, mine, :], wkv_own),
        (grid_in, wide.at[pl.ds(RIM, G), :]),
        (wm_in.at[:, mine, :], wm.at[0]),
        (wm_in.at[:, other, :], wm.at[1]),
        (wmo_in.at[:, mine], wmo.at[0]),
        (wmo_in.at[:, other], wmo.at[1]),
    ]
    loads = [pltpu.make_async_copy(a, b, lsem.at[i]) for i, (a, b) in enumerate(local)]
    for c in loads:
        c.start()

    first = [partner, (across, o), (across, g), (sib, g), (far, g)]
    first += [(along(axis, d) + y * (across - s), g) for axis in range(2) for d in (1, 2, 3) for y in range(2)]
    barrier = pltpu.get_barrier_semaphore()
    for dev in first:
        pl.semaphore_signal(barrier, inc=1, device_id=dev, device_id_type=MESH)
    pl.semaphore_wait(barrier, len(first))

    e1m = remote(mesh_in, mf.at[1], E1M, partner)
    e1c = remote(cot_in, cf.at[1], E1C, partner)
    hup = remote(grid_in.at[pl.ds(G - RIM, RIM), :], wide.at[pl.ds(0, RIM), :], HUP, (up, g))
    hdown = remote(grid_in.at[pl.ds(0, RIM), :], wide.at[pl.ds(RIM + G, RIM), :], HDOWN, (down, g))

    def piece(k, axis, q):
        return wkv_oth.at[k, pl.ds(pl.multiple_of(axis * 256 + q * 64, 64), 64), :]

    at = (at_x, at_z)
    wy, wring, wfwd, wback = [], [], [], []
    for axis in range(2):
        rows = pl.ds(pl.multiple_of(o * F + axis * 256 + at[axis] * 64, 64), 64)
        here = piece(core, axis, at[axis])
        wy.append(remote(wkv_in.at[core, rows, :], here, WY + axis, (across, o)))
        for d in range(4):
            q = (at[axis] + 4 - d) % 4
            if d:
                n = WR + 3 * axis + d - 1
                wring.append((
                    remote(here, here, n, (along(axis, d), g)),
                    remote(piece(core, axis, q), piece(core, axis, q), n, partner),
                ))
            n = WF + 4 * axis + d
            wfwd.append(remote(piece(core, axis, q), piece(core, axis, q), n, (sib, g)))
            wback.append(remote(piece(1 - core, axis, q), piece(1 - core, axis, q), n, (sib, g)))
    for c in wy:
        c.start()
    hup.start()
    hdown.start()
    e1m.start()
    e1c.start()

    base = s * G - RIM
    source = src[...].astype(F32).T.astype(I32)
    nodes[...] = source
    rel = source - base
    rel = jnp.where((rel >= 0) & (rel < WIDE), rel, 4095)
    hi = (rel // 64).astype(F32).astype(BF)
    lo = (rel % 64).astype(F32).astype(BF)
    spread = jnp.where(iota((K, 256), 0) == (iota((K, 256), 1) & 15), 1.0, 0.0).astype(BF)
    flat = dot(hi, spread) * 64.0 + dot(lo, spread)
    flat = jnp.where((iota((M, 256), 0) & 15) == iota((M, 256), 1) // 16, flat, 0.0)
    for t in range(8):
        srow[0:1, t * 256 : (t + 1) * 256] = jnp.sum(
            flat[t * 16 : (t + 1) * 16], axis=0, keepdims=True
        )

    for c in wy:
        c.wait_recv()
    for c, _ in wring:
        c.start()
    wfwd[0].start()
    wfwd[4].start()

    loads[7].wait()
    hup.wait_recv()
    hdown.wait_recv()

    def gather(t, carry):
        n = pl.multiple_of(t * 32, 32)
        part = (nodes[pl.ds(n, 32), :] - base).astype(F32)
        part = jnp.broadcast_to(part[:, None, :], (32, K, K)).reshape(512, K)
        pick = (iota((512, K), 0) & 15) == iota((512, K), 1)
        col = jnp.sum(jnp.where(pick, part, 0.0), axis=1, keepdims=True).astype(I32)
        hot = jnp.where(iota((512, WIDE), 1) == col, 1.0, 0.0).astype(BF)
        xs[pl.ds(pl.multiple_of(t * 512, 512), 512), :] = dot(hot, wide[...]).astype(BF)
        return carry

    lax.fori_loop(0, 2, gather, 0)

    for n in (0, 1, 2, 3):
        loads[n].wait()
    loads[4].wait()
    loads[5].wait()
    qa = dot(mf[0], wq[0])
    e1m.wait_recv()
    qd[0, 0] = (qa + dot(mf[1], wq[1])).astype(BF)
    e2 = remote(qd.at[0, 0], qd.at[1, 0], E2, partner)
    e2.start()
    da = dot_t(cf[0], wo[0])
    e1c.wait_recv()
    qd[0, 1] = (da + dot_t(cf[1], wo[1])).astype(BF)
    e2d = remote(qd.at[0, 1], qd.at[1, 1], E2D, partner)
    e2d.start()
    for n, (_, c) in enumerate(wring):
        c.wait_recv()
        wfwd[n + 1 + n // 3].start()

    lax.fori_loop(2, 4, gather, 0)

    def turn(side):
        for k in range(2):
            qdt[side, k] = qd[side, k].astype(F32).T.astype(BF)

    turn(0)

    def expand(side, weights):
        for k in range(2):
            for a in range(2):
                x4 = qd[side, k, :, a * 256 : (a + 1) * 256].astype(F32)
                head = iota((M, 256), 1) // 64
                lhs = jnp.concatenate(
                    [jnp.where(head == i, x4, 0.0).astype(BF) for i in range(4)], axis=0
                )
                out = dot_t(lhs, weights[k, :, a * 256 : (a + 1) * 256]).astype(BF)
                n = side * HL + a * 4
                ut[k, n : n + 4] = out.reshape(4, M, F)

    loads[6].wait()
    expand(0, wkv_own)


    def scores(side):
        def step(t, carry):
            xg = xs[pl.ds(pl.multiple_of(t * 256, 256), 256), :]
            lane = iota((K, 256), 1) & 15
            ug = ut[:, side * HL : side * HL + HL, pl.ds(pl.multiple_of(t * 16, 16), 16), :]
            full = dot_t(xg, ug.reshape(256, F)).reshape(16, K, 256)
            total = jnp.where(lane == 0, full[0], 0.0)
            for m in range(1, 16):
                total = total + jnp.where(lane == m, full[m], 0.0)
            sd[side, t] = total
            sd_send[side, t] = total.astype(BF)
            return carry

        lax.fori_loop(0, 8, step, 0, unroll=2)

    e3a = remote(sd_send.at[0], sd_recv.at[1], E3A, partner)
    e3b = remote(sd_send.at[1], sd_recv.at[0], E3B, partner)
    scores(0)
    e3a.start()
    e2.wait_recv()
    e2d.wait_recv()
    turn(1)
    for c in wback:
        c.wait_recv()
    expand(1, wkv_oth)

    scores(1)
    e3b.start()

    dg = deg[...].astype(F32)
    dg = jnp.where(iota((8, M), 1) // 16 == iota((8, M), 0), dg, 0.0).astype(BF)
    tile = jnp.where((iota((M, 128), 0) & 15) == (iota((M, 128), 1) & 15), 1.0, 0.0).astype(BF)
    dlane = dot(dg, tile)
    live = iota((8, K, 128), 1).astype(F32) < dlane[:, None, :]

    for side in (1, 0):
        (e3a if side else e3b).wait_recv()
        raw = (sd[side, :, :, :128] + sd_recv[side, :, :, :128].astype(F32)) * SCALE
        dp = sd[side, :, :, 128:] + sd_recv[side, :, :, 128:].astype(F32)
        th = jnp.tanh(raw * (1.0 / CAP))
        wgt = jnp.where(live, jnp.exp(CAP * th), 0.0)
        prob = wgt / jnp.sum(wgt, axis=1, keepdims=True)
        ds = prob * (dp - jnp.sum(prob * dp, axis=1, keepdims=True))
        dr = ds * (1.0 - th * th) * SCALE
        a = side * 128
        pb[:, :, a : a + 128] = dr.astype(BF)
        pb[:, :, 256 + a : 256 + a + 128] = prob.astype(BF)

    def sums(t, carry):
        xg = xs[pl.ds(pl.multiple_of(t * 256, 256), 256), :]
        same = (iota((512, 256), 0) & 15) == iota((512, 256), 1) // 16
        sel = jnp.where(iota((K, 256), 0) == (iota((K, 256), 1) & 15), 1.0, 0.0).astype(BF)
        pt = jnp.where(same, dot_first(pb[t], sel), 0.0).astype(BF)
        out = dot(pt, xg).astype(BF)
        zy[:, :, pl.ds(pl.multiple_of(t * 16, 16), 16), :] = out.reshape(2, 16, 16, F)
        return carry

    lax.fori_loop(0, 8, sums, 0, unroll=2)

    def diagonal(x):
        x = x.reshape(4, M, 256)
        head = iota((M, 256), 1) // 64
        out = jnp.zeros((M, 256), F32)
        for i in range(4):
            out = out + jnp.where(head == i, x[i], 0.0)
        return out

    def weight_terms(n, carry):
        k = (1 - core) + n * (2 * core - 1)
        for side in range(2):
            for p in range(4):
                xt = qdt[side, k, p * 128 : (p + 1) * 128, :].astype(F32)
                first = iota((128, M), 0) < 64
                lhs = jnp.concatenate(
                    [jnp.where(first, xt, 0.0).astype(BF), jnp.where(first, 0.0, xt).astype(BF)], axis=1
                )
                h = side * HL + 2 * p
                rhs = zy[k, h : h + 2].reshape(2 * M, F)
                out = dot(lhs, rhs).astype(BF)
                for f in range(4):
                    x, y = 2 * side + p // 2, p % 2
                    gb[k, 0, f, 2 * x + y] = out[:64, f * 128 : (f + 1) * 128]
                    gb[k, 1, x, 2 * f + y] = out[64:, f * 128 : (f + 1) * 128]
        return carry

    line = (at_z, at_x)
    axis_of = (1, 0)

    def ring(h, stage, d):
        return (along(axis_of[h] if stage == 1 else 1 - axis_of[h], d), g)

    def ahead(n, d):
        return (n + d) % 4

    weight_terms(0, 0)
    presum = [
        remote(gb.at[1 - core, h, ahead(line[h], d)], pre.at[h, ahead(line[h], d)], PRE + 4 * h + d, (sib, g))
        for h in range(2)
        for d in range(4)
    ]
    order = [0, 1, 2, 4, 5, 6, 3, 7]
    order = [(n // 4, (n % 4 + 1) % 4) for n in order]
    for h, d in order:
        presum[4 * h + d].start()
    for a in range(2):
        z4 = zy[1, HL + a * 4 : HL + a * 4 + 4].reshape(4 * M, F)
        att_send[:, a * 256 : (a + 1) * 256] = diagonal(
            dot(z4, wkv_oth[1, :, a * 256 : (a + 1) * 256])
        ).astype(BF)
    e4 = remote(att_send, att_recv, E4, partner)
    e4.start()
    weight_terms(1, 0)
    for a in range(2):
        z4 = zy[1, a * 4 : a * 4 + 4].reshape(4 * M, F)
        att_own[:, a * 256 : (a + 1) * 256] = diagonal(
            dot(z4, wkv_own[1, :, a * 256 : (a + 1) * 256])
        )


    stage1 = [
        remote(gb.at[core, h, ahead(line[h], d)], rs1.at[h, d - 1], RS1 + 3 * h + d - 1, ring(h, 1, d))
        for h in range(2)
        for d in (1, 2, 3)
    ]
    for h, d in order:
        presum[4 * h + d].wait_recv()
        n = ahead(line[h], d)
        gb[core, h, n] = (gb[core, h, n].astype(F32) + pre[h, n].astype(F32)).astype(BF)
        if d:
            stage1[3 * h + d - 1].start()

    e4.wait_recv()
    att = (att_own[...] + att_recv[...].astype(F32)).astype(BF)
    enc_send[...] = dot(att, wo[1]).astype(BF)
    e5 = remote(enc_send, enc_recv, E5, partner)
    e5.start()
    enc_own[...] = dot(att, wo[0])

    def edge_grads(t, carry):
        rows = pl.ds(pl.multiple_of(t * 16, 16), 16)
        match = (iota((16, K, 512), 2) & 15) == iota((16, K, 512), 0)
        p = jnp.broadcast_to(pb[t].astype(F32)[None], (16, K, 512))
        p = jnp.where(match, p, 0.0).astype(BF).reshape(256, 512)
        total = dot(p, ut[:, :, rows, :].reshape(512, F))
        gedge[pl.ds(pl.multiple_of(t * 256, 256), 256), :] = total.astype(BF)
        return carry

    lax.fori_loop(0, 8, edge_grads, 0, unroll=2)

    def rows_of(first, count):
        hot = jnp.where(
            (iota((count, G), 0) + first).astype(F32) == srow[0:1, :], 1.0, 0.0
        ).astype(BF)
        return dot(hot, gedge[...])

    halo_send[0] = rows_of(0, RIM).astype(BF)
    halo_send[1] = rows_of(RIM + G, RIM).astype(BF)
    gdown = remote(halo_send.at[0], halo_recv.at[1], GDOWN, (down, g))
    gup = remote(halo_send.at[1], halo_recv.at[0], GUP, (up, g))
    gdown.start()
    gup.start()

    e5.wait_recv()
    enc = (mf[0].astype(F32) + enc_own[...] + enc_recv[...].astype(F32)).astype(BF)
    ef[0] = enc
    e6 = remote(ef.at[0], ef.at[1], E6, partner)
    e6.start()
    enc_copy = pltpu.make_async_copy(ef.at[0], enc_out, osem.at[0])
    enc_copy.start()

    stage2 = [
        remote(
            rsum.at[h, pl.ds(2 * ahead(line[1 - h], d), 2)], rs2.at[h, d - 1], RS2 + 3 * h + d - 1, ring(h, 2, d)
        )
        for h in range(2)
        for d in (1, 2, 3)
    ]
    for h in range(2):
        for d in range(3):
            stage1[3 * h + d].wait_recv()
        total = gb[core, h, line[h]].astype(F32)
        for d in range(3):
            total = total + rs1[h, d].astype(F32)
        rsum[h] = total.astype(BF)
        for c in stage2[3 * h : 3 * h + 3]:
            c.start()

    def interior(t, carry):
        n = pl.multiple_of(t * 512, 512)
        ggs[pl.ds(n, 512), :] = rows_of(n + RIM, 512).astype(BF)
        return carry

    lax.fori_loop(0, 2, interior, 0)

    late = at_x // 2
    for h in range(2):
        for d in range(3):
            stage2[3 * h + d].wait_recv()
        total = rsum[h, pl.ds(2 * line[1 - h], 2)].astype(F32)
        for d in range(3):
            total = total + rs2[h, d].astype(F32)
        for y in range(2):
            tt[y, h] = total[y].astype(BF)
    stage3 = remote(tt.at[1 - ylo], rec, RS3, (across, g + late * (1 - 2 * g)))
    stage3p = remote(tt.at[ylo], tp, RS3P, partner)
    stage3.start()

    @pl.when(late == 1)
    def _():
        stage3p.start()

    loads[8].wait()
    loads[9].wait()
    e6.wait_recv()
    for k in range(2):
        mkv[k, R : R + M, :] = (dot(ef[0], wm[0, 1 + k]) + dot(ef[1], wm[1, 1 + k])).astype(BF)
    kup = remote(mkv.at[:, pl.ds(M, R), :], mkv.at[:, pl.ds(0, R), :], KUP, (up, g))
    kdown = remote(mkv.at[:, pl.ds(R, R), :], mkv.at[:, pl.ds(R + M, R), :], KDOWN, (down, g))
    kup.start()
    kdown.start()
    mq[...] = (dot(ef[0], wm[0, 0]) + dot(ef[1], wm[1, 0])).astype(BF)

    stage3.wait_recv()

    @pl.when(late == 0)
    def _():
        tp[...] = tt[ylo]

    @pl.when(late == 1)
    def _():
        stage3p.wait()

    block = (tp[...].astype(F32) + rec[...].astype(F32)).reshape(128, 128).T.astype(BF)

    bq[0] = block[:64]
    bq[1] = block[64:]
    back2, back2_in, back3, back3_in = [], [], [], []
    for h in range(2):
        for d in range(4):
            to, of = ring(h, 2, d)[0], ahead(line[1 - h], 4 - d)
            for y in range(2):
                if d or y:
                    n = AG2 + 7 * h + 2 * d + y - 1
                    back2.append(remote(bq.at[h], bp.at[h, line[1 - h], ylo], n, (to + y * (across - s), g)))
                    came = bp.at[h, of, ylo + y * (1 - 2 * ylo)]
                    back2_in.append(remote(bq.at[h], came, n, partner))
        for d in (1, 2, 3):
            n = AG3 + 3 * h + d - 1
            back3.append(remote(bp.at[h], blocks.at[core, h, line[h]], n, ring(h, 1, d)))
            back3_in.append(remote(bp.at[h], blocks.at[core, h, ahead(line[h], 4 - d)], n, partner))
    for c in back2:
        c.start()
    for h in range(2):
        bp[h, line[1 - h], ylo] = bq[h]
    lax.fori_loop(2, 3, interior, 0)

    where_n = iota((M, 256), 1) - R
    delta = where_n - iota((M, 256), 0)
    allowed = delta == off[0]
    for j in range(1, W):
        allowed = allowed | (delta == off[j])
    where_g = where_n + s * M
    allowed = allowed & (where_g >= 0) & (where_g < M * SPACE)
    allow = jnp.where(allowed[:, : M + 2 * R], 1.0, 0.0)
    allow4 = jnp.concatenate([allow] * 4, axis=0)
    kup.wait_recv()
    kdown.wait_recv()
    matts = []
    for a in range(2):
        cols = slice(a * 256, (a + 1) * 256)
        x4 = mq[:, cols].astype(F32)
        head = iota((M, 256), 1) // 64
        lhs = jnp.concatenate([jnp.where(head == i, x4, 0.0).astype(BF) for i in range(4)], axis=0)
        raw = dot_t(lhs, mkv[0, :, cols]) * SCALE
        wgt = jnp.exp(CAP * jnp.tanh(raw * (1.0 / CAP))) * allow4
        prob = (wgt / jnp.sum(wgt, axis=1, keepdims=True)).astype(BF)
        matts.append(diagonal(dot(prob, mkv[1, :, cols])).astype(BF))
    matt = jnp.concatenate(matts, axis=1)
    loads[10].wait()
    loads[11].wait()
    mo_send[...] = dot(matt, wmo[1]).astype(BF)
    e8 = remote(mo_send, mo_recv, E8, partner)
    e8.start()
    mo_own[...] = dot(matt, wmo[0])

    for h in range(2):
        for c in back2_in[7 * h : 7 * h + 7]:
            c.wait_recv()
        for c in back3[3 * h : 3 * h + 3]:
            c.start()
        blocks[core, h, line[h]] = bp[h]

    def pass_copy(k, h, d):
        part = blocks.at[k, h, ahead(line[h], 4 - d)]
        return remote(part, part, AGF + 4 * h + d, (sib, g))

    def result_copy(k, h, d):
        n = ahead(line[h], 4 - d)
        return pltpu.make_async_copy(blocks.at[k, h, n], gkv_out.at[k, h, n], out_s.at[k, 4 * h + d])

    passed = [pass_copy(core, h, d) for h in range(2) for d in range(4)]
    handed = [pass_copy(1 - core, h, d) for h in range(2) for d in range(4)]
    mine_out = [result_copy(core, h, d) for h in range(2) for d in range(4)]
    other_out = [result_copy(1 - core, h, d) for h in range(2) for d in range(4)]
    for n in (0, 4):
        passed[n].start()
        mine_out[n].start()

    lax.fori_loop(3, 4, interior, 0)
    gdown.wait_recv()
    gup.wait_recv()
    ggs[0:RIM, :] = (ggs[0:RIM, :].astype(F32) + halo_recv[0].astype(F32)).astype(BF)
    ggs[G - RIM : G, :] = (ggs[G - RIM : G, :].astype(F32) + halo_recv[1].astype(F32)).astype(BF)
    gg_copy = pltpu.make_async_copy(ggs, gg_out, osem.at[2])
    gg_copy.start()

    singles = [e1m, e1c, hup, hdown, e2, e2d, e3a, e3b, e4, e5, e6, kup, kdown, gdown, gup, stage3]
    for c in singles + wy + [c for c, _ in wring] + wfwd + presum + stage1 + stage2 + back2:
        c.wait_send()
    e8.wait()
    mo_val[...] = (ef[0].astype(F32) + mo_own[...] + mo_recv[...].astype(F32)).astype(BF)
    mo_copy = pltpu.make_async_copy(mo_val, mesh_out, osem.at[3])
    mo_copy.start()

    for d in (1, 2, 3):
        for h in range(2):
            back3_in[3 * h + d - 1].wait_recv()
            passed[4 * h + d].start()
            mine_out[4 * h + d].start()
    for c in back3:
        c.wait_send()
    for d in range(4):
        for h in range(2):
            handed[4 * h + d].wait_recv()
            other_out[4 * h + d].start()
    for c in passed:
        c.wait_send()
    enc_copy.wait()
    gg_copy.wait()
    mo_copy.wait()
    for c in mine_out + other_out:
        c.wait()


def write_results(enc, mesh_o, gg, gkv, enc_out, mesh_out, gg_out, gkv_out, e, m, r, low, wide, s_in, s_out, k_in, k_out):
    plain = ((enc, e, enc_out), (mesh_o, m, mesh_out), (gg, r, gg_out))
    g = lax.axis_index("head")
    loads = [pltpu.make_async_copy(gkv.at[k], low.at[k], k_in.at[k]) for k in range(2)]
    others = [pltpu.make_async_copy(a, b, s_in.at[n]) for n, (a, b, _) in enumerate(plain)]
    for c in loads + others:
        c.start()
    stores = []
    for k in range(2):
        loads[k].wait()
        for n in range(2):
            half = g if n == 0 else 1 - g
            for x in (2 * n, 2 * n + 1):
                for z in range(4):
                    for y in range(2):
                        col = (x % 2 * 2 + y) * 128
                        for h in range(2):
                            rows = pl.ds(pl.multiple_of(half * F + z * 128 + h * 64, 64), 64)
                            part = low[k, 0, z, x, y] if h == 0 else low[k, 1, x, z, y]
                            wide[k, rows, col : col + 128] = part.astype(F32)
            rows = pl.ds(pl.multiple_of(half * F, F), F)
            stores.append(pltpu.make_async_copy(wide.at[k, rows], gkv_out.at[k, rows], k_out.at[2 * k + n]))
            stores[-1].start()
    for n, (_, b, c) in enumerate(plain):
        others[n].wait()
        stores.append(pltpu.make_async_copy(b, c, s_out.at[n]))
        stores[-1].start()
    for c in stores:
        c.wait()


def shards(
    grid_feat, mesh_feat, edge_src, degree, offsets, w_kv, w_query, w_out, w_mesh, w_mesh_out, cotangent
):
    hbm = pl.BlockSpec(memory_space=pl.ANY)
    vmem = pl.BlockSpec(memory_space=pltpu.VMEM)
    smem = pl.BlockSpec(memory_space=pltpu.SMEM)

    def v(*shape, dtype=BF):
        return pltpu.VMEM(shape, dtype)

    dma = pltpu.SemaphoreType.DMA
    scratch = dict(
        nodes=v(M, K, dtype=I32), wide=v(WIDE, F), mf=v(2, M, F), cf=v(2, M, F), wkv_own=v(2, F, F), wkv_oth=v(2, F, F),
        wq=v(2, F, F), wo=v(2, F, F), wm=v(2, 3, F, F), wmo=v(2, F, F),
        qd=v(2, 2, M, F), qdt=v(2, 2, F, M), xs=v(G, F), ut=v(2, 16, M, F), zy=v(2, 16, M, F),
        srow=v(8, G, dtype=F32),
        sd=v(2, 8, K, 256, dtype=F32), sd_send=v(2, 8, K, 256), sd_recv=v(2, 8, K, 256), pb=v(8, K, 512),
        att_own=v(M, F, dtype=F32), att_send=v(M, F), att_recv=v(M, F),
        enc_own=v(M, F, dtype=F32), enc_send=v(M, F), enc_recv=v(M, F), ef=v(2, M, F),
        mkv=v(2, M + 2 * R, F), mq=v(M, F),
        mo_own=v(M, F, dtype=F32), mo_send=v(M, F), mo_recv=v(M, F), mo_val=v(M, F),
        gedge=v(G, F), halo_send=v(2, RIM, F), halo_recv=v(2, RIM, F), ggs=v(G, F),
        gb=v(2, 2, 4, 8, 64, 128), pre=v(2, 4, 8, 64, 128), rs1=v(2, 3, 8, 64, 128), rsum=v(2, 8, 64, 128),
        rs2=v(2, 3, 2, 64, 128), tt=v(2, 2, 64, 128), tp=v(2, 64, 128), rec=v(2, 64, 128),
        bq=v(2, 64, 128), bp=v(2, 4, 2, 64, 128), blocks=v(2, 2, 4, 4, 2, 64, 128),
        lsem=dma((12,)), osem=dma((4,)), ssem=dma((N_REMOTE,)), rsem=dma((N_REMOTE,)),
        out_s=dma((2, 8)),
    )
    enc, mesh_out, grad_grid, grad_kv = pl.pallas_call(
        body,
        out_shape=(
            jax.ShapeDtypeStruct((M, F), BF),
            jax.ShapeDtypeStruct((M, F), BF),
            jax.ShapeDtypeStruct((G, F), BF),
            jax.ShapeDtypeStruct((2, 2, 4, 4, 2, 64, 128), BF),
        ),
        in_specs=[hbm, hbm, vmem, vmem, smem, hbm, hbm, hbm, hbm, hbm, hbm],
        out_specs=(hbm, hbm, hbm, hbm),
        scratch_shapes=list(scratch.values()),
        compiler_params=pltpu.CompilerParams(
            collective_id=0, has_side_effects=True, vmem_limit_bytes=58 * 2**20
        ),
        name="encoder",
    )(
        grid_feat, mesh_feat, edge_src.T, degree.reshape(1, M), offsets, w_kv, w_query, w_out, w_mesh,
        w_mesh_out, cotangent,
    )
    dma = pltpu.SemaphoreType.DMA
    return pl.pallas_call(
        write_results,
        out_shape=(
            jax.ShapeDtypeStruct((M, F), BF),
            jax.ShapeDtypeStruct((M, F), BF),
            jax.ShapeDtypeStruct((G, F), BF),
            jax.ShapeDtypeStruct((2, 2 * F, F), F32),
        ),
        in_specs=[hbm] * 4,
        out_specs=(hbm,) * 4,
        scratch_shapes=[
            v(M, F), v(M, F), v(G, F), v(2, 2, 4, 4, 2, 64, 128), v(2, 2 * F, F, dtype=F32),
            dma((3,)), dma((3,)), dma((2,)), dma((4,)),
        ],
        compiler_params=pltpu.CompilerParams(vmem_limit_bytes=58 * 2**20),
        name="results",
    )(enc, mesh_out, grad_grid, grad_kv)


def solution(mesh):
    in_specs = (
        P("space", "head"),
        P("space", "head"),
        P("space", None),
        P("space"),
        P(),
        P(None, None, "head"),
        P(None, "head"),
        P("head", None),
        P(None, None, "head"),
        P("head", None),
        P("space", "head"),
    )
    out_specs = (P("space", "head"), P("space", "head"), P("space", "head"), P(None, None, "head"))
    return jax.shard_map(shards, mesh=mesh, in_specs=in_specs, out_specs=out_specs, check_vma=False)
```

```python
import functools

import jax
import jax.numpy as jnp
from jax import lax
from jax.experimental import pallas as pl
from jax.experimental.pallas import tpu as pltpu
from jax.sharding import PartitionSpec as P

BF = jnp.bfloat16
F32 = jnp.float32
I32 = jnp.int32
MESH = pl.DeviceIdType.MESH

M = 128
K = 16
G = 2048
RIM = 128
WIDE = G + 2 * RIM
R = 32
W = 16
F = 512
HL = 8
SPACE = 64
CHIPS = SPACE // 2
CAP = 3.0
SCALE = 0.125

(
    E1M, E1C, HUP, HDOWN, E2, E3A, E3B, E4, E5, E6, KUP, KDOWN, E8, GUP, GDOWN,
    RS3, RS3P, E2D, WY, WR, WF, PRE, RS1, RS2, AG2, AG3, AGF,
) = list(range(19)) + [20, 26, 34, 42, 48, 54, 68, 74]
N_REMOTE = 82


def dot(a, b):
    return jnp.dot(a, b, preferred_element_type=F32)


def dot_t(a, b):
    return lax.dot_general(a, b, (((1,), (1,)), ((), ())), preferred_element_type=F32)


def dot_first(a, b):
    return lax.dot_general(a, b, (((0,), (0,)), ((), ())), preferred_element_type=F32)


def iota(shape, dim):
    return lax.broadcasted_iota(I32, shape, dim)


def body(
    grid_in, mesh_in, src, deg, off, wkv_in, wq_in, wo_in, wm_in, wmo_in, cot_in,
    enc_out, mesh_out, gg_out, gkv_out,
    nodes, wide, mf, cf, wkv_own, wkv_oth, wq, wo, wm, wmo, qd, qdt, xs, ut, zy, srow,
    sd, sd_send, sd_recv, pb, att_own, att_send, att_recv, enc_own, enc_send, enc_recv, ef, mkv, mq,
    mo_own, mo_send, mo_recv, mo_val, gedge, halo_send, halo_recv, ggs,
    gb, pre, rs1, rsum, rs2, tt, tp, rec, bq, bp, blocks,
    lsem, osem, ssem, rsem, out_s,
):
    s = lax.axis_index("space")
    g = lax.axis_index("head")
    o = 1 - g
    core = s % 2
    chip = s // 2
    sib = s + 1 - 2 * core
    up = (s + 1) % SPACE
    down = (s + SPACE - 1) % SPACE

    def flip(bit):
        return s + bit - 2 * bit * ((s // bit) % 2)

    ylo = (s // 8) % 2
    across = flip(8)
    at_x, at_z = chip // 8, chip % 4

    def along(axis, d):
        return (s + 16 * d) % SPACE if axis == 0 else s - 2 * at_z + 2 * ((at_z + d) % 4)

    far = s - 1 + 2 * core
    far = (far + SPACE) % SPACE

    def remote(src_ref, dst_ref, n, dev):
        return pltpu.make_async_remote_copy(
            src_ref=src_ref, dst_ref=dst_ref, send_sem=ssem.at[n], recv_sem=rsem.at[n],
            device_id=dev, device_id_type=MESH,
        )

    partner = (s, o)
    mine = pl.ds(pl.multiple_of(g * F, F), F)
    other = pl.ds(pl.multiple_of(o * F, F), F)

    local = [
        (mesh_in, mf.at[0]),
        (cot_in, cf.at[0]),
        (wq_in.at[mine, :], wq.at[0]),
        (wo_in.at[:, mine], wo.at[0]),
        (wq_in.at[other, :], wq.at[1]),
        (wo_in.at[:, other], wo.at[1]),
        (wkv_in.at[:, mine, :], wkv_own),
        (grid_in, wide.at[pl.ds(RIM, G), :]),
        (wm_in.at[:, mine, :], wm.at[0]),
        (wm_in.at[:, other, :], wm.at[1]),
        (wmo_in.at[:, mine], wmo.at[0]),
        (wmo_in.at[:, other], wmo.at[1]),
    ]
    loads = [pltpu.make_async_copy(a, b, lsem.at[i]) for i, (a, b) in enumerate(local)]
    for c in loads:
        c.start()

    first = [partner, (across, o), (across, g), (sib, g), (far, g)]
    first += [(along(axis, d) + y * (across - s), g) for axis in range(2) for d in (1, 2, 3) for y in range(2)]
    barrier = pltpu.get_barrier_semaphore()
    for dev in first:
        pl.semaphore_signal(barrier, inc=1, device_id=dev, device_id_type=MESH)
    pl.semaphore_wait(barrier, len(first))

    e1m = remote(mesh_in, mf.at[1], E1M, partner)
    e1c = remote(cot_in, cf.at[1], E1C, partner)
    hup = remote(grid_in.at[pl.ds(G - RIM, RIM), :], wide.at[pl.ds(0, RIM), :], HUP, (up, g))
    hdown = remote(grid_in.at[pl.ds(0, RIM), :], wide.at[pl.ds(RIM + G, RIM), :], HDOWN, (down, g))

    def piece(k, axis, q):
        return wkv_oth.at[k, pl.ds(pl.multiple_of(axis * 256 + q * 64, 64), 64), :]

    at = (at_x, at_z)
    wy, wring, wfwd, wback = [], [], [], []
    for axis in range(2):
        rows = pl.ds(pl.multiple_of(o * F + axis * 256 + at[axis] * 64, 64), 64)
        here = piece(core, axis, at[axis])
        wy.append(remote(wkv_in.at[core, rows, :], here, WY + axis, (across, o)))
        for d in range(4):
            q = (at[axis] + 4 - d) % 4
            if d:
                n = WR + 3 * axis + d - 1
                wring.append((
                    remote(here, here, n, (along(axis, d), g)),
                    remote(piece(core, axis, q), piece(core, axis, q), n, partner),
                ))
            n = WF + 4 * axis + d
            wfwd.append(remote(piece(core, axis, q), piece(core, axis, q), n, (sib, g)))
            wback.append(remote(piece(1 - core, axis, q), piece(1 - core, axis, q), n, (sib, g)))
    for c in wy:
        c.start()
    hup.start()
    hdown.start()
    e1m.start()
    e1c.start()

    base = s * G - RIM
    source = src[...].astype(F32).T.astype(I32)
    nodes[...] = source
    rel = source - base
    rel = jnp.where((rel >= 0) & (rel < WIDE), rel, 4095)
    hi = (rel // 64).astype(F32).astype(BF)
    lo = (rel % 64).astype(F32).astype(BF)
    spread = jnp.where(iota((K, 256), 0) == (iota((K, 256), 1) & 15), 1.0, 0.0).astype(BF)
    flat = dot(hi, spread) * 64.0 + dot(lo, spread)
    flat = jnp.where((iota((M, 256), 0) & 15) == iota((M, 256), 1) // 16, flat, 0.0)
    for t in range(8):
        srow[0:1, t * 256 : (t + 1) * 256] = jnp.sum(
            flat[t * 16 : (t + 1) * 16], axis=0, keepdims=True
        )

    for c in wy:
        c.wait_recv()
    for c, _ in wring:
        c.start()
    wfwd[0].start()
    wfwd[4].start()

    loads[7].wait()
    hup.wait_recv()
    hdown.wait_recv()

    def gather(t, carry):
        n = pl.multiple_of(t * 32, 32)
        part = (nodes[pl.ds(n, 32), :] - base).astype(F32)
        part = jnp.broadcast_to(part[:, None, :], (32, K, K)).reshape(512, K)
        pick = (iota((512, K), 0) & 15) == iota((512, K), 1)
        col = jnp.sum(jnp.where(pick, part, 0.0), axis=1, keepdims=True).astype(I32)
        hot = jnp.where(iota((512, WIDE), 1) == col, 1.0, 0.0).astype(BF)
        xs[pl.ds(pl.multiple_of(t * 512, 512), 512), :] = dot(hot, wide[...]).astype(BF)
        return carry

    lax.fori_loop(0, 2, gather, 0)

    for n in (0, 1, 2, 3):
        loads[n].wait()
    loads[4].wait()
    loads[5].wait()
    qa = dot(mf[0], wq[0])
    e1m.wait_recv()
    qd[0, 0] = (qa + dot(mf[1], wq[1])).astype(BF)
    e2 = remote(qd.at[0, 0], qd.at[1, 0], E2, partner)
    e2.start()
    da = dot_t(cf[0], wo[0])
    e1c.wait_recv()
    qd[0, 1] = (da + dot_t(cf[1], wo[1])).astype(BF)
    e2d = remote(qd.at[0, 1], qd.at[1, 1], E2D, partner)
    e2d.start()
    for n, (_, c) in enumerate(wring):
        c.wait_recv()
        wfwd[n + 1 + n // 3].start()

    lax.fori_loop(2, 4, gather, 0)

    def turn(side):
        for k in range(2):
            qdt[side, k] = qd[side, k].astype(F32).T.astype(BF)

    turn(0)

    def expand(side, weights):
        for k in range(2):
            for a in range(2):
                x4 = qd[side, k, :, a * 256 : (a + 1) * 256].astype(F32)
                head = iota((M, 256), 1) // 64
                lhs = jnp.concatenate(
                    [jnp.where(head == i, x4, 0.0).astype(BF) for i in range(4)], axis=0
                )
                out = dot_t(lhs, weights[k, :, a * 256 : (a + 1) * 256]).astype(BF)
                n = side * HL + a * 4
                ut[k, n : n + 4] = out.reshape(4, M, F)

    loads[6].wait()
    expand(0, wkv_own)


    def scores(side):
        def step(t, carry):
            xg = xs[pl.ds(pl.multiple_of(t * 256, 256), 256), :]
            lane = iota((K, 256), 1) & 15
            ug = ut[:, side * HL : side * HL + HL, pl.ds(pl.multiple_of(t * 16, 16), 16), :]
            full = dot_t(xg, ug.reshape(256, F)).reshape(16, K, 256)
            total = jnp.where(lane == 0, full[0], 0.0)
            for m in range(1, 16):
                total = total + jnp.where(lane == m, full[m], 0.0)
            sd[side, t] = total
            sd_send[side, t] = total.astype(BF)
            return carry

        lax.fori_loop(0, 8, step, 0, unroll=4)

    e3a = remote(sd_send.at[0], sd_recv.at[1], E3A, partner)
    e3b = remote(sd_send.at[1], sd_recv.at[0], E3B, partner)
    scores(0)
    e3a.start()
    e2.wait_recv()
    e2d.wait_recv()
    turn(1)
    for c in wback:
        c.wait_recv()
    expand(1, wkv_oth)

    scores(1)
    e3b.start()

    dg = deg[...].astype(F32)
    dg = jnp.where(iota((8, M), 1) // 16 == iota((8, M), 0), dg, 0.0).astype(BF)
    tile = jnp.where((iota((M, 128), 0) & 15) == (iota((M, 128), 1) & 15), 1.0, 0.0).astype(BF)
    dlane = dot(dg, tile)
    live = iota((8, K, 128), 1).astype(F32) < dlane[:, None, :]

    for side in (1, 0):
        (e3a if side else e3b).wait_recv()
        raw = (sd[side, :, :, :128] + sd_recv[side, :, :, :128].astype(F32)) * SCALE
        dp = sd[side, :, :, 128:] + sd_recv[side, :, :, 128:].astype(F32)
        th = jnp.tanh(raw * (1.0 / CAP))
        wgt = jnp.where(live, jnp.exp(CAP * th), 0.0)
        prob = wgt / jnp.sum(wgt, axis=1, keepdims=True)
        ds = prob * (dp - jnp.sum(prob * dp, axis=1, keepdims=True))
        dr = ds * (1.0 - th * th) * SCALE
        a = side * 128
        pb[:, :, a : a + 128] = dr.astype(BF)
        pb[:, :, 256 + a : 256 + a + 128] = prob.astype(BF)

    def sums(t, carry):
        xg = xs[pl.ds(pl.multiple_of(t * 256, 256), 256), :]
        same = (iota((512, 256), 0) & 15) == iota((512, 256), 1) // 16
        sel = jnp.where(iota((K, 256), 0) == (iota((K, 256), 1) & 15), 1.0, 0.0).astype(BF)
        pt = jnp.where(same, dot_first(pb[t], sel), 0.0).astype(BF)
        out = dot(pt, xg).astype(BF)
        zy[:, :, pl.ds(pl.multiple_of(t * 16, 16), 16), :] = out.reshape(2, 16, 16, F)
        return carry

    lax.fori_loop(0, 8, sums, 0, unroll=4)

    def diagonal(x):
        x = x.reshape(4, M, 256)
        head = iota((M, 256), 1) // 64
        out = jnp.zeros((M, 256), F32)
        for i in range(4):
            out = out + jnp.where(head == i, x[i], 0.0)
        return out

    def weight_terms(n, carry):
        k = (1 - core) + n * (2 * core - 1)
        for side in range(2):
            for p in range(4):
                xt = qdt[side, k, p * 128 : (p + 1) * 128, :].astype(F32)
                first = iota((128, M), 0) < 64
                lhs = jnp.concatenate(
                    [jnp.where(first, xt, 0.0).astype(BF), jnp.where(first, 0.0, xt).astype(BF)], axis=1
                )
                h = side * HL + 2 * p
                rhs = zy[k, h : h + 2].reshape(2 * M, F)
                out = dot(lhs, rhs).astype(BF)
                for f in range(4):
                    x, y = 2 * side + p // 2, p % 2
                    gb[k, 0, f, 2 * x + y] = out[:64, f * 128 : (f + 1) * 128]
                    gb[k, 1, x, 2 * f + y] = out[64:, f * 128 : (f + 1) * 128]
        return carry

    line = (at_z, at_x)
    axis_of = (1, 0)

    def ring(h, stage, d):
        return (along(axis_of[h] if stage == 1 else 1 - axis_of[h], d), g)

    def ahead(n, d):
        return (n + d) % 4

    weight_terms(0, 0)
    presum = [
        remote(gb.at[1 - core, h, ahead(line[h], d)], pre.at[h, ahead(line[h], d)], PRE + 4 * h + d, (sib, g))
        for h in range(2)
        for d in range(4)
    ]
    order = [0, 1, 2, 4, 5, 6, 3, 7]
    order = [(n // 4, (n % 4 + 1) % 4) for n in order]
    for h, d in order:
        presum[4 * h + d].start()
    for a in range(2):
        z4 = zy[1, HL + a * 4 : HL + a * 4 + 4].reshape(4 * M, F)
        att_send[:, a * 256 : (a + 1) * 256] = diagonal(
            dot(z4, wkv_oth[1, :, a * 256 : (a + 1) * 256])
        ).astype(BF)
    e4 = remote(att_send, att_recv, E4, partner)
    e4.start()
    weight_terms(1, 0)
    for a in range(2):
        z4 = zy[1, a * 4 : a * 4 + 4].reshape(4 * M, F)
        att_own[:, a * 256 : (a + 1) * 256] = diagonal(
            dot(z4, wkv_own[1, :, a * 256 : (a + 1) * 256])
        )


    stage1 = [
        remote(gb.at[core, h, ahead(line[h], d)], rs1.at[h, d - 1], RS1 + 3 * h + d - 1, ring(h, 1, d))
        for h in range(2)
        for d in (1, 2, 3)
    ]
    for h, d in order:
        presum[4 * h + d].wait_recv()
        n = ahead(line[h], d)
        gb[core, h, n] = (gb[core, h, n].astype(F32) + pre[h, n].astype(F32)).astype(BF)
        if d:
            stage1[3 * h + d - 1].start()

    e4.wait_recv()
    att = (att_own[...] + att_recv[...].astype(F32)).astype(BF)
    enc_send[...] = dot(att, wo[1]).astype(BF)
    e5 = remote(enc_send, enc_recv, E5, partner)
    e5.start()
    enc_own[...] = dot(att, wo[0])

    def edge_grads(t, carry):
        rows = pl.ds(pl.multiple_of(t * 16, 16), 16)
        match = (iota((16, K, 512), 2) & 15) == iota((16, K, 512), 0)
        p = jnp.broadcast_to(pb[t].astype(F32)[None], (16, K, 512))
        p = jnp.where(match, p, 0.0).astype(BF).reshape(256, 512)
        total = dot(p, ut[:, :, rows, :].reshape(512, F))
        gedge[pl.ds(pl.multiple_of(t * 256, 256), 256), :] = total.astype(BF)
        return carry

    lax.fori_loop(0, 8, edge_grads, 0, unroll=2)

    def rows_of(first, count):
        hot = jnp.where(
            (iota((count, G), 0) + first).astype(F32) == srow[0:1, :], 1.0, 0.0
        ).astype(BF)
        return dot(hot, gedge[...])

    halo_send[0] = rows_of(0, RIM).astype(BF)
    halo_send[1] = rows_of(RIM + G, RIM).astype(BF)
    gdown = remote(halo_send.at[0], halo_recv.at[1], GDOWN, (down, g))
    gup = remote(halo_send.at[1], halo_recv.at[0], GUP, (up, g))
    gdown.start()
    gup.start()

    e5.wait_recv()
    enc = (mf[0].astype(F32) + enc_own[...] + enc_recv[...].astype(F32)).astype(BF)
    ef[0] = enc
    e6 = remote(ef.at[0], ef.at[1], E6, partner)
    e6.start()
    enc_copy = pltpu.make_async_copy(ef.at[0], enc_out, osem.at[0])
    enc_copy.start()

    stage2 = [
        remote(
            rsum.at[h, pl.ds(2 * ahead(line[1 - h], d), 2)], rs2.at[h, d - 1], RS2 + 3 * h + d - 1, ring(h, 2, d)
        )
        for h in range(2)
        for d in (1, 2, 3)
    ]
    for h in range(2):
        for d in range(3):
            stage1[3 * h + d].wait_recv()
        total = gb[core, h, line[h]].astype(F32)
        for d in range(3):
            total = total + rs1[h, d].astype(F32)
        rsum[h] = total.astype(BF)
        for c in stage2[3 * h : 3 * h + 3]:
            c.start()

    def interior(t, carry):
        n = pl.multiple_of(t * 512, 512)
        ggs[pl.ds(n, 512), :] = rows_of(n + RIM, 512).astype(BF)
        return carry

    lax.fori_loop(0, 2, interior, 0)

    late = at_x // 2
    for h in range(2):
        for d in range(3):
            stage2[3 * h + d].wait_recv()
        total = rsum[h, pl.ds(2 * line[1 - h], 2)].astype(F32)
        for d in range(3):
            total = total + rs2[h, d].astype(F32)
        for y in range(2):
            tt[y, h] = total[y].astype(BF)
    stage3 = remote(tt.at[1 - ylo], rec, RS3, (across, g + late * (1 - 2 * g)))
    stage3p = remote(tt.at[ylo], tp, RS3P, partner)
    stage3.start()

    @pl.when(late == 1)
    def _():
        stage3p.start()

    loads[8].wait()
    loads[9].wait()
    e6.wait_recv()
    for k in range(2):
        mkv[k, R : R + M, :] = (dot(ef[0], wm[0, 1 + k]) + dot(ef[1], wm[1, 1 + k])).astype(BF)
    kup = remote(mkv.at[:, pl.ds(M, R), :], mkv.at[:, pl.ds(0, R), :], KUP, (up, g))
    kdown = remote(mkv.at[:, pl.ds(R, R), :], mkv.at[:, pl.ds(R + M, R), :], KDOWN, (down, g))
    kup.start()
    kdown.start()
    mq[...] = (dot(ef[0], wm[0, 0]) + dot(ef[1], wm[1, 0])).astype(BF)

    stage3.wait_recv()

    @pl.when(late == 0)
    def _():
        tp[...] = tt[ylo]

    @pl.when(late == 1)
    def _():
        stage3p.wait()

    block = (tp[...].astype(F32) + rec[...].astype(F32)).reshape(128, 128).T.astype(BF)

    bq[0] = block[:64]
    bq[1] = block[64:]
    back2, back2_in, back3, back3_in = [], [], [], []
    for h in range(2):
        for d in range(4):
            to, of = ring(h, 2, d)[0], ahead(line[1 - h], 4 - d)
            for y in range(2):
                if d or y:
                    n = AG2 + 7 * h + 2 * d + y - 1
                    back2.append(remote(bq.at[h], bp.at[h, line[1 - h], ylo], n, (to + y * (across - s), g)))
                    came = bp.at[h, of, ylo + y * (1 - 2 * ylo)]
                    back2_in.append(remote(bq.at[h], came, n, partner))
        for d in (1, 2, 3):
            n = AG3 + 3 * h + d - 1
            back3.append(remote(bp.at[h], blocks.at[core, h, line[h]], n, ring(h, 1, d)))
            back3_in.append(remote(bp.at[h], blocks.at[core, h, ahead(line[h], 4 - d)], n, partner))
    for c in back2:
        c.start()
    for h in range(2):
        bp[h, line[1 - h], ylo] = bq[h]
    lax.fori_loop(2, 4, interior, 0)

    for h in range(2):
        for c in back2_in[7 * h : 7 * h + 7]:
            c.wait_recv()
        for c in back3[3 * h : 3 * h + 3]:
            c.start()
        blocks[core, h, line[h]] = bp[h]

    def pass_copy(k, h, d):
        part = blocks.at[k, h, ahead(line[h], 4 - d)]
        return remote(part, part, AGF + 4 * h + d, (sib, g))

    def result_copy(k, h, d):
        n = ahead(line[h], 4 - d)
        return pltpu.make_async_copy(blocks.at[k, h, n], gkv_out.at[k, h, n], out_s.at[k, 4 * h + d])

    passed = [pass_copy(core, h, d) for h in range(2) for d in range(4)]
    handed = [pass_copy(1 - core, h, d) for h in range(2) for d in range(4)]
    mine_out = [result_copy(core, h, d) for h in range(2) for d in range(4)]
    other_out = [result_copy(1 - core, h, d) for h in range(2) for d in range(4)]
    for n in (0, 4):
        passed[n].start()
        mine_out[n].start()

    where_n = iota((M, 256), 1) - R
    delta = where_n - iota((M, 256), 0)
    allowed = delta == off[0]
    for j in range(1, W):
        allowed = allowed | (delta == off[j])
    where_g = where_n + s * M
    allowed = allowed & (where_g >= 0) & (where_g < M * SPACE)
    allow = jnp.where(allowed[:, : M + 2 * R], 1.0, 0.0)
    allow4 = jnp.concatenate([allow] * 4, axis=0)
    kup.wait_recv()
    kdown.wait_recv()
    matts = []
    for a in range(2):
        cols = slice(a * 256, (a + 1) * 256)
        x4 = mq[:, cols].astype(F32)
        head = iota((M, 256), 1) // 64
        lhs = jnp.concatenate([jnp.where(head == i, x4, 0.0).astype(BF) for i in range(4)], axis=0)
        raw = dot_t(lhs, mkv[0, :, cols]) * SCALE
        wgt = jnp.exp(CAP * jnp.tanh(raw * (1.0 / CAP))) * allow4
        prob = (wgt / jnp.sum(wgt, axis=1, keepdims=True)).astype(BF)
        matts.append(diagonal(dot(prob, mkv[1, :, cols])).astype(BF))
    matt = jnp.concatenate(matts, axis=1)
    loads[10].wait()
    loads[11].wait()
    mo_send[...] = dot(matt, wmo[1]).astype(BF)
    e8 = remote(mo_send, mo_recv, E8, partner)
    e8.start()
    mo_own[...] = dot(matt, wmo[0])

    gdown.wait_recv()
    gup.wait_recv()
    ggs[0:RIM, :] = (ggs[0:RIM, :].astype(F32) + halo_recv[0].astype(F32)).astype(BF)
    ggs[G - RIM : G, :] = (ggs[G - RIM : G, :].astype(F32) + halo_recv[1].astype(F32)).astype(BF)
    gg_copy = pltpu.make_async_copy(ggs, gg_out, osem.at[2])
    gg_copy.start()

    singles = [e1m, e1c, hup, hdown, e2, e2d, e3a, e3b, e4, e5, e6, kup, kdown, gdown, gup, stage3]
    for c in singles + wy + [c for c, _ in wring] + wfwd + presum + stage1 + stage2 + back2:
        c.wait_send()
    for d in (1, 2, 3):
        for h in range(2):
            back3_in[3 * h + d - 1].wait_recv()
            passed[4 * h + d].start()
            mine_out[4 * h + d].start()
    e8.wait()
    mo_val[...] = (ef[0].astype(F32) + mo_own[...] + mo_recv[...].astype(F32)).astype(BF)
    mo_copy = pltpu.make_async_copy(mo_val, mesh_out, osem.at[3])
    mo_copy.start()

    for c in back3:
        c.wait_send()
    for d in range(4):
        for h in range(2):
            handed[4 * h + d].wait_recv()
            other_out[4 * h + d].start()
    for c in passed:
        c.wait_send()
    enc_copy.wait()
    gg_copy.wait()
    mo_copy.wait()
    for c in mine_out + other_out:
        c.wait()


def write_results(enc, mesh_o, gg, gkv, enc_out, mesh_out, gg_out, gkv_out, e, m, r, low, wide, s_in, s_out, k_in, k_out):
    plain = ((enc, e, enc_out), (mesh_o, m, mesh_out), (gg, r, gg_out))
    g = lax.axis_index("head")
    loads = [pltpu.make_async_copy(gkv.at[k], low.at[k], k_in.at[k]) for k in range(2)]
    others = [pltpu.make_async_copy(a, b, s_in.at[n]) for n, (a, b, _) in enumerate(plain)]
    for c in loads:
        c.start()
    stores = []
    for k in range(2):
        loads[k].wait()
        if k == 0:
            for c in others[::-1]:
                c.start()
        for n in range(2):
            half = g if n == 0 else 1 - g
            for x in (2 * n, 2 * n + 1):
                for z in range(4):
                    for y in range(2):
                        col = (x % 2 * 2 + y) * 128
                        for h in range(2):
                            rows = pl.ds(pl.multiple_of(half * F + z * 128 + h * 64, 64), 64)
                            part = low[k, 0, z, x, y] if h == 0 else low[k, 1, x, z, y]
                            wide[k, rows, col : col + 128] = part.astype(F32)
            rows = pl.ds(pl.multiple_of(half * F, F), F)
            stores.append(pltpu.make_async_copy(wide.at[k, rows], gkv_out.at[k, rows], k_out.at[2 * k + n]))
            stores[-1].start()
    for n, (_, b, c) in enumerate(plain):
        others[n].wait()
        stores.append(pltpu.make_async_copy(b, c, s_out.at[n]))
        stores[-1].start()
    for c in stores:
        c.wait()


def shards(
    grid_feat, mesh_feat, edge_src, degree, offsets, w_kv, w_query, w_out, w_mesh, w_mesh_out, cotangent
):
    hbm = pl.BlockSpec(memory_space=pl.ANY)
    vmem = pl.BlockSpec(memory_space=pltpu.VMEM)
    smem = pl.BlockSpec(memory_space=pltpu.SMEM)

    def v(*shape, dtype=BF):
        return pltpu.VMEM(shape, dtype)

    dma = pltpu.SemaphoreType.DMA
    scratch = dict(
        nodes=v(M, K, dtype=I32), wide=v(WIDE, F), mf=v(2, M, F), cf=v(2, M, F), wkv_own=v(2, F, F), wkv_oth=v(2, F, F),
        wq=v(2, F, F), wo=v(2, F, F), wm=v(2, 3, F, F), wmo=v(2, F, F),
        qd=v(2, 2, M, F), qdt=v(2, 2, F, M), xs=v(G, F), ut=v(2, 16, M, F), zy=v(2, 16, M, F),
        srow=v(8, G, dtype=F32),
        sd=v(2, 8, K, 256, dtype=F32), sd_send=v(2, 8, K, 256), sd_recv=v(2, 8, K, 256), pb=v(8, K, 512),
        att_own=v(M, F, dtype=F32), att_send=v(M, F), att_recv=v(M, F),
        enc_own=v(M, F, dtype=F32), enc_send=v(M, F), enc_recv=v(M, F), ef=v(2, M, F),
        mkv=v(2, M + 2 * R, F), mq=v(M, F),
        mo_own=v(M, F, dtype=F32), mo_send=v(M, F), mo_recv=v(M, F), mo_val=v(M, F),
        gedge=v(G, F), halo_send=v(2, RIM, F), halo_recv=v(2, RIM, F), ggs=v(G, F),
        gb=v(2, 2, 4, 8, 64, 128), pre=v(2, 4, 8, 64, 128), rs1=v(2, 3, 8, 64, 128), rsum=v(2, 8, 64, 128),
        rs2=v(2, 3, 2, 64, 128), tt=v(2, 2, 64, 128), tp=v(2, 64, 128), rec=v(2, 64, 128),
        bq=v(2, 64, 128), bp=v(2, 4, 2, 64, 128), blocks=v(2, 2, 4, 4, 2, 64, 128),
        lsem=dma((12,)), osem=dma((4,)), ssem=dma((N_REMOTE,)), rsem=dma((N_REMOTE,)),
        out_s=dma((2, 8)),
    )
    enc, mesh_out, grad_grid, grad_kv = pl.pallas_call(
        body,
        out_shape=(
            jax.ShapeDtypeStruct((M, F), BF),
            jax.ShapeDtypeStruct((M, F), BF),
            jax.ShapeDtypeStruct((G, F), BF),
            jax.ShapeDtypeStruct((2, 2, 4, 4, 2, 64, 128), BF),
        ),
        in_specs=[hbm, hbm, vmem, vmem, smem, hbm, hbm, hbm, hbm, hbm, hbm],
        out_specs=(hbm, hbm, hbm, hbm),
        scratch_shapes=list(scratch.values()),
        compiler_params=pltpu.CompilerParams(
            collective_id=0, has_side_effects=True, vmem_limit_bytes=58 * 2**20
        ),
        name="encoder",
    )(
        grid_feat, mesh_feat, edge_src.T, degree.reshape(1, M), offsets, w_kv, w_query, w_out, w_mesh,
        w_mesh_out, cotangent,
    )
    dma = pltpu.SemaphoreType.DMA
    return pl.pallas_call(
        write_results,
        out_shape=(
            jax.ShapeDtypeStruct((M, F), BF),
            jax.ShapeDtypeStruct((M, F), BF),
            jax.ShapeDtypeStruct((G, F), BF),
            jax.ShapeDtypeStruct((2, 2 * F, F), F32),
        ),
        in_specs=[hbm] * 4,
        out_specs=(hbm,) * 4,
        scratch_shapes=[
            v(M, F), v(M, F), v(G, F), v(2, 2, 4, 4, 2, 64, 128), v(2, 2 * F, F, dtype=F32),
            dma((3,)), dma((3,)), dma((2,)), dma((4,)),
        ],
        compiler_params=pltpu.CompilerParams(vmem_limit_bytes=58 * 2**20),
        name="results",
    )(enc, mesh_out, grad_grid, grad_kv)


def solution(mesh):
    in_specs = (
        P("space", "head"),
        P("space", "head"),
        P("space", None),
        P("space"),
        P(),
        P(None, None, "head"),
        P(None, "head"),
        P("head", None),
        P(None, None, "head"),
        P("head", None),
        P("space", "head"),
    )
    out_specs = (P("space", "head"), P("space", "head"), P("space", "head"), P(None, None, "head"))
    return jax.shard_map(shards, mesh=mesh, in_specs=in_specs, out_specs=out_specs, check_vma=False)
```

```python
import functools

import jax
import jax.numpy as jnp
from jax import lax
from jax.experimental import pallas as pl
from jax.experimental.pallas import tpu as pltpu
from jax.sharding import PartitionSpec as P

BF = jnp.bfloat16
F32 = jnp.float32
I32 = jnp.int32
MESH = pl.DeviceIdType.MESH

M = 128
K = 16
G = 2048
RIM = 128
WIDE = G + 2 * RIM
R = 32
W = 16
F = 512
HL = 8
SPACE = 64
CHIPS = SPACE // 2
CAP = 3.0
SCALE = 0.125

(
    E1M, E1C, HUP, HDOWN, E2, E3A, E3B, E4, E5, E6, KUP, KDOWN, E8, GUP, GDOWN,
    RS3, RS3P, E2D, WY, WR, WF, PRE, RS1, RS2, AG2, AG3, AGF,
) = list(range(19)) + [20, 26, 34, 42, 48, 54, 68, 74]
N_REMOTE = 82


def dot(a, b):
    return jnp.dot(a, b, preferred_element_type=F32)


def dot_t(a, b):
    return lax.dot_general(a, b, (((1,), (1,)), ((), ())), preferred_element_type=F32)


def dot_first(a, b):
    return lax.dot_general(a, b, (((0,), (0,)), ((), ())), preferred_element_type=F32)


def iota(shape, dim):
    return lax.broadcasted_iota(I32, shape, dim)


def body(
    grid_in, mesh_in, src, deg, off, wkv_in, wq_in, wo_in, wm_in, wmo_in, cot_in,
    enc_out, mesh_out, gg_out, gkv_out,
    nodes, wide, mf, cf, wkv_own, wkv_oth, wq, wo, wm, wmo, qd, qdt, xs, ut, zy, srow,
    sd, sd_send, sd_recv, pb, att_own, att_send, att_recv, enc_own, enc_send, enc_recv, ef, mkv, mq,
    mo_own, mo_send, mo_recv, mo_val, gedge, halo_send, halo_recv, ggs,
    gb, pre, rs1, rsum, rs2, tt, tp, rec, bq, bp, blocks,
    lsem, osem, ssem, rsem, out_s,
):
    s = lax.axis_index("space")
    g = lax.axis_index("head")
    o = 1 - g
    core = s % 2
    chip = s // 2
    sib = s + 1 - 2 * core
    up = (s + 1) % SPACE
    down = (s + SPACE - 1) % SPACE

    def flip(bit):
        return s + bit - 2 * bit * ((s // bit) % 2)

    ylo = (s // 8) % 2
    across = flip(8)
    at_x, at_z = chip // 8, chip % 4

    def along(axis, d):
        return (s + 16 * d) % SPACE if axis == 0 else s - 2 * at_z + 2 * ((at_z + d) % 4)

    far = s - 1 + 2 * core
    far = (far + SPACE) % SPACE

    def remote(src_ref, dst_ref, n, dev):
        return pltpu.make_async_remote_copy(
            src_ref=src_ref, dst_ref=dst_ref, send_sem=ssem.at[n], recv_sem=rsem.at[n],
            device_id=dev, device_id_type=MESH,
        )

    partner = (s, o)
    mine = pl.ds(pl.multiple_of(g * F, F), F)
    other = pl.ds(pl.multiple_of(o * F, F), F)

    local = [
        (mesh_in, mf.at[0]),
        (cot_in, cf.at[0]),
        (wq_in.at[mine, :], wq.at[0]),
        (wo_in.at[:, mine], wo.at[0]),
        (wq_in.at[other, :], wq.at[1]),
        (wo_in.at[:, other], wo.at[1]),
        (wkv_in.at[:, mine, :], wkv_own),
        (grid_in, wide.at[pl.ds(RIM, G), :]),
        (wm_in.at[:, mine, :], wm.at[0]),
        (wm_in.at[:, other, :], wm.at[1]),
        (wmo_in.at[:, mine], wmo.at[0]),
        (wmo_in.at[:, other], wmo.at[1]),
    ]
    loads = [pltpu.make_async_copy(a, b, lsem.at[i]) for i, (a, b) in enumerate(local)]
    for c in loads:
        c.start()

    first = [partner, (across, o), (across, g), (sib, g), (far, g)]
    first += [(along(axis, d) + y * (across - s), g) for axis in range(2) for d in (1, 2, 3) for y in range(2)]
    barrier = pltpu.get_barrier_semaphore()
    for dev in first:
        pl.semaphore_signal(barrier, inc=1, device_id=dev, device_id_type=MESH)
    pl.semaphore_wait(barrier, len(first))

    e1m = remote(mesh_in, mf.at[1], E1M, partner)
    e1c = remote(cot_in, cf.at[1], E1C, partner)
    hup = remote(grid_in.at[pl.ds(G - RIM, RIM), :], wide.at[pl.ds(0, RIM), :], HUP, (up, g))
    hdown = remote(grid_in.at[pl.ds(0, RIM), :], wide.at[pl.ds(RIM + G, RIM), :], HDOWN, (down, g))

    def piece(k, axis, q):
        return wkv_oth.at[k, pl.ds(pl.multiple_of(axis * 256 + q * 64, 64), 64), :]

    at = (at_x, at_z)
    wy, wring, wfwd, wback = [], [], [], []
    for axis in range(2):
        rows = pl.ds(pl.multiple_of(o * F + axis * 256 + at[axis] * 64, 64), 64)
        here = piece(core, axis, at[axis])
        wy.append(remote(wkv_in.at[core, rows, :], here, WY + axis, (across, o)))
        for d in range(4):
            q = (at[axis] + 4 - d) % 4
            if d:
                n = WR + 3 * axis + d - 1
                wring.append((
                    remote(here, here, n, (along(axis, d), g)),
                    remote(piece(core, axis, q), piece(core, axis, q), n, partner),
                ))
            n = WF + 4 * axis + d
            wfwd.append(remote(piece(core, axis, q), piece(core, axis, q), n, (sib, g)))
            wback.append(remote(piece(1 - core, axis, q), piece(1 - core, axis, q), n, (sib, g)))
    for c in wy:
        c.start()
    hup.start()
    hdown.start()
    e1m.start()
    e1c.start()

    base = s * G - RIM
    source = src[...].astype(F32).T.astype(I32)
    nodes[...] = source
    rel = source - base
    rel = jnp.where((rel >= 0) & (rel < WIDE), rel, 4095)
    hi = (rel // 64).astype(F32).astype(BF)
    lo = (rel % 64).astype(F32).astype(BF)
    spread = jnp.where(iota((K, 256), 0) == (iota((K, 256), 1) & 15), 1.0, 0.0).astype(BF)
    flat = dot(hi, spread) * 64.0 + dot(lo, spread)
    flat = jnp.where((iota((M, 256), 0) & 15) == iota((M, 256), 1) // 16, flat, 0.0)
    for t in range(8):
        srow[0:1, t * 256 : (t + 1) * 256] = jnp.sum(
            flat[t * 16 : (t + 1) * 16], axis=0, keepdims=True
        )

    for c in wy:
        c.wait_recv()
    for c, _ in wring:
        c.start()
    wfwd[0].start()
    wfwd[4].start()

    loads[7].wait()
    hup.wait_recv()
    hdown.wait_recv()

    def gather(t, carry):
        n = pl.multiple_of(t * 32, 32)
        part = (nodes[pl.ds(n, 32), :] - base).astype(F32)
        part = jnp.broadcast_to(part[:, None, :], (32, K, K)).reshape(512, K)
        pick = (iota((512, K), 0) & 15) == iota((512, K), 1)
        col = jnp.sum(jnp.where(pick, part, 0.0), axis=1, keepdims=True).astype(I32)
        hot = jnp.where(iota((512, WIDE), 1) == col, 1.0, 0.0).astype(BF)
        xs[pl.ds(pl.multiple_of(t * 512, 512), 512), :] = dot(hot, wide[...]).astype(BF)
        return carry

    lax.fori_loop(0, 2, gather, 0)

    for n in (0, 1, 2, 3):
        loads[n].wait()
    loads[4].wait()
    loads[5].wait()
    qa = dot(mf[0], wq[0])
    e1m.wait_recv()
    qd[0, 0] = (qa + dot(mf[1], wq[1])).astype(BF)
    e2 = remote(qd.at[0, 0], qd.at[1, 0], E2, partner)
    e2.start()
    da = dot_t(cf[0], wo[0])
    e1c.wait_recv()
    qd[0, 1] = (da + dot_t(cf[1], wo[1])).astype(BF)
    e2d = remote(qd.at[0, 1], qd.at[1, 1], E2D, partner)
    e2d.start()
    for n, (_, c) in enumerate(wring):
        c.wait_recv()
        wfwd[n + 1 + n // 3].start()

    lax.fori_loop(2, 4, gather, 0)

    def turn(side):
        for k in range(2):
            qdt[side, k] = qd[side, k].astype(F32).T.astype(BF)

    turn(0)

    def expand(side, weights):
        for k in range(2):
            for a in range(2):
                x4 = qd[side, k, :, a * 256 : (a + 1) * 256].astype(F32)
                head = iota((M, 256), 1) // 64
                lhs = jnp.concatenate(
                    [jnp.where(head == i, x4, 0.0).astype(BF) for i in range(4)], axis=0
                )
                out = dot_t(lhs, weights[k, :, a * 256 : (a + 1) * 256]).astype(BF)
                n = side * HL + a * 4
                ut[k, n : n + 4] = out.reshape(4, M, F)

    loads[6].wait()
    expand(0, wkv_own)


    def scores(side):
        def step(t, carry):
            xg = xs[pl.ds(pl.multiple_of(t * 256, 256), 256), :]
            lane = iota((K, 256), 1) & 15
            ug = ut[:, side * HL : side * HL + HL, pl.ds(pl.multiple_of(t * 16, 16), 16), :]
            full = dot_t(xg, ug.reshape(256, F)).reshape(16, K, 256)
            total = jnp.where(lane == 0, full[0], 0.0)
            for m in range(1, 16):
                total = total + jnp.where(lane == m, full[m], 0.0)
            sd[side, t] = total
            sd_send[side, t] = total.astype(BF)
            return carry

        lax.fori_loop(0, 8, step, 0, unroll=4)

    e3a = remote(sd_send.at[0], sd_recv.at[1], E3A, partner)
    e3b = remote(sd_send.at[1], sd_recv.at[0], E3B, partner)
    scores(0)
    e3a.start()
    e2.wait_recv()
    e2d.wait_recv()
    turn(1)
    for c in wback:
        c.wait_recv()
    expand(1, wkv_oth)

    scores(1)
    e3b.start()

    dg = deg[...].astype(F32)
    dg = jnp.where(iota((8, M), 1) // 16 == iota((8, M), 0), dg, 0.0).astype(BF)
    tile = jnp.where((iota((M, 128), 0) & 15) == (iota((M, 128), 1) & 15), 1.0, 0.0).astype(BF)
    dlane = dot(dg, tile)
    live = iota((8, K, 128), 1).astype(F32) < dlane[:, None, :]

    for side in (1, 0):
        (e3a if side else e3b).wait_recv()
        raw = (sd[side, :, :, :128] + sd_recv[side, :, :, :128].astype(F32)) * SCALE
        dp = sd[side, :, :, 128:] + sd_recv[side, :, :, 128:].astype(F32)
        th = jnp.tanh(raw * (1.0 / CAP))
        wgt = jnp.where(live, jnp.exp(CAP * th), 0.0)
        prob = wgt / jnp.sum(wgt, axis=1, keepdims=True)
        ds = prob * (dp - jnp.sum(prob * dp, axis=1, keepdims=True))
        dr = ds * (1.0 - th * th) * SCALE
        a = side * 128
        pb[:, :, a : a + 128] = dr.astype(BF)
        pb[:, :, 256 + a : 256 + a + 128] = prob.astype(BF)

    def sums(t, carry):
        xg = xs[pl.ds(pl.multiple_of(t * 256, 256), 256), :]
        same = (iota((512, 256), 0) & 15) == iota((512, 256), 1) // 16
        sel = jnp.where(iota((K, 256), 0) == (iota((K, 256), 1) & 15), 1.0, 0.0).astype(BF)
        pt = jnp.where(same, dot_first(pb[t], sel), 0.0).astype(BF)
        out = dot(pt, xg).astype(BF)
        zy[:, :, pl.ds(pl.multiple_of(t * 16, 16), 16), :] = out.reshape(2, 16, 16, F)
        return carry

    lax.fori_loop(0, 8, sums, 0, unroll=4)

    def diagonal(x):
        x = x.reshape(4, M, 256)
        head = iota((M, 256), 1) // 64
        out = jnp.zeros((M, 256), F32)
        for i in range(4):
            out = out + jnp.where(head == i, x[i], 0.0)
        return out

    def weight_terms(n, carry):
        k = (1 - core) + n * (2 * core - 1)
        for side in range(2):
            for p in range(4):
                xt = qdt[side, k, p * 128 : (p + 1) * 128, :].astype(F32)
                first = iota((128, M), 0) < 64
                lhs = jnp.concatenate(
                    [jnp.where(first, xt, 0.0).astype(BF), jnp.where(first, 0.0, xt).astype(BF)], axis=1
                )
                h = side * HL + 2 * p
                rhs = zy[k, h : h + 2].reshape(2 * M, F)
                out = dot(lhs, rhs).astype(BF)
                for f in range(4):
                    x, y = 2 * side + p // 2, p % 2
                    gb[k, 0, f, 2 * x + y] = out[:64, f * 128 : (f + 1) * 128]
                    gb[k, 1, x, 2 * f + y] = out[64:, f * 128 : (f + 1) * 128]
        return carry

    line = (at_z, at_x)
    axis_of = (1, 0)

    def ring(h, stage, d):
        return (along(axis_of[h] if stage == 1 else 1 - axis_of[h], d), g)

    def ahead(n, d):
        return (n + d) % 4

    weight_terms(0, 0)
    presum = [
        remote(gb.at[1 - core, h, ahead(line[h], d)], pre.at[h, ahead(line[h], d)], PRE + 4 * h + d, (sib, g))
        for h in range(2)
        for d in range(4)
    ]
    order = [0, 1, 2, 4, 5, 6, 3, 7]
    order = [(n // 4, (n % 4 + 1) % 4) for n in order]
    for h, d in order:
        presum[4 * h + d].start()
    for a in range(2):
        z4 = zy[1, HL + a * 4 : HL + a * 4 + 4].reshape(4 * M, F)
        att_send[:, a * 256 : (a + 1) * 256] = diagonal(
            dot(z4, wkv_oth[1, :, a * 256 : (a + 1) * 256])
        ).astype(BF)
    e4 = remote(att_send, att_recv, E4, partner)
    e4.start()
    weight_terms(1, 0)
    for a in range(2):
        z4 = zy[1, a * 4 : a * 4 + 4].reshape(4 * M, F)
        att_own[:, a * 256 : (a + 1) * 256] = diagonal(
            dot(z4, wkv_own[1, :, a * 256 : (a + 1) * 256])
        )


    stage1 = [
        remote(gb.at[core, h, ahead(line[h], d)], rs1.at[h, d - 1], RS1 + 3 * h + d - 1, ring(h, 1, d))
        for h in range(2)
        for d in (1, 2, 3)
    ]
    for h, d in order:
        presum[4 * h + d].wait_recv()
        n = ahead(line[h], d)
        gb[core, h, n] = (gb[core, h, n].astype(F32) + pre[h, n].astype(F32)).astype(BF)
        if d:
            stage1[3 * h + d - 1].start()

    e4.wait_recv()
    att = (att_own[...] + att_recv[...].astype(F32)).astype(BF)
    enc_send[...] = dot(att, wo[1]).astype(BF)
    e5 = remote(enc_send, enc_recv, E5, partner)
    e5.start()
    enc_own[...] = dot(att, wo[0])

    def edge_grads(t, carry):
        rows = pl.ds(pl.multiple_of(t * 16, 16), 16)
        match = (iota((16, K, 512), 2) & 15) == iota((16, K, 512), 0)
        p = jnp.broadcast_to(pb[t].astype(F32)[None], (16, K, 512))
        p = jnp.where(match, p, 0.0).astype(BF).reshape(256, 512)
        total = dot(p, ut[:, :, rows, :].reshape(512, F))
        gedge[pl.ds(pl.multiple_of(t * 256, 256), 256), :] = total.astype(BF)
        return carry

    lax.fori_loop(0, 8, edge_grads, 0, unroll=2)

    def rows_of(first, count):
        hot = jnp.where(
            (iota((count, G), 0) + first).astype(F32) == srow[0:1, :], 1.0, 0.0
        ).astype(BF)
        return dot(hot, gedge[...])

    halo_send[0] = rows_of(0, RIM).astype(BF)
    halo_send[1] = rows_of(RIM + G, RIM).astype(BF)
    gdown = remote(halo_send.at[0], halo_recv.at[1], GDOWN, (down, g))
    gup = remote(halo_send.at[1], halo_recv.at[0], GUP, (up, g))
    gdown.start()
    gup.start()

    e5.wait_recv()
    enc = (mf[0].astype(F32) + enc_own[...] + enc_recv[...].astype(F32)).astype(BF)
    ef[0] = enc
    e6 = remote(ef.at[0], ef.at[1], E6, partner)
    e6.start()
    enc_copy = pltpu.make_async_copy(ef.at[0], enc_out, osem.at[0])
    enc_copy.start()

    stage2 = [
        remote(
            rsum.at[h, pl.ds(2 * ahead(line[1 - h], d), 2)], rs2.at[h, d - 1], RS2 + 3 * h + d - 1, ring(h, 2, d)
        )
        for h in range(2)
        for d in (1, 2, 3)
    ]
    for h in range(2):
        for d in range(3):
            stage1[3 * h + d].wait_recv()
        total = gb[core, h, line[h]].astype(F32)
        for d in range(3):
            total = total + rs1[h, d].astype(F32)
        rsum[h] = total.astype(BF)
        for c in stage2[3 * h : 3 * h + 3]:
            c.start()

    def interior(t, carry):
        n = pl.multiple_of(t * 512, 512)
        ggs[pl.ds(n, 512), :] = rows_of(n + RIM, 512).astype(BF)
        return carry

    lax.fori_loop(0, 2, interior, 0)

    late = at_x // 2
    for h in range(2):
        for d in range(3):
            stage2[3 * h + d].wait_recv()
        total = rsum[h, pl.ds(2 * line[1 - h], 2)].astype(F32)
        for d in range(3):
            total = total + rs2[h, d].astype(F32)
        for y in range(2):
            tt[y, h] = total[y].astype(BF)
    stage3 = remote(tt.at[1 - ylo], rec, RS3, (across, g + late * (1 - 2 * g)))
    stage3p = remote(tt.at[ylo], tp, RS3P, partner)
    stage3.start()

    @pl.when(late == 1)
    def _():
        stage3p.start()

    lax.fori_loop(2, 3, interior, 0)
    stage3.wait_recv()

    @pl.when(late == 0)
    def _():
        tp[...] = tt[ylo]

    @pl.when(late == 1)
    def _():
        stage3p.wait()

    block = (tp[...].astype(F32) + rec[...].astype(F32)).reshape(128, 128).T.astype(BF)

    bq[0] = block[:64]
    bq[1] = block[64:]
    back2, back2_in, back3, back3_in = [], [], [], []
    for h in range(2):
        for d in range(4):
            to, of = ring(h, 2, d)[0], ahead(line[1 - h], 4 - d)
            for y in range(2):
                if d or y:
                    n = AG2 + 7 * h + 2 * d + y - 1
                    back2.append(remote(bq.at[h], bp.at[h, line[1 - h], ylo], n, (to + y * (across - s), g)))
                    came = bp.at[h, of, ylo + y * (1 - 2 * ylo)]
                    back2_in.append(remote(bq.at[h], came, n, partner))
        for d in (1, 2, 3):
            n = AG3 + 3 * h + d - 1
            back3.append(remote(bp.at[h], blocks.at[core, h, line[h]], n, ring(h, 1, d)))
            back3_in.append(remote(bp.at[h], blocks.at[core, h, ahead(line[h], 4 - d)], n, partner))
    for c in back2:
        c.start()
    for h in range(2):
        bp[h, line[1 - h], ylo] = bq[h]
    loads[8].wait()
    loads[9].wait()
    e6.wait_recv()
    for k in range(2):
        mkv[k, R : R + M, :] = (dot(ef[0], wm[0, 1 + k]) + dot(ef[1], wm[1, 1 + k])).astype(BF)
    kup = remote(mkv.at[:, pl.ds(M, R), :], mkv.at[:, pl.ds(0, R), :], KUP, (up, g))
    kdown = remote(mkv.at[:, pl.ds(R, R), :], mkv.at[:, pl.ds(R + M, R), :], KDOWN, (down, g))
    kup.start()
    kdown.start()
    mq[...] = (dot(ef[0], wm[0, 0]) + dot(ef[1], wm[1, 0])).astype(BF)

    lax.fori_loop(3, 4, interior, 0)

    for h in range(2):
        for c in back2_in[7 * h : 7 * h + 7]:
            c.wait_recv()
        for c in back3[3 * h : 3 * h + 3]:
            c.start()
        blocks[core, h, line[h]] = bp[h]

    def pass_copy(k, h, d):
        part = blocks.at[k, h, ahead(line[h], 4 - d)]
        return remote(part, part, AGF + 4 * h + d, (sib, g))

    def result_copy(k, h, d):
        n = ahead(line[h], 4 - d)
        return pltpu.make_async_copy(blocks.at[k, h, n], gkv_out.at[k, h, n], out_s.at[k, 4 * h + d])

    passed = [pass_copy(core, h, d) for h in range(2) for d in range(4)]
    handed = [pass_copy(1 - core, h, d) for h in range(2) for d in range(4)]
    mine_out = [result_copy(core, h, d) for h in range(2) for d in range(4)]
    other_out = [result_copy(1 - core, h, d) for h in range(2) for d in range(4)]
    for n in (0, 4):
        passed[n].start()
        mine_out[n].start()

    where_n = iota((M, 256), 1) - R
    delta = where_n - iota((M, 256), 0)
    allowed = delta == off[0]
    for j in range(1, W):
        allowed = allowed | (delta == off[j])
    where_g = where_n + s * M
    allowed = allowed & (where_g >= 0) & (where_g < M * SPACE)
    allow = jnp.where(allowed[:, : M + 2 * R], 1.0, 0.0)
    allow4 = jnp.concatenate([allow] * 4, axis=0)
    kup.wait_recv()
    kdown.wait_recv()
    matts = []
    for a in range(2):
        cols = slice(a * 256, (a + 1) * 256)
        x4 = mq[:, cols].astype(F32)
        head = iota((M, 256), 1) // 64
        lhs = jnp.concatenate([jnp.where(head == i, x4, 0.0).astype(BF) for i in range(4)], axis=0)
        raw = dot_t(lhs, mkv[0, :, cols]) * SCALE
        wgt = jnp.exp(CAP * jnp.tanh(raw * (1.0 / CAP))) * allow4
        prob = (wgt / jnp.sum(wgt, axis=1, keepdims=True)).astype(BF)
        matts.append(diagonal(dot(prob, mkv[1, :, cols])).astype(BF))
    matt = jnp.concatenate(matts, axis=1)
    loads[10].wait()
    loads[11].wait()
    mo_send[...] = dot(matt, wmo[1]).astype(BF)
    e8 = remote(mo_send, mo_recv, E8, partner)
    e8.start()
    mo_own[...] = dot(matt, wmo[0])

    gdown.wait_recv()
    gup.wait_recv()
    ggs[0:RIM, :] = (ggs[0:RIM, :].astype(F32) + halo_recv[0].astype(F32)).astype(BF)
    ggs[G - RIM : G, :] = (ggs[G - RIM : G, :].astype(F32) + halo_recv[1].astype(F32)).astype(BF)
    gg_copy = pltpu.make_async_copy(ggs, gg_out, osem.at[2])
    gg_copy.start()

    singles = [e1m, e1c, hup, hdown, e2, e2d, e3a, e3b, e4, e5, e6, kup, kdown, gdown, gup, stage3]
    for c in singles + wy + [c for c, _ in wring] + wfwd + presum + stage1 + stage2 + back2:
        c.wait_send()
    for d in (1, 2, 3):
        for h in range(2):
            back3_in[3 * h + d - 1].wait_recv()
            passed[4 * h + d].start()
            mine_out[4 * h + d].start()
    e8.wait()
    mo_val[...] = (ef[0].astype(F32) + mo_own[...] + mo_recv[...].astype(F32)).astype(BF)
    mo_copy = pltpu.make_async_copy(mo_val, mesh_out, osem.at[3])
    mo_copy.start()

    for c in back3:
        c.wait_send()
    for d in range(4):
        for h in range(2):
            handed[4 * h + d].wait_recv()
            other_out[4 * h + d].start()
    for c in passed:
        c.wait_send()
    enc_copy.wait()
    gg_copy.wait()
    mo_copy.wait()
    for c in mine_out + other_out:
        c.wait()


def write_results(enc, mesh_o, gg, gkv, enc_out, mesh_out, gg_out, gkv_out, e, m, r, low, wide, s_in, s_out, k_in, k_out):
    plain = ((enc, e, enc_out), (mesh_o, m, mesh_out), (gg, r, gg_out))
    g = lax.axis_index("head")
    loads = [pltpu.make_async_copy(gkv.at[k], low.at[k], k_in.at[k]) for k in range(2)]
    others = [pltpu.make_async_copy(a, b, s_in.at[n]) for n, (a, b, _) in enumerate(plain)]
    for c in loads + others:
        c.start()
    stores = []
    for k in range(2):
        loads[k].wait()
        for n in range(2):
            half = g if n == 0 else 1 - g
            for x in (2 * n, 2 * n + 1):
                for z in range(4):
                    for y in range(2):
                        col = (x % 2 * 2 + y) * 128
                        for h in range(2):
                            rows = pl.ds(pl.multiple_of(half * F + z * 128 + h * 64, 64), 64)
                            part = low[k, 0, z, x, y] if h == 0 else low[k, 1, x, z, y]
                            wide[k, rows, col : col + 128] = part.astype(F32)
            rows = pl.ds(pl.multiple_of(half * F, F), F)
            stores.append(pltpu.make_async_copy(wide.at[k, rows], gkv_out.at[k, rows], k_out.at[2 * k + n]))
            stores[-1].start()
    for n, (_, b, c) in enumerate(plain):
        others[n].wait()
        stores.append(pltpu.make_async_copy(b, c, s_out.at[n]))
        stores[-1].start()
    for c in stores:
        c.wait()


def shards(
    grid_feat, mesh_feat, edge_src, degree, offsets, w_kv, w_query, w_out, w_mesh, w_mesh_out, cotangent
):
    hbm = pl.BlockSpec(memory_space=pl.ANY)
    vmem = pl.BlockSpec(memory_space=pltpu.VMEM)
    smem = pl.BlockSpec(memory_space=pltpu.SMEM)

    def v(*shape, dtype=BF):
        return pltpu.VMEM(shape, dtype)

    dma = pltpu.SemaphoreType.DMA
    scratch = dict(
        nodes=v(M, K, dtype=I32), wide=v(WIDE, F), mf=v(2, M, F), cf=v(2, M, F), wkv_own=v(2, F, F), wkv_oth=v(2, F, F),
        wq=v(2, F, F), wo=v(2, F, F), wm=v(2, 3, F, F), wmo=v(2, F, F),
        qd=v(2, 2, M, F), qdt=v(2, 2, F, M), xs=v(G, F), ut=v(2, 16, M, F), zy=v(2, 16, M, F),
        srow=v(8, G, dtype=F32),
        sd=v(2, 8, K, 256, dtype=F32), sd_send=v(2, 8, K, 256), sd_recv=v(2, 8, K, 256), pb=v(8, K, 512),
        att_own=v(M, F, dtype=F32), att_send=v(M, F), att_recv=v(M, F),
        enc_own=v(M, F, dtype=F32), enc_send=v(M, F), enc_recv=v(M, F), ef=v(2, M, F),
        mkv=v(2, M + 2 * R, F), mq=v(M, F),
        mo_own=v(M, F, dtype=F32), mo_send=v(M, F), mo_recv=v(M, F), mo_val=v(M, F),
        gedge=v(G, F), halo_send=v(2, RIM, F), halo_recv=v(2, RIM, F), ggs=v(G, F),
        gb=v(2, 2, 4, 8, 64, 128), pre=v(2, 4, 8, 64, 128), rs1=v(2, 3, 8, 64, 128), rsum=v(2, 8, 64, 128),
        rs2=v(2, 3, 2, 64, 128), tt=v(2, 2, 64, 128), tp=v(2, 64, 128), rec=v(2, 64, 128),
        bq=v(2, 64, 128), bp=v(2, 4, 2, 64, 128), blocks=v(2, 2, 4, 4, 2, 64, 128),
        lsem=dma((12,)), osem=dma((4,)), ssem=dma((N_REMOTE,)), rsem=dma((N_REMOTE,)),
        out_s=dma((2, 8)),
    )
    enc, mesh_out, grad_grid, grad_kv = pl.pallas_call(
        body,
        out_shape=(
            jax.ShapeDtypeStruct((M, F), BF),
            jax.ShapeDtypeStruct((M, F), BF),
            jax.ShapeDtypeStruct((G, F), BF),
            jax.ShapeDtypeStruct((2, 2, 4, 4, 2, 64, 128), BF),
        ),
        in_specs=[hbm, hbm, vmem, vmem, smem, hbm, hbm, hbm, hbm, hbm, hbm],
        out_specs=(hbm, hbm, hbm, hbm),
        scratch_shapes=list(scratch.values()),
        compiler_params=pltpu.CompilerParams(
            collective_id=0, has_side_effects=True, vmem_limit_bytes=58 * 2**20
        ),
        name="encoder",
    )(
        grid_feat, mesh_feat, edge_src.T, degree.reshape(1, M), offsets, w_kv, w_query, w_out, w_mesh,
        w_mesh_out, cotangent,
    )
    dma = pltpu.SemaphoreType.DMA
    return pl.pallas_call(
        write_results,
        out_shape=(
            jax.ShapeDtypeStruct((M, F), BF),
            jax.ShapeDtypeStruct((M, F), BF),
            jax.ShapeDtypeStruct((G, F), BF),
            jax.ShapeDtypeStruct((2, 2 * F, F), F32),
        ),
        in_specs=[hbm] * 4,
        out_specs=(hbm,) * 4,
        scratch_shapes=[
            v(M, F), v(M, F), v(G, F), v(2, 2, 4, 4, 2, 64, 128), v(2, 2 * F, F, dtype=F32),
            dma((3,)), dma((3,)), dma((2,)), dma((4,)),
        ],
        compiler_params=pltpu.CompilerParams(vmem_limit_bytes=58 * 2**20),
        name="results",
    )(enc, mesh_out, grad_grid, grad_kv)


def solution(mesh):
    in_specs = (
        P("space", "head"),
        P("space", "head"),
        P("space", None),
        P("space"),
        P(),
        P(None, None, "head"),
        P(None, "head"),
        P("head", None),
        P(None, None, "head"),
        P("head", None),
        P("space", "head"),
    )
    out_specs = (P("space", "head"), P("space", "head"), P("space", "head"), P(None, None, "head"))
    return jax.shard_map(shards, mesh=mesh, in_specs=in_specs, out_specs=out_specs, check_vma=False)
```

```python
import functools

import jax
import jax.numpy as jnp
from jax import lax
from jax.experimental import pallas as pl
from jax.experimental.pallas import tpu as pltpu
from jax.sharding import PartitionSpec as P

BF = jnp.bfloat16
F32 = jnp.float32
I32 = jnp.int32
MESH = pl.DeviceIdType.MESH

M = 128
K = 16
G = 2048
RIM = 128
WIDE = G + 2 * RIM
R = 32
W = 16
F = 512
HL = 8
SPACE = 64
CHIPS = SPACE // 2
CAP = 3.0
SCALE = 0.125

(
    E1M, E1C, HUP, HDOWN, E2, E3A, E3B, E4, E5, E6, KUP, KDOWN, E8, GUP, GDOWN,
    RS3, RS3P, E2D, WY, WR, WF, PRE, RS1, RS2, AG2, AG3, AGF,
) = list(range(19)) + [20, 26, 34, 42, 48, 54, 68, 74]
N_REMOTE = 82


def dot(a, b):
    return jnp.dot(a, b, preferred_element_type=F32)


def dot_t(a, b):
    return lax.dot_general(a, b, (((1,), (1,)), ((), ())), preferred_element_type=F32)


def dot_first(a, b):
    return lax.dot_general(a, b, (((0,), (0,)), ((), ())), preferred_element_type=F32)


def iota(shape, dim):
    return lax.broadcasted_iota(I32, shape, dim)


def body(
    grid_in, mesh_in, src, deg, off, wkv_in, wq_in, wo_in, wm_in, wmo_in, cot_in,
    enc_out, mesh_out, gg_out, gkv_out,
    nodes, wide, mf, cf, wkv_own, wkv_oth, wq, wo, wm, wmo, qd, qdt, xs, ut, zy, srow,
    sd, sd_send, sd_recv, pb, att_own, att_send, att_recv, enc_own, enc_send, enc_recv, ef, mkv, mq,
    mo_own, mo_send, mo_recv, mo_val, gedge, halo_send, halo_recv, ggs,
    gb, pre, rs1, rsum, rs2, tt, tp, rec, bq, bp, blocks,
    lsem, osem, ssem, rsem, out_s,
):
    s = lax.axis_index("space")
    g = lax.axis_index("head")
    o = 1 - g
    core = s % 2
    chip = s // 2
    sib = s + 1 - 2 * core
    up = (s + 1) % SPACE
    down = (s + SPACE - 1) % SPACE

    def flip(bit):
        return s + bit - 2 * bit * ((s // bit) % 2)

    ylo = (s // 8) % 2
    across = flip(8)
    at_x, at_z = chip // 8, chip % 4

    def along(axis, d):
        return (s + 16 * d) % SPACE if axis == 0 else s - 2 * at_z + 2 * ((at_z + d) % 4)

    far = s - 1 + 2 * core
    far = (far + SPACE) % SPACE

    def remote(src_ref, dst_ref, n, dev):
        return pltpu.make_async_remote_copy(
            src_ref=src_ref, dst_ref=dst_ref, send_sem=ssem.at[n], recv_sem=rsem.at[n],
            device_id=dev, device_id_type=MESH,
        )

    partner = (s, o)
    mine = pl.ds(pl.multiple_of(g * F, F), F)
    other = pl.ds(pl.multiple_of(o * F, F), F)

    local = [
        (mesh_in, mf.at[0]),
        (cot_in, cf.at[0]),
        (wq_in.at[mine, :], wq.at[0]),
        (wo_in.at[:, mine], wo.at[0]),
        (wq_in.at[other, :], wq.at[1]),
        (wo_in.at[:, other], wo.at[1]),
        (wkv_in.at[:, mine, :], wkv_own),
        (grid_in, wide.at[pl.ds(RIM, G), :]),
        (wm_in.at[:, mine, :], wm.at[0]),
        (wm_in.at[:, other, :], wm.at[1]),
        (wmo_in.at[:, mine], wmo.at[0]),
        (wmo_in.at[:, other], wmo.at[1]),
    ]
    loads = [pltpu.make_async_copy(a, b, lsem.at[i]) for i, (a, b) in enumerate(local)]
    for c in loads:
        c.start()

    first = [partner, (across, o), (across, g), (sib, g), (far, g)]
    first += [(along(axis, d) + y * (across - s), g) for axis in range(2) for d in (1, 2, 3) for y in range(2)]
    barrier = pltpu.get_barrier_semaphore()
    for dev in first:
        pl.semaphore_signal(barrier, inc=1, device_id=dev, device_id_type=MESH)
    pl.semaphore_wait(barrier, len(first))

    e1m = remote(mesh_in, mf.at[1], E1M, partner)
    e1c = remote(cot_in, cf.at[1], E1C, partner)
    hup = remote(grid_in.at[pl.ds(G - RIM, RIM), :], wide.at[pl.ds(0, RIM), :], HUP, (up, g))
    hdown = remote(grid_in.at[pl.ds(0, RIM), :], wide.at[pl.ds(RIM + G, RIM), :], HDOWN, (down, g))

    def piece(k, axis, q):
        return wkv_oth.at[k, pl.ds(pl.multiple_of(axis * 256 + q * 64, 64), 64), :]

    at = (at_x, at_z)
    wy, wring, wfwd, wback = [], [], [], []
    for axis in range(2):
        rows = pl.ds(pl.multiple_of(o * F + axis * 256 + at[axis] * 64, 64), 64)
        here = piece(core, axis, at[axis])
        wy.append(remote(wkv_in.at[core, rows, :], here, WY + axis, (across, o)))
        for d in range(4):
            q = (at[axis] + 4 - d) % 4
            if d:
                n = WR + 3 * axis + d - 1
                wring.append((
                    remote(here, here, n, (along(axis, d), g)),
                    remote(piece(core, axis, q), piece(core, axis, q), n, partner),
                ))
            n = WF + 4 * axis + d
            wfwd.append(remote(piece(core, axis, q), piece(core, axis, q), n, (sib, g)))
            wback.append(remote(piece(1 - core, axis, q), piece(1 - core, axis, q), n, (sib, g)))
    for c in wy:
        c.start()
    hup.start()
    hdown.start()
    e1m.start()
    e1c.start()

    base = s * G - RIM
    source = src[...].astype(F32).T.astype(I32)
    nodes[...] = source
    rel = source - base
    rel = jnp.where((rel >= 0) & (rel < WIDE), rel, 4095)
    hi = (rel // 64).astype(F32).astype(BF)
    lo = (rel % 64).astype(F32).astype(BF)
    spread = jnp.where(iota((K, 256), 0) == (iota((K, 256), 1) & 15), 1.0, 0.0).astype(BF)
    flat = dot(hi, spread) * 64.0 + dot(lo, spread)
    flat = jnp.where((iota((M, 256), 0) & 15) == iota((M, 256), 1) // 16, flat, 0.0)
    for t in range(8):
        srow[0:1, t * 256 : (t + 1) * 256] = jnp.sum(
            flat[t * 16 : (t + 1) * 16], axis=0, keepdims=True
        )

    for c in wy:
        c.wait_recv()
    for c, _ in wring:
        c.start()
    wfwd[0].start()
    wfwd[4].start()

    loads[7].wait()
    hup.wait_recv()
    hdown.wait_recv()

    def gather(t, carry):
        n = pl.multiple_of(t * 32, 32)
        part = (nodes[pl.ds(n, 32), :] - base).astype(F32)
        part = jnp.broadcast_to(part[:, None, :], (32, K, K)).reshape(512, K)
        pick = (iota((512, K), 0) & 15) == iota((512, K), 1)
        col = jnp.sum(jnp.where(pick, part, 0.0), axis=1, keepdims=True).astype(I32)
        hot = jnp.where(iota((512, WIDE), 1) == col, 1.0, 0.0).astype(BF)
        xs[pl.ds(pl.multiple_of(t * 512, 512), 512), :] = dot(hot, wide[...]).astype(BF)
        return carry

    lax.fori_loop(0, 2, gather, 0)

    for n in (0, 1, 2, 3):
        loads[n].wait()
    loads[4].wait()
    loads[5].wait()
    qa = dot(mf[0], wq[0])
    e1m.wait_recv()
    qd[0, 0] = (qa + dot(mf[1], wq[1])).astype(BF)
    e2 = remote(qd.at[0, 0], qd.at[1, 0], E2, partner)
    e2.start()
    da = dot_t(cf[0], wo[0])
    e1c.wait_recv()
    qd[0, 1] = (da + dot_t(cf[1], wo[1])).astype(BF)
    e2d = remote(qd.at[0, 1], qd.at[1, 1], E2D, partner)
    e2d.start()
    for n, (_, c) in enumerate(wring):
        c.wait_recv()
        wfwd[n + 1 + n // 3].start()

    lax.fori_loop(2, 4, gather, 0)

    def turn(side):
        for k in range(2):
            qdt[side, k] = qd[side, k].astype(F32).T.astype(BF)

    turn(0)

    def expand(side, weights):
        for k in range(2):
            for a in range(2):
                x4 = qd[side, k, :, a * 256 : (a + 1) * 256].astype(F32)
                head = iota((M, 256), 1) // 64
                lhs = jnp.concatenate(
                    [jnp.where(head == i, x4, 0.0).astype(BF) for i in range(4)], axis=0
                )
                out = dot_t(lhs, weights[k, :, a * 256 : (a + 1) * 256]).astype(BF)
                n = side * HL + a * 4
                ut[k, n : n + 4] = out.reshape(4, M, F)

    loads[6].wait()
    expand(0, wkv_own)


    def scores(side):
        def step(t, carry):
            xg = xs[pl.ds(pl.multiple_of(t * 256, 256), 256), :]
            lane = iota((K, 256), 1) & 15
            ug = ut[:, side * HL : side * HL + HL, pl.ds(pl.multiple_of(t * 16, 16), 16), :]
            full = dot_t(xg, ug.reshape(256, F)).reshape(16, K, 256)
            total = jnp.where(lane == 0, full[0], 0.0)
            for m in range(1, 16):
                total = total + jnp.where(lane == m, full[m], 0.0)
            sd[side, t] = total
            sd_send[side, t] = total.astype(BF)
            return carry

        lax.fori_loop(0, 8, step, 0, unroll=4)

    e3a = remote(sd_send.at[0], sd_recv.at[1], E3A, partner)
    e3b = remote(sd_send.at[1], sd_recv.at[0], E3B, partner)
    scores(0)
    e3a.start()
    e2.wait_recv()
    e2d.wait_recv()
    turn(1)
    for c in wback:
        c.wait_recv()
    expand(1, wkv_oth)

    scores(1)
    e3b.start()

    dg = deg[...].astype(F32)
    dg = jnp.where(iota((8, M), 1) // 16 == iota((8, M), 0), dg, 0.0).astype(BF)
    tile = jnp.where((iota((M, 128), 0) & 15) == (iota((M, 128), 1) & 15), 1.0, 0.0).astype(BF)
    dlane = dot(dg, tile)
    live = iota((8, K, 128), 1).astype(F32) < dlane[:, None, :]

    def softmax(side):
        (e3a if side else e3b).wait_recv()
        raw = (sd[side, :, :, :128] + sd_recv[side, :, :, :128].astype(F32)) * SCALE
        dp = sd[side, :, :, 128:] + sd_recv[side, :, :, 128:].astype(F32)
        th = jnp.tanh(raw * (1.0 / CAP))
        wgt = jnp.where(live, jnp.exp(CAP * th), 0.0)
        prob = wgt / jnp.sum(wgt, axis=1, keepdims=True)
        ds = prob * (dp - jnp.sum(prob * dp, axis=1, keepdims=True))
        dr = ds * (1.0 - th * th) * SCALE
        a = side * 128
        pb[:, :, a : a + 128] = dr.astype(BF)
        pb[:, :, 256 + a : 256 + a + 128] = prob.astype(BF)

    def sums(side):
        def step(t, carry):
            xg = xs[pl.ds(pl.multiple_of(t * 256, 256), 256), :]
            same = (iota((256, 256), 0) & 15) == iota((256, 256), 1) // 16
            sel = jnp.where(iota((K, 256), 0) == (iota((K, 256), 1) & 15), 1.0, 0.0).astype(BF)
            a = side * 128
            both = jnp.concatenate([pb[t, :, a : a + 128], pb[t, :, 256 + a : 256 + a + 128]], axis=1)
            pt = jnp.where(same, dot_first(both, sel), 0.0).astype(BF)
            out = dot(pt, xg).astype(BF).reshape(2, HL, 16, F)
            zy[:, side * HL : side * HL + HL, pl.ds(pl.multiple_of(t * 16, 16), 16), :] = out
            return carry

        lax.fori_loop(0, 8, step, 0, unroll=4)

    def diagonal(x):
        x = x.reshape(4, M, 256)
        head = iota((M, 256), 1) // 64
        out = jnp.zeros((M, 256), F32)
        for i in range(4):
            out = out + jnp.where(head == i, x[i], 0.0)
        return out

    def weight_terms(n, side):
        k = (1 - core) + n * (2 * core - 1)
        for p in range(4):
            xt = qdt[side, k, p * 128 : (p + 1) * 128, :].astype(F32)
            first = iota((128, M), 0) < 64
            lhs = jnp.concatenate(
                [jnp.where(first, xt, 0.0).astype(BF), jnp.where(first, 0.0, xt).astype(BF)], axis=1
            )
            h = side * HL + 2 * p
            rhs = zy[k, h : h + 2].reshape(2 * M, F)
            out = dot(lhs, rhs).astype(BF)
            for f in range(4):
                x, y = 2 * side + p // 2, p % 2
                gb[k, 0, f, 2 * x + y] = out[:64, f * 128 : (f + 1) * 128]
                gb[k, 1, x, 2 * f + y] = out[64:, f * 128 : (f + 1) * 128]

    line = (at_z, at_x)
    axis_of = (1, 0)

    def ring(h, stage, d):
        return (along(axis_of[h] if stage == 1 else 1 - axis_of[h], d), g)

    def ahead(n, d):
        return (n + d) % 4

    softmax(1)
    sums(1)
    for a in range(2):
        z4 = zy[1, HL + a * 4 : HL + a * 4 + 4].reshape(4 * M, F)
        att_send[:, a * 256 : (a + 1) * 256] = diagonal(
            dot(z4, wkv_oth[1, :, a * 256 : (a + 1) * 256])
        ).astype(BF)
    e4 = remote(att_send, att_recv, E4, partner)
    e4.start()
    weight_terms(0, 1)
    weight_terms(1, 1)
    softmax(0)
    sums(0)
    weight_terms(0, 0)
    presum = [
        remote(gb.at[1 - core, h, ahead(line[h], d)], pre.at[h, ahead(line[h], d)], PRE + 4 * h + d, (sib, g))
        for h in range(2)
        for d in range(4)
    ]
    order = [0, 1, 2, 4, 5, 6, 3, 7]
    order = [(n // 4, (n % 4 + 1) % 4) for n in order]
    for h, d in order:
        presum[4 * h + d].start()
    weight_terms(1, 0)
    for a in range(2):
        z4 = zy[1, a * 4 : a * 4 + 4].reshape(4 * M, F)
        att_own[:, a * 256 : (a + 1) * 256] = diagonal(
            dot(z4, wkv_own[1, :, a * 256 : (a + 1) * 256])
        )


    stage1 = [
        remote(gb.at[core, h, ahead(line[h], d)], rs1.at[h, d - 1], RS1 + 3 * h + d - 1, ring(h, 1, d))
        for h in range(2)
        for d in (1, 2, 3)
    ]
    for h, d in order:
        presum[4 * h + d].wait_recv()
        n = ahead(line[h], d)
        gb[core, h, n] = (gb[core, h, n].astype(F32) + pre[h, n].astype(F32)).astype(BF)
        if d:
            stage1[3 * h + d - 1].start()

    e4.wait_recv()
    att = (att_own[...] + att_recv[...].astype(F32)).astype(BF)
    enc_send[...] = dot(att, wo[1]).astype(BF)
    e5 = remote(enc_send, enc_recv, E5, partner)
    e5.start()
    enc_own[...] = dot(att, wo[0])

    def edge_grads(t, carry):
        rows = pl.ds(pl.multiple_of(t * 16, 16), 16)
        match = (iota((16, K, 512), 2) & 15) == iota((16, K, 512), 0)
        p = jnp.broadcast_to(pb[t].astype(F32)[None], (16, K, 512))
        p = jnp.where(match, p, 0.0).astype(BF).reshape(256, 512)
        total = dot(p, ut[:, :, rows, :].reshape(512, F))
        gedge[pl.ds(pl.multiple_of(t * 256, 256), 256), :] = total.astype(BF)
        return carry

    lax.fori_loop(0, 8, edge_grads, 0, unroll=2)

    def rows_of(first, count):
        hot = jnp.where(
            (iota((count, G), 0) + first).astype(F32) == srow[0:1, :], 1.0, 0.0
        ).astype(BF)
        return dot(hot, gedge[...])

    halo_send[0] = rows_of(0, RIM).astype(BF)
    halo_send[1] = rows_of(RIM + G, RIM).astype(BF)
    gdown = remote(halo_send.at[0], halo_recv.at[1], GDOWN, (down, g))
    gup = remote(halo_send.at[1], halo_recv.at[0], GUP, (up, g))
    gdown.start()
    gup.start()

    e5.wait_recv()
    enc = (mf[0].astype(F32) + enc_own[...] + enc_recv[...].astype(F32)).astype(BF)
    ef[0] = enc
    e6 = remote(ef.at[0], ef.at[1], E6, partner)
    e6.start()
    enc_copy = pltpu.make_async_copy(ef.at[0], enc_out, osem.at[0])
    enc_copy.start()

    stage2 = [
        remote(
            rsum.at[h, pl.ds(2 * ahead(line[1 - h], d), 2)], rs2.at[h, d - 1], RS2 + 3 * h + d - 1, ring(h, 2, d)
        )
        for h in range(2)
        for d in (1, 2, 3)
    ]
    for h in range(2):
        for d in range(3):
            stage1[3 * h + d].wait_recv()
        total = gb[core, h, line[h]].astype(F32)
        for d in range(3):
            total = total + rs1[h, d].astype(F32)
        rsum[h] = total.astype(BF)
        for c in stage2[3 * h : 3 * h + 3]:
            c.start()

    def interior(t, carry):
        n = pl.multiple_of(t * 512, 512)
        ggs[pl.ds(n, 512), :] = rows_of(n + RIM, 512).astype(BF)
        return carry

    lax.fori_loop(0, 2, interior, 0)

    late = at_x // 2
    for h in range(2):
        for d in range(3):
            stage2[3 * h + d].wait_recv()
        total = rsum[h, pl.ds(2 * line[1 - h], 2)].astype(F32)
        for d in range(3):
            total = total + rs2[h, d].astype(F32)
        for y in range(2):
            tt[y, h] = total[y].astype(BF)
    stage3 = remote(tt.at[1 - ylo], rec, RS3, (across, g + late * (1 - 2 * g)))
    stage3p = remote(tt.at[ylo], tp, RS3P, partner)
    stage3.start()

    @pl.when(late == 1)
    def _():
        stage3p.start()

    lax.fori_loop(2, 3, interior, 0)
    stage3.wait_recv()

    @pl.when(late == 0)
    def _():
        tp[...] = tt[ylo]

    @pl.when(late == 1)
    def _():
        stage3p.wait()

    block = (tp[...].astype(F32) + rec[...].astype(F32)).reshape(128, 128).T.astype(BF)

    bq[0] = block[:64]
    bq[1] = block[64:]
    back2, back2_in, back3, back3_in = [], [], [], []
    for h in range(2):
        for d in range(4):
            to, of = ring(h, 2, d)[0], ahead(line[1 - h], 4 - d)
            for y in range(2):
                if d or y:
                    n = AG2 + 7 * h + 2 * d + y - 1
                    back2.append(remote(bq.at[h], bp.at[h, line[1 - h], ylo], n, (to + y * (across - s), g)))
                    came = bp.at[h, of, ylo + y * (1 - 2 * ylo)]
                    back2_in.append(remote(bq.at[h], came, n, partner))
        for d in (1, 2, 3):
            n = AG3 + 3 * h + d - 1
            back3.append(remote(bp.at[h], blocks.at[core, h, line[h]], n, ring(h, 1, d)))
            back3_in.append(remote(bp.at[h], blocks.at[core, h, ahead(line[h], 4 - d)], n, partner))
    for c in back2:
        c.start()
    for h in range(2):
        bp[h, line[1 - h], ylo] = bq[h]
    loads[8].wait()
    loads[9].wait()
    e6.wait_recv()
    for k in range(2):
        mkv[k, R : R + M, :] = (dot(ef[0], wm[0, 1 + k]) + dot(ef[1], wm[1, 1 + k])).astype(BF)
    kup = remote(mkv.at[:, pl.ds(M, R), :], mkv.at[:, pl.ds(0, R), :], KUP, (up, g))
    kdown = remote(mkv.at[:, pl.ds(R, R), :], mkv.at[:, pl.ds(R + M, R), :], KDOWN, (down, g))
    kup.start()
    kdown.start()
    mq[...] = (dot(ef[0], wm[0, 0]) + dot(ef[1], wm[1, 0])).astype(BF)

    lax.fori_loop(3, 4, interior, 0)

    for h in range(2):
        for c in back2_in[7 * h : 7 * h + 7]:
            c.wait_recv()
        for c in back3[3 * h : 3 * h + 3]:
            c.start()
        blocks[core, h, line[h]] = bp[h]

    def pass_copy(k, h, d):
        part = blocks.at[k, h, ahead(line[h], 4 - d)]
        return remote(part, part, AGF + 4 * h + d, (sib, g))

    def result_copy(k, h, d):
        n = ahead(line[h], 4 - d)
        return pltpu.make_async_copy(blocks.at[k, h, n], gkv_out.at[k, h, n], out_s.at[k, 4 * h + d])

    passed = [pass_copy(core, h, d) for h in range(2) for d in range(4)]
    handed = [pass_copy(1 - core, h, d) for h in range(2) for d in range(4)]
    mine_out = [result_copy(core, h, d) for h in range(2) for d in range(4)]
    other_out = [result_copy(1 - core, h, d) for h in range(2) for d in range(4)]
    for n in (0, 4):
        passed[n].start()
        mine_out[n].start()

    where_n = iota((M, 256), 1) - R
    delta = where_n - iota((M, 256), 0)
    allowed = delta == off[0]
    for j in range(1, W):
        allowed = allowed | (delta == off[j])
    where_g = where_n + s * M
    allowed = allowed & (where_g >= 0) & (where_g < M * SPACE)
    allow = jnp.where(allowed[:, : M + 2 * R], 1.0, 0.0)
    allow4 = jnp.concatenate([allow] * 4, axis=0)
    kup.wait_recv()
    kdown.wait_recv()
    matts = []
    for a in range(2):
        cols = slice(a * 256, (a + 1) * 256)
        x4 = mq[:, cols].astype(F32)
        head = iota((M, 256), 1) // 64
        lhs = jnp.concatenate([jnp.where(head == i, x4, 0.0).astype(BF) for i in range(4)], axis=0)
        raw = dot_t(lhs, mkv[0, :, cols]) * SCALE
        wgt = jnp.exp(CAP * jnp.tanh(raw * (1.0 / CAP))) * allow4
        prob = (wgt / jnp.sum(wgt, axis=1, keepdims=True)).astype(BF)
        matts.append(diagonal(dot(prob, mkv[1, :, cols])).astype(BF))
    matt = jnp.concatenate(matts, axis=1)
    loads[10].wait()
    loads[11].wait()
    mo_send[...] = dot(matt, wmo[1]).astype(BF)
    e8 = remote(mo_send, mo_recv, E8, partner)
    e8.start()
    mo_own[...] = dot(matt, wmo[0])

    gdown.wait_recv()
    gup.wait_recv()
    ggs[0:RIM, :] = (ggs[0:RIM, :].astype(F32) + halo_recv[0].astype(F32)).astype(BF)
    ggs[G - RIM : G, :] = (ggs[G - RIM : G, :].astype(F32) + halo_recv[1].astype(F32)).astype(BF)
    gg_copy = pltpu.make_async_copy(ggs, gg_out, osem.at[2])
    gg_copy.start()

    singles = [e1m, e1c, hup, hdown, e2, e2d, e3a, e3b, e4, e5, e6, kup, kdown, gdown, gup, stage3]
    for c in singles + wy + [c for c, _ in wring] + wfwd + presum + stage1 + stage2 + back2:
        c.wait_send()
    for d in (1, 2, 3):
        for h in range(2):
            back3_in[3 * h + d - 1].wait_recv()
            passed[4 * h + d].start()
            mine_out[4 * h + d].start()
    e8.wait()
    mo_val[...] = (ef[0].astype(F32) + mo_own[...] + mo_recv[...].astype(F32)).astype(BF)
    mo_copy = pltpu.make_async_copy(mo_val, mesh_out, osem.at[3])
    mo_copy.start()

    for c in back3:
        c.wait_send()
    for d in range(4):
        for h in range(2):
            handed[4 * h + d].wait_recv()
            other_out[4 * h + d].start()
    for c in passed:
        c.wait_send()
    enc_copy.wait()
    gg_copy.wait()
    mo_copy.wait()
    for c in mine_out + other_out:
        c.wait()


def write_results(enc, mesh_o, gg, gkv, enc_out, mesh_out, gg_out, gkv_out, e, m, r, low, wide, s_in, s_out, k_in, k_out):
    plain = ((enc, e, enc_out), (mesh_o, m, mesh_out), (gg, r, gg_out))
    g = lax.axis_index("head")
    loads = [pltpu.make_async_copy(gkv.at[k], low.at[k], k_in.at[k]) for k in range(2)]
    others = [pltpu.make_async_copy(a, b, s_in.at[n]) for n, (a, b, _) in enumerate(plain)]
    for c in loads + others:
        c.start()
    stores = []
    for k in range(2):
        loads[k].wait()
        for n in range(2):
            half = g if n == 0 else 1 - g
            for x in (2 * n, 2 * n + 1):
                for z in range(4):
                    for y in range(2):
                        col = (x % 2 * 2 + y) * 128
                        for h in range(2):
                            rows = pl.ds(pl.multiple_of(half * F + z * 128 + h * 64, 64), 64)
                            part = low[k, 0, z, x, y] if h == 0 else low[k, 1, x, z, y]
                            wide[k, rows, col : col + 128] = part.astype(F32)
            rows = pl.ds(pl.multiple_of(half * F, F), F)
            stores.append(pltpu.make_async_copy(wide.at[k, rows], gkv_out.at[k, rows], k_out.at[2 * k + n]))
            stores[-1].start()
    for n, (_, b, c) in enumerate(plain):
        others[n].wait()
        stores.append(pltpu.make_async_copy(b, c, s_out.at[n]))
        stores[-1].start()
    for c in stores:
        c.wait()


def shards(
    grid_feat, mesh_feat, edge_src, degree, offsets, w_kv, w_query, w_out, w_mesh, w_mesh_out, cotangent
):
    hbm = pl.BlockSpec(memory_space=pl.ANY)
    vmem = pl.BlockSpec(memory_space=pltpu.VMEM)
    smem = pl.BlockSpec(memory_space=pltpu.SMEM)

    def v(*shape, dtype=BF):
        return pltpu.VMEM(shape, dtype)

    dma = pltpu.SemaphoreType.DMA
    scratch = dict(
        nodes=v(M, K, dtype=I32), wide=v(WIDE, F), mf=v(2, M, F), cf=v(2, M, F), wkv_own=v(2, F, F), wkv_oth=v(2, F, F),
        wq=v(2, F, F), wo=v(2, F, F), wm=v(2, 3, F, F), wmo=v(2, F, F),
        qd=v(2, 2, M, F), qdt=v(2, 2, F, M), xs=v(G, F), ut=v(2, 16, M, F), zy=v(2, 16, M, F),
        srow=v(8, G, dtype=F32),
        sd=v(2, 8, K, 256, dtype=F32), sd_send=v(2, 8, K, 256), sd_recv=v(2, 8, K, 256), pb=v(8, K, 512),
        att_own=v(M, F, dtype=F32), att_send=v(M, F), att_recv=v(M, F),
        enc_own=v(M, F, dtype=F32), enc_send=v(M, F), enc_recv=v(M, F), ef=v(2, M, F),
        mkv=v(2, M + 2 * R, F), mq=v(M, F),
        mo_own=v(M, F, dtype=F32), mo_send=v(M, F), mo_recv=v(M, F), mo_val=v(M, F),
        gedge=v(G, F), halo_send=v(2, RIM, F), halo_recv=v(2, RIM, F), ggs=v(G, F),
        gb=v(2, 2, 4, 8, 64, 128), pre=v(2, 4, 8, 64, 128), rs1=v(2, 3, 8, 64, 128), rsum=v(2, 8, 64, 128),
        rs2=v(2, 3, 2, 64, 128), tt=v(2, 2, 64, 128), tp=v(2, 64, 128), rec=v(2, 64, 128),
        bq=v(2, 64, 128), bp=v(2, 4, 2, 64, 128), blocks=v(2, 2, 4, 4, 2, 64, 128),
        lsem=dma((12,)), osem=dma((4,)), ssem=dma((N_REMOTE,)), rsem=dma((N_REMOTE,)),
        out_s=dma((2, 8)),
    )
    enc, mesh_out, grad_grid, grad_kv = pl.pallas_call(
        body,
        out_shape=(
            jax.ShapeDtypeStruct((M, F), BF),
            jax.ShapeDtypeStruct((M, F), BF),
            jax.ShapeDtypeStruct((G, F), BF),
            jax.ShapeDtypeStruct((2, 2, 4, 4, 2, 64, 128), BF),
        ),
        in_specs=[hbm, hbm, vmem, vmem, smem, hbm, hbm, hbm, hbm, hbm, hbm],
        out_specs=(hbm, hbm, hbm, hbm),
        scratch_shapes=list(scratch.values()),
        compiler_params=pltpu.CompilerParams(
            collective_id=0, has_side_effects=True, vmem_limit_bytes=58 * 2**20
        ),
        name="encoder",
    )(
        grid_feat, mesh_feat, edge_src.T, degree.reshape(1, M), offsets, w_kv, w_query, w_out, w_mesh,
        w_mesh_out, cotangent,
    )
    dma = pltpu.SemaphoreType.DMA
    return pl.pallas_call(
        write_results,
        out_shape=(
            jax.ShapeDtypeStruct((M, F), BF),
            jax.ShapeDtypeStruct((M, F), BF),
            jax.ShapeDtypeStruct((G, F), BF),
            jax.ShapeDtypeStruct((2, 2 * F, F), F32),
        ),
        in_specs=[hbm] * 4,
        out_specs=(hbm,) * 4,
        scratch_shapes=[
            v(M, F), v(M, F), v(G, F), v(2, 2, 4, 4, 2, 64, 128), v(2, 2 * F, F, dtype=F32),
            dma((3,)), dma((3,)), dma((2,)), dma((4,)),
        ],
        compiler_params=pltpu.CompilerParams(vmem_limit_bytes=58 * 2**20),
        name="results",
    )(enc, mesh_out, grad_grid, grad_kv)


def solution(mesh):
    in_specs = (
        P("space", "head"),
        P("space", "head"),
        P("space", None),
        P("space"),
        P(),
        P(None, None, "head"),
        P(None, "head"),
        P("head", None),
        P(None, None, "head"),
        P("head", None),
        P("space", "head"),
    )
    out_specs = (P("space", "head"), P("space", "head"), P("space", "head"), P(None, None, "head"))
    return jax.shard_map(shards, mesh=mesh, in_specs=in_specs, out_specs=out_specs, check_vma=False)
```
